256 devices in a mesh: dp: 64 (over x, z, core), mp: 4 (over y).
Axes of the slice: x: 4, y: 4, z: 8, core: 2. Of those that a mesh axis runs over, the one named last changes fastest.
Arguments:
- features: bfloat16 [65536, 1024], P('dp'), may hold values from -6 to 6
- out_grads: bfloat16 [65536, 4, 1024], P('dp', None, 'mp'), may hold values from -0.0234375 to 0.0234375
- norm_grads: float32 [64, 2048], P('dp'), may hold values from -0.75 to 0.75
- owners: int32 [5], replicated, may hold values from 0 to 63, as said below
- moment1: float32 [4, 1024, 1024], P(None, 'dp', 'mp'), may hold values from -6 to 6
- moment2: float32 [4, 1024, 1024], P(None, 'dp', 'mp'), may hold values from 0.1 to 10
- left_stats: float32 [4, 1024, 1024], P(None, 'dp', 'mp'), may hold values from -1024 to 1024, as said below
- right_stats: float32 [4, 1024, 1024], P(None, 'dp', 'mp'), may hold values from -1024 to 1024, as said below
- left_basis: float32 [4, 1024, 1024], P(None, 'dp', 'mp'), may hold values from -1 to 2
- right_basis: float32 [4, 1024, 1024], P(None, 'dp', 'mp'), may hold values from -1 to 2
- norm_m: float32 [2048], P('dp'), may hold values from -6 to 6
- norm_v: float32 [2048], P('dp'), may hold values from 0.1 to 10
Outputs:
- new_moment1: float32 [4, 1024, 1024], P(None, 'dp', 'mp')
- new_moment2: float32 [4, 1024, 1024], P(None, 'dp', 'mp')
- new_left_stats: float32 [4, 1024, 1024], P(None, 'dp', 'mp')
- new_right_stats: float32 [4, 1024, 1024], P(None, 'dp', 'mp')
- new_left_basis: float32 [4, 1024, 1024], P(None, 'dp', 'mp')
- new_right_basis: float32 [4, 1024, 1024], P(None, 'dp', 'mp')
- update_slots: bfloat16 [64, 1024, 1024], P('dp', None, 'mp')
- new_norm_m: float32 [2048], P('dp')
- new_norm_v: float32 [2048], P('dp')
- norm_slots: float32 [64, 2048], P('dp')
The draws below stay inside these ranges and needn't reach their ends.
Inputs may be any that keep to these rules, and one draw needn't show every extreme that they name: `owners`: the first 4 entries are distinct, so a dp index owns at most one tile; the last entry may equal any of them. `left_stats`: each tile of statistics is symmetric. `right_stats`: each tile of statistics is symmetric.
All inputs are finite; a program needn't handle non-finite values.
Results may differ from the reference program's by a relative error of at most 0.0072.
Values may be sent and summed in bfloat16 or wider, within the bound.
No kernel may reach another device: no remote copies, remote signals or barrier semaphores. Data moves between devices by JAX's collectives and lax.ppermute only.
A program may use at most 128 MiB of HBM per device.

```python
import math
import jax
import jax.numpy as jnp
from jax import lax

D = 2048
TILE = 1024
NT = 4
TOKENS = 65536
N_DP = 64


def stats_single(key):
    key_diag, key_noise = jax.random.split(key)
    diag = TILE * jnp.exp(jax.random.uniform(key_diag, (TILE,), jnp.float32, math.log(0.1), 0.0))
    noise = jax.random.normal(key_noise, (TILE, TILE), jnp.float32)
    symmetric = (noise + noise.T) * 0.70710678
    scale = jnp.sqrt(diag[:, None] * diag[None, :]) * (0.3 / math.sqrt(TILE))
    positions = jnp.arange(TILE, dtype=jnp.int32)
    on_diag = positions[:, None] == positions[None, :]
    return jnp.where(on_diag, diag[:, None], scale * symmetric)


def basis_single(key):
    noise = jax.random.normal(key, (TILE, TILE), jnp.float32)
    positions = jnp.arange(TILE, dtype=jnp.int32)
    on_diag = (positions[:, None] == positions[None, :]).astype(jnp.float32)
    return on_diag + noise * (0.3 / math.sqrt(TILE))


def draw_owners(key, part):
    key_perm, key_mix, key_norm = jax.random.split(jax.random.fold_in(key, 5), 3)
    middle = (1 + jax.random.permutation(key_perm, N_DP - 2)[:NT - 2]).astype(jnp.int32)
    ends = jnp.array([0, N_DP - 1], dtype=jnp.int32)
    tiles = jax.random.permutation(key_mix, jnp.concatenate([ends, middle])).astype(jnp.int32)
    norm_owner = jax.random.randint(key_norm, (1,), 0, N_DP).astype(jnp.int32)
    return jnp.concatenate([tiles, norm_owner]).astype(jnp.int32)


def draw_left_stats(key, part):
    return jax.vmap(stats_single)(jax.random.split(jax.random.fold_in(key, 11), NT))


def draw_right_stats(key, part):
    return jax.vmap(stats_single)(jax.random.split(jax.random.fold_in(key, 13), NT))


def draw_left_basis(key, part):
    return jax.vmap(basis_single)(jax.random.split(jax.random.fold_in(key, 17), NT))


def draw_right_basis(key, part):
    return jax.vmap(basis_single)(jax.random.split(jax.random.fold_in(key, 19), NT))


def block_levels(stream_key, shape, cuts, low, top_value):
    gain = 1.0
    for dim, shards_of in cuts:
        heights = jax.random.uniform(jax.random.fold_in(jax.random.fold_in(stream_key, 6), dim), (shards_of,), jnp.float32, low / len(cuts), top_value / len(cuts))
        gain = gain * jnp.repeat(jnp.exp(heights), shape[dim] // shards_of).reshape((-1,) + (1,) * (len(shape) - 1 - dim))
    return gain


def gaussian(key, extent, scale, reach, pieces=(), kind=jnp.bfloat16):
    gain = block_levels(key, extent, pieces, -0.22, 0.18) if pieces else 1.0
    values = jax.random.normal(key, extent, jnp.float32) * scale * gain
    return jnp.minimum(jnp.maximum(values, -reach), reach).astype(kind)


def setup_inputs(seed: int = 0) -> dict:
    streams_of = jax.random.split(jax.random.key(seed), 13)
    return {
        "features": gaussian(streams_of[0], (TOKENS, TILE), 1.0, 6.0, ((0, 64),)),
        "out_grads": gaussian(streams_of[1], (TOKENS, NT, TILE), TOKENS ** -0.5, 0.0234375, ((0, 64), (2, 4))),
        "norm_grads": gaussian(streams_of[2], (N_DP, D), N_DP ** -0.5, 0.75, ((0, 64),), jnp.float32),
        "owners": draw_owners(jax.random.fold_in(streams_of[12], 71), 0),
        "moment1": gaussian(streams_of[4], (NT, TILE, TILE), 1.0, 6.0, ((1, 64), (2, 4)), jnp.float32),
        "moment2": jnp.clip(jnp.exp(math.log(10.0) - 4.6051702 * jax.random.uniform(streams_of[5], (NT, TILE, TILE), jnp.float32) ** block_levels(streams_of[5], (NT, TILE, TILE), ((1, 64), (2, 4)), -0.2, 0.2)), 0.1, 10.0),
        "left_stats": draw_left_stats(jax.random.fold_in(streams_of[12], 71), 0),
        "right_stats": draw_right_stats(jax.random.fold_in(streams_of[12], 71), 0),
        "left_basis": draw_left_basis(jax.random.fold_in(streams_of[12], 71), 0),
        "right_basis": draw_right_basis(jax.random.fold_in(streams_of[12], 71), 0),
        "norm_m": gaussian(streams_of[10], (D,), 1.0, 6.0, ((0, 64),), jnp.float32),
        "norm_v": jnp.clip(jnp.exp(math.log(10.0) - 4.6051702 * jax.random.uniform(streams_of[11], (D,), jnp.float32) ** block_levels(streams_of[11], (D,), ((0, 64),), -0.2, 0.2)), 0.1, 10.0),
    }


FIX_ONE = 1.0 - 0.9 ** 10
FIX_TWO = 1.0 - 0.95 ** 10

def contract(left, right, left_dim, right_dim):
    return lax.dot_general(left, right, (((left_dim,), (right_dim,)), ((), ())), preferred_element_type=jnp.float32)

def reference(features, out_grads, norm_grads, owners, moment1, moment2, left_stats, right_stats, left_basis, right_basis, norm_m, norm_v):

    def tile_step(items):
        index, mom_one, mom_two, stats_l, stats_r, basis_l, basis_r = items
        grad_cols = lax.dynamic_index_in_dim(out_grads, index, 1, keepdims=False)
        grad = contract(features, grad_cols, 0, 0)
        grad_b = grad.astype(jnp.bfloat16)
        left_b = basis_l.astype(jnp.bfloat16)
        right_b = basis_r.astype(jnp.bfloat16)
        inner = jnp.dot(grad_b, right_b, preferred_element_type=jnp.float32).astype(jnp.bfloat16)
        rotated = contract(left_b, inner, 0, 0)
        new_one = 0.9 * mom_one + 0.1 * rotated
        new_two = 0.95 * mom_two + 0.05 * rotated * rotated
        direction = (new_one / FIX_ONE / (jnp.sqrt(new_two / FIX_TWO) + 1e-08)).astype(jnp.bfloat16)
        back = contract(direction, right_b, 1, 1).astype(jnp.bfloat16)
        update = jnp.dot(left_b, back, preferred_element_type=jnp.float32).astype(jnp.bfloat16)
        new_sl = 0.95 * stats_l + 0.05 * contract(grad_b, grad_b, 1, 1)
        new_sr = 0.95 * stats_r + 0.05 * contract(grad_b, grad_b, 0, 0)
        power_l = jnp.dot(new_sl.astype(jnp.bfloat16), left_b, preferred_element_type=jnp.float32)
        power_r = jnp.dot(new_sr.astype(jnp.bfloat16), right_b, preferred_element_type=jnp.float32)
        iter_l = (power_l * lax.rsqrt(lax.optimization_barrier(jnp.sum(power_l * power_l, axis=0, keepdims=True)) + 1e-06)).astype(jnp.bfloat16)
        iter_r = (power_r * lax.rsqrt(lax.optimization_barrier(jnp.sum(power_r * power_r, axis=0, keepdims=True)) + 1e-06)).astype(jnp.bfloat16)
        gram_l = contract(iter_l, iter_l, 0, 0).astype(jnp.bfloat16)
        gram_r = contract(iter_r, iter_r, 0, 0).astype(jnp.bfloat16)
        new_bl = 1.5 * iter_l.astype(jnp.float32) - 0.5 * jnp.dot(iter_l, gram_l, preferred_element_type=jnp.float32)
        new_br = 1.5 * iter_r.astype(jnp.float32) - 0.5 * jnp.dot(iter_r, gram_r, preferred_element_type=jnp.float32)
        return (new_one, new_two, new_sl, new_sr, new_bl, new_br, update)
    indices = jnp.arange(NT, dtype=jnp.int32)
    results = lax.map(tile_step, (indices, moment1, moment2, left_stats, right_stats, left_basis, right_basis))
    new_one, new_two, new_sl, new_sr, new_bl, new_br, updates = results
    update_slots = jnp.zeros((N_DP, TILE, TILE), jnp.bfloat16).at[owners[:NT]].set(updates)
    norm_total = lax.optimization_barrier(jnp.sum(norm_grads, axis=0))
    new_nm = 0.9 * norm_m + 0.1 * norm_total
    new_nv = 0.95 * norm_v + 0.05 * norm_total * norm_total
    norm_step = new_nm / FIX_ONE / (jnp.sqrt(new_nv / FIX_TWO) + 1e-08)
    norm_slots = jnp.zeros((N_DP, D), jnp.float32).at[owners[NT]].set(norm_step)
    return (new_one, new_two, new_sl, new_sr, new_bl, new_br, update_slots, new_nm, new_nv, norm_slots)
```

```python
import jax
import jax.numpy as jnp
from jax import lax
from jax.sharding import Mesh, PartitionSpec as P

FIX_ONE = 1.0 - 0.9**10
FIX_TWO = 1.0 - 0.95**10
F32 = jnp.float32
BF = jnp.bfloat16
NX, NZ, NC, NM = 4, 8, 2, 4
B = 16
W = 256
PAD = 16


def contract(left, right, left_dim, right_dim):
    return lax.dot_general(
        left, right, (((left_dim,), (right_dim,)), ((), ())), preferred_element_type=F32
    )


def swap_cores(value):
    return lax.ppermute(value, "c", [(0, 1), (1, 0)])


def exchange(value, axis):
    return lax.all_to_all(value, axis, 0, 0, tiled=True)


def everyone(value, axis, count):
    return exchange(jnp.broadcast_to(value[None], (count, *value.shape)), axis)


def ordered(core, mine, other):
    return jnp.where(core == 0, jnp.stack([mine, other]), jnp.stack([other, mine]))


def shards(
    features,
    out_grads,
    norm_grads,
    owners,
    moment1,
    moment2,
    left_stats,
    right_stats,
    left_basis,
    right_basis,
    norm_m,
    norm_v,
):
    xi = lax.axis_index("x")
    zi = lax.axis_index("z")
    ci = lax.axis_index("c")
    mi = lax.axis_index("mp")
    mine_dp = (xi * NZ + zi) * NC + ci
    other_dp = (xi * NZ + zi) * NC + (1 - ci)
    left_core = ci == 0

    with jax.named_scope("state_rows"):
        home = jnp.stack(
            [
                v.astype(BF)
                for v in (left_basis, right_basis, moment1, moment2, left_stats, right_stats)
            ],
            axis=1,
        )
        rows = exchange(home, "x")
        stats_mine = jnp.where(left_core, rows[:, 4], rows[:, 5])
        stats_send = jnp.where(left_core, rows[:, 5], rows[:, 4])
        stats_recv = swap_cores(stats_send)
        stats_rows = ordered(ci, stats_mine, stats_recv)
        pack = jnp.concatenate(
            [rows[:, :4].swapaxes(0, 1).reshape(16, B, W), stats_rows.reshape(8, B, W)], axis=0
        )
        pack = lax.all_gather(pack, "z", axis=0)
        bases = lax.all_gather(pack[:, :8], "mp", axis=0)
        stats = lax.all_gather(pack[:, 16:], "mp", axis=0)
        mom = pack[:, 8:16].reshape(NZ, 2, NX, B, W).transpose(1, 2, 0, 3, 4)
        mom = mom.reshape(2, NX * NZ * B, W)
        bases_other = swap_cores(bases)
        both = ordered(ci, bases, bases_other).reshape(NC, NM, NZ, 2, NX, B, W)
        both = both.transpose(3, 4, 2, 0, 5, 1, 6).reshape(2, NX * NZ * NC * B, NM * W)
        left, right = both[0], both[1]
        stats = stats.reshape(NM, NZ, NC, NX, B, W).transpose(3, 1, 2, 4, 0, 5)
        stats = stats.reshape(NX * NZ * NC * B, NM * W)

    with jax.named_scope("grad_sum"):
        half = features.shape[1] // 2
        feat_other = lax.dynamic_slice_in_dim(features, (1 - ci) * half, half, 1)
        feat_mine = lax.dynamic_slice_in_dim(features, ci * half, half, 1)
        norm_parts = norm_grads[0].reshape(NX, NZ, NC, 32)

        def partial(feat, core):
            grads = jnp.einsum("ti,tnc->nic", feat, out_grads, preferred_element_type=F32)
            norm = lax.dynamic_index_in_dim(norm_parts, core, 2, keepdims=False)
            norm = jnp.pad(norm.reshape(NX, 1, W), ((0, 0), (0, PAD - 1), (0, 0)))
            return grads, norm

        grads_o, norm_o = partial(feat_other, 1 - ci)
        sent = jnp.concatenate([grads_o.astype(BF), norm_o.astype(BF)], axis=1)
        got = swap_cores(sent)
        grads_s, norm_s = partial(feat_mine, ci)
        acc = jnp.concatenate([grads_s, norm_s], axis=1) + got.astype(F32)
        acc = exchange(acc.astype(BF), "x")
        acc = jnp.sum(acc.astype(F32), axis=0)
        norm_z = jnp.pad(acc[half].reshape(NZ, 1, 32), ((0, 0), (0, PAD - 1), (0, W - 32)))
        acc = jnp.concatenate([acc[:half].reshape(NZ, half // NZ, W), norm_z], axis=1)
        acc = exchange(acc.astype(BF), "z")
        acc = jnp.sum(acc.astype(F32), axis=0)
        grad_rows = acc[: half // NZ].astype(BF)
        norm_total = acc[half // NZ, :32]

    new_nm = 0.9 * norm_m + 0.1 * norm_total
    new_nv = 0.95 * norm_v + 0.05 * norm_total * norm_total
    norm_step = new_nm / FIX_ONE / (jnp.sqrt(new_nv / FIX_TWO) + 1e-08)

    with jax.named_scope("grad_all"):
        norm_row = jnp.pad(norm_step.astype(BF)[None], ((0, PAD - 1), (0, W - 32)))
        grad_z = everyone(jnp.concatenate([grad_rows, norm_row], axis=0), "z", NZ)
        norm_zs = grad_z[:, half // NZ, :32].reshape(1, W)
        grad_half = grad_z[:, : half // NZ].reshape(half, W)
        grad_half = everyone(grad_half, "mp", NM)
        grad_other = swap_cores(grad_half)
        grad = ordered(ci, grad_half, grad_other).transpose(0, 2, 1, 3).reshape(2 * half, NM * W)

    col = mi * W

    def cols(value):
        return lax.dynamic_slice_in_dim(value, col, W, 1)

    def rows_of(value):
        return lax.dynamic_slice_in_dim(value, col, W, 0)

    def left_side(grad, left, right):
        work = contract(grad, left, 0, 0).astype(BF)
        rotated = contract(work, cols(right), 0, 0)
        return work, rotated

    def right_side(grad, left, right):
        work = contract(grad, right, 1, 0).astype(BF)
        rotated = contract(left, cols(work), 0, 0)
        return work, rotated

    with jax.named_scope("rotate"):
        work, rotated = lax.cond(left_core, left_side, right_side, grad, left, right)
        rot_c = lax.dynamic_index_in_dim(
            rotated.reshape(NX, NZ, NC, B, W), ci, 2, keepdims=False
        )
        rot_flat = rot_c.reshape(-1, W)
        one = 0.9 * mom[0].astype(F32) + 0.1 * rot_flat
        two = 0.95 * mom[1].astype(F32) + 0.05 * rot_flat * rot_flat
        direction = (one / FIX_ONE / (jnp.sqrt(two / FIX_TWO) + 1e-08)).astype(BF)
        rot_home = lax.dynamic_index_in_dim(rot_c, zi, 1, keepdims=False).astype(BF)
    with jax.named_scope("update"):
        direction = everyone(direction, "mp", NM)
        direction = direction.transpose(1, 0, 2).reshape(half, NM * W)
        back = contract(direction, rows_of(right), 1, 1).astype(BF)
        back_other = swap_cores(back)
        back = ordered(ci, back, back_other).reshape(NC, NX, NZ, B, W)
        back = back.transpose(1, 2, 0, 3, 4).reshape(2 * half, W)
        left_half = lax.dynamic_slice_in_dim(left, ci * half, half, 0)
        update = jnp.dot(left_half, back, preferred_element_type=F32).astype(BF)

    with jax.named_scope("power"):

        def left_power(grad, work, basis, other):
            outer = contract(grad, rows_of(grad), 1, 1)
            power = contract(grad, work, 1, 0)
            return outer, power, contract(stats, basis, 1, 0)

        def right_power(grad, work, other, basis):
            outer = contract(grad, cols(grad), 0, 0)
            power = contract(grad, work, 0, 0)
            return outer, power, contract(stats, basis, 1, 0)

        outer, power, power_old = lax.cond(
            left_core, left_power, right_power, grad, work, left, right
        )
        power = 0.95 * power_old + 0.05 * power
        norm = lax.rsqrt(jnp.sum(power * power, axis=0, keepdims=True) + 1e-06)
        iterate = (power * norm).astype(BF)
        gram = contract(iterate, cols(iterate), 0, 0).astype(BF)

        def rows_z(value):
            return lax.dynamic_index_in_dim(
                value.reshape(NX, NZ, NC * B, -1), zi, 1, keepdims=False
            )

        iter_z = rows_z(iterate).reshape(NX * NC * B, NM * W)
        basis_new = 1.5 * cols(iter_z).astype(F32) - 0.5 * jnp.dot(
            iter_z, gram, preferred_element_type=F32
        )
        basis_new = basis_new.astype(BF).reshape(NX, NC * B, W)
        outer_z = rows_z(outer).astype(BF)

    with jax.named_scope("home"):
        everywhere = jnp.broadcast_to(update[None], (NX, half, W))
        norm_pad = jnp.broadcast_to(
            jnp.pad(norm_zs, ((0, PAD - 1), (0, 0)))[None], (NX, PAD, W)
        )
        sent = jnp.concatenate([everywhere, rot_home, outer_z, basis_new, norm_pad], axis=1)
        got = exchange(sent, "x")
        updates = got[:, :half]
        rot_home = got[:, half : half + B]
        outer_home = got[:, half + B : half + 3 * B].reshape(NX, NC, B, W)
        basis_home = got[:, half + 3 * B : half + 5 * B].reshape(NX, NC, B, W)
        norm_xz = got[:, half + 5 * B : half + 5 * B + 1].reshape(NX, W)

        tile_owner = owners[:NX]

        def owned(index):
            hit = tile_owner == index
            which = jnp.sum(jnp.where(hit, jnp.arange(NX, dtype=jnp.int32), 0))
            tile = lax.dynamic_index_in_dim(updates, which, 0, keepdims=False)
            return jnp.where(jnp.any(hit), tile, jnp.zeros_like(tile))

        def of_core(value, core):
            return lax.dynamic_index_in_dim(value, core, 1, keepdims=False)

        pieces = [
            owned(other_dp),
            of_core(outer_home, 1 - ci).reshape(-1, W),
            of_core(basis_home, 1 - ci).reshape(-1, W),
            jnp.pad(norm_xz, ((0, PAD - NX), (0, 0))),
        ]
        sent = jnp.concatenate(pieces, axis=0)
        got = swap_cores(sent)
        update_slot = ordered(ci, owned(mine_dp), got[:half]).reshape(1, 2 * half, W)
        nb = NX * B
        outer_both = ordered(
            ci, of_core(outer_home, ci), got[half : half + nb].reshape(NX, B, W)
        ).astype(F32)
        basis_both = ordered(
            ci, of_core(basis_home, ci), got[half + nb : half + 2 * nb].reshape(NX, B, W)
        ).astype(F32)
        norm_all = ordered(ci, norm_xz, got[half + 2 * nb : half + 2 * nb + NX])
        norm_all = norm_all.reshape(NC, NX, NZ, 32).transpose(1, 2, 0, 3).reshape(1, -1)
        norm_slot = jnp.where(mine_dp == owners[NX], norm_all.astype(F32), 0.0)
        rot = rot_home.astype(F32)
        new_one = 0.9 * moment1 + 0.1 * rot
        new_two = 0.95 * moment2 + 0.05 * rot * rot
        new_sl = 0.95 * left_stats + 0.05 * outer_both[0]
        new_sr = 0.95 * right_stats + 0.05 * outer_both[1]
    return (
        new_one,
        new_two,
        new_sl,
        new_sr,
        basis_both[0],
        basis_both[1],
        update_slot,
        new_nm,
        new_nv,
        norm_slot,
    )


def solution(mesh):
    mesh = Mesh(mesh.devices.reshape(NX, NZ, NC, NM), ("x", "z", "c", "mp"))
    dp = ("x", "z", "c")
    state = P(None, dp, "mp")
    in_specs = (
        P(dp, None),
        P(dp, None, "mp"),
        P(dp, None),
        P(),
        state,
        state,
        state,
        state,
        state,
        state,
        P(dp),
        P(dp),
    )
    out_specs = (
        state,
        state,
        state,
        state,
        state,
        state,
        P(dp, None, "mp"),
        P(dp),
        P(dp),
        P(dp, None),
    )
    return jax.shard_map(shards, mesh=mesh, in_specs=in_specs, out_specs=out_specs, check_vma=False)
```

```python
import jax
import jax.numpy as jnp
from jax import lax
from jax.experimental import pallas as pl
from jax.experimental.pallas import tpu as pltpu
from jax.sharding import Mesh, PartitionSpec as P

FIX_ONE = 1.0 - 0.9**10
FIX_TWO = 1.0 - 0.95**10
F32 = jnp.float32
BF = jnp.bfloat16
NX, NZ, NC, NM = 4, 8, 2, 4
B = 16
W = 256
PAD = 16


def contract(left, right, left_dim, right_dim):
    return lax.dot_general(
        left, right, (((left_dim,), (right_dim,)), ((), ())), preferred_element_type=F32
    )


def swap_cores(value):
    return lax.ppermute(value, "c", [(0, 1), (1, 0)])


def exchange(value, axis):
    return lax.all_to_all(value, axis, 0, 0, tiled=True)


def everyone(value, axis, count):
    return exchange(jnp.broadcast_to(value[None], (count, *value.shape)), axis)


def ordered(core, mine, other):
    return jnp.where(core == 0, jnp.stack([mine, other]), jnp.stack([other, mine]))


VMEM = pl.BlockSpec(memory_space=pltpu.VMEM)
SMEM = pl.BlockSpec(memory_space=pltpu.SMEM)


def dot_nn(a, b):
    return contract(a, b, 1, 0)


def dot_nt(a, b):
    return contract(a, b, 1, 1)


def dot_tn(a, b):
    return contract(a, b, 0, 0)


def call(kernel, name, outs, scratch, *args):
    n_scalar = 1
    return pl.pallas_call(
        kernel,
        out_shape=[jax.ShapeDtypeStruct(s, d) for s, d in outs],
        in_specs=[SMEM] * n_scalar + [VMEM] * (len(args) - n_scalar),
        out_specs=[VMEM] * len(outs),
        scratch_shapes=[pltpu.VMEM(s, d) for s, d in scratch],
        compiler_params=pltpu.CompilerParams(vmem_limit_bytes=48 * 1024 * 1024),
        name=name,
    )(*args)


def pack_kernel(where, lb, rb, m1, m2, sl, sr, out):
    for k, ref in enumerate((lb, rb, m1, m2, sl, sr)):
        out[:, k] = ref[...].astype(BF)


def block_start(index, size):
    return pl.multiple_of(index * size, size)


def prep_kernel(where, own, oth, left, right):
    c = where[2]

    def step(k, carry):
        z, xp = k // NX, k % NX
        start = xp * (NZ * NC * B) + z * (NC * B)
        for ref, core in ((own, c), (oth, 1 - c)):
            row = pl.multiple_of(start + core * B, B)
            for arr, out in ((0, left), (1, right)):
                for m in range(NM):
                    out[pl.ds(row, B), m * W : (m + 1) * W] = ref[m, z, arr * NX + xp]
        return carry

    lax.fori_loop(0, NZ * NX, step, 0)


def old_power_kernel(where, s0, s1, s2, s3, left, right, out, stats):
    c, m = where[2], where[3]

    def step(k, carry):
        z, xp = k // NX, k % NX
        for core in range(NC):
            row = pl.multiple_of(xp * (NZ * NC * B) + z * (NC * B) + core * B, B)
            for shift, ref in enumerate((s0, s1, s2, s3)):
                col = block_start(lax.rem(m + NM - shift, NM), W)
                stats[pl.ds(row, B), pl.ds(col, W)] = ref[z, core * NX + xp]
        return carry

    lax.fori_loop(0, NZ * NX, step, 0)

    def product(basis):
        def rows(i, carry):
            r = pl.ds(block_start(i, W), W)
            out[r, :] = dot_nn(stats[r, :], basis[...])
            return carry

        lax.fori_loop(0, NM, rows, 0)

    @pl.when(c == 0)
    def _():
        product(left)

    @pl.when(c == 1)
    def _():
        product(right)


def rotate_kernel(where, own, oth, left, right, pack, grad, work, direct, rot_home, rot):
    z, c, m = where[1], where[2], where[3]
    half = own.shape[1]
    for ref, core in ((own, c), (oth, 1 - c)):
        r = pl.ds(block_start(core, half), half)
        for k in range(NM):
            grad[r, k * W : (k + 1) * W] = ref[k]
    col = pl.ds(block_start(m, W), W)

    @pl.when(c == 0)
    def _():
        def rows(i, carry):
            r = pl.ds(block_start(i, W), W)
            work[r, :] = dot_tn(left[:, r], grad[...]).astype(BF)
            rot[r, :] = dot_nn(work[r, :], right[:, col])
            return carry

        lax.fori_loop(0, NM, rows, 0)

    @pl.when(c == 1)
    def _():
        def rows(i, carry):
            r = pl.ds(block_start(i, W), W)
            work[r, :] = dot_nn(grad[r, :], right[...]).astype(BF)
            return carry

        lax.fori_loop(0, NM, rows, 0)

        def more(i, carry):
            r = pl.ds(block_start(i, W), W)
            rot[r, :] = dot_tn(left[:, r], work[:, col])
            return carry

        lax.fori_loop(0, NM, more, 0)

    def step(k, carry):
        xp, zp = k // NZ, k % NZ
        value = rot[pl.ds(pl.multiple_of(k * (NC * B) + c * B, B), B), :]
        one = 0.9 * pack[zp, 2 * NX + xp].astype(F32) + 0.1 * value
        two = 0.95 * pack[zp, 3 * NX + xp].astype(F32) + 0.05 * value * value
        value = (one / FIX_ONE / (jnp.sqrt(two / FIX_TWO) + 1e-08)).astype(BF)
        for copy in range(NM):
            direct[copy, pl.ds(block_start(k, B), B), :] = value
        return carry

    lax.fori_loop(0, NX * NZ, step, 0)
    for xp in range(NX):
        row = pl.multiple_of(xp * (NZ * NC * B) + z * (NC * B) + c * B, B)
        rot_home[xp] = rot[pl.ds(row, B), :].astype(BF)


def power_kernel(where, grad, work, old, outer, basis, power, iterate):
    z, c, m = where[1], where[2], where[3]
    col = pl.ds(block_start(m, W), W)
    total = NM * W

    def z_rows(xp):
        return pl.ds(pl.multiple_of(xp * (NZ * NC * B) + z * (NC * B), NC * B), NC * B)

    @pl.when(c == 0)
    def _():
        def rows(i, sums):
            r = pl.ds(block_start(i, W), W)
            value = 0.95 * old[r, :] + 0.05 * dot_nt(grad[r, :], work[...])
            power[r, :] = value
            return sums + jnp.sum(value * value, axis=0, keepdims=True)

        sums = lax.fori_loop(0, NM, rows, jnp.zeros((1, total), F32))
        scale = lax.rsqrt(sums + 1e-06)
        for i in range(NM):
            r = slice(i * W, (i + 1) * W)
            iterate[r, :] = (power[r, :] * scale).astype(BF)
        for xp in range(NX):
            outer[xp] = dot_nt(grad[z_rows(xp), :], grad[col, :]).astype(BF)

    @pl.when(c == 1)
    def _():
        def rows(i, sums):
            r = pl.ds(block_start(i, W), W)
            value = 0.95 * old[r, :] + 0.05 * dot_tn(grad[:, r], work[...])
            power[r, :] = value
            return sums + jnp.sum(value * value, axis=0, keepdims=True)

        sums = lax.fori_loop(0, NM, rows, jnp.zeros((1, total), F32))
        scale = lax.rsqrt(sums + 1e-06)
        for i in range(NM):
            r = slice(i * W, (i + 1) * W)
            iterate[r, :] = (power[r, :] * scale).astype(BF)

        def gram_rows(i, carry):
            r = pl.ds(block_start(i, W), W)
            power[r, 0:W] = dot_tn(grad[:, r], grad[:, col])
            return carry

        lax.fori_loop(0, NM, gram_rows, 0)
        for xp in range(NX):
            outer[xp] = power[z_rows(xp), 0:W].astype(BF)

    gram = dot_tn(iterate[:, col], iterate[...]).astype(BF)
    for xp in range(NX):
        here = iterate[z_rows(xp), :]
        value = 1.5 * iterate[z_rows(xp), col].astype(F32) - 0.5 * dot_nt(here, gram)
        basis[xp] = value.astype(BF)


def back_kernel(where, direct, right, back):
    m = where[3]
    rows = pl.ds(block_start(m, W), W)
    total = dot_nt(direct[0], right[rows, 0:W])
    for k in range(1, NM):
        total += dot_nt(direct[k], right[rows, k * W : (k + 1) * W])
    back[...] = total.astype(BF)


def update_kernel(where, own, oth, left, rot_home, outer, basis, norm, sent, back):
    c = where[2]
    half = own.shape[0]

    def step(k, carry):
        src = pl.ds(block_start(k, B), B)
        for ref, core in ((own, c), (oth, 1 - c)):
            back[pl.ds(pl.multiple_of(k * (NC * B) + core * B, B), B), :] = ref[src, :]
        return carry

    lax.fori_loop(0, NX * NZ, step, 0)
    value = dot_nn(left[pl.ds(block_start(c, half), half), :], back[...]).astype(BF)
    for xp in range(NX):
        sent[xp, :half] = value
        sent[xp, half : half + B] = rot_home[xp]
        sent[xp, half + B : half + 3 * B] = outer[xp]
        sent[xp, half + 3 * B : half + 5 * B] = basis[xp]
        sent[xp, half + 5 * B :] = norm[...]


def relay_kernel(where, got, own_slot, sent):
    c = where[2]
    half = own_slot.shape[0]

    def owned(hit, tile):
        value = got[tile, :half]
        return jnp.where(hit > 0, value.astype(F32), 0.0).astype(BF)

    own_slot[...] = owned(where[4], where[5])
    sent[:half] = owned(where[6], where[7])
    nb = NX * B
    for t in range(NX):
        row = pl.multiple_of((1 - c) * B, B)
        sent[half + t * B : half + (t + 1) * B] = got[t, pl.ds(half + B + row, B)]
        sent[half + nb + t * B : half + nb + (t + 1) * B] = got[
            t, pl.ds(half + 3 * B + row, B)
        ]
    sent[half + 2 * nb :] = got[0, half + 5 * B :]
    for t in range(NX):
        sent[half + 2 * nb + t : half + 2 * nb + t + 1] = got[t, half + 5 * B : half + 5 * B + 1]


def final_kernel(
    where, got, own_slot, recv, m1, m2, sl, sr, o1, o2, osl, osr, obl, obr, slot
):
    c = where[2]
    half = own_slot.shape[0]
    nb = NX * B
    slot[0, pl.ds(block_start(c, half), half)] = own_slot[...]
    slot[0, pl.ds(block_start(1 - c, half), half)] = recv[:half]
    row = pl.multiple_of(c * B, B)
    for t in range(NX):
        rot = got[t, half : half + B].astype(F32)
        o1[t] = 0.9 * m1[t] + 0.1 * rot
        o2[t] = 0.95 * m2[t] + 0.05 * rot * rot
        outer_own = got[t, pl.ds(half + B + row, B)].astype(F32)
        outer_oth = recv[half + t * B : half + (t + 1) * B].astype(F32)
        basis_own = got[t, pl.ds(half + 3 * B + row, B)].astype(F32)
        basis_oth = recv[half + nb + t * B : half + nb + (t + 1) * B].astype(F32)
        osl[t] = 0.95 * sl[t] + 0.05 * jnp.where(c == 0, outer_own, outer_oth)
        osr[t] = 0.95 * sr[t] + 0.05 * jnp.where(c == 0, outer_oth, outer_own)
        obl[t] = jnp.where(c == 0, basis_own, basis_oth)
        obr[t] = jnp.where(c == 0, basis_oth, basis_own)


def shards(
    features,
    out_grads,
    norm_grads,
    owners,
    moment1,
    moment2,
    left_stats,
    right_stats,
    left_basis,
    right_basis,
    norm_m,
    norm_v,
):
    xi = lax.axis_index("x")
    zi = lax.axis_index("z")
    ci = lax.axis_index("c")
    mi = lax.axis_index("mp")
    mine_dp = (xi * NZ + zi) * NC + ci
    other_dp = (xi * NZ + zi) * NC + (1 - ci)
    left_core = ci == 0
    half = features.shape[1] // 2
    full = 2 * half
    tile_owner = owners[:NX]

    def owned(index):
        hit = tile_owner == index
        which = jnp.sum(jnp.where(hit, jnp.arange(NX, dtype=jnp.int32), 0))
        return [jnp.any(hit).astype(jnp.int32), which]

    where = jnp.stack([xi, zi, ci, mi, *owned(mine_dp), *owned(other_dp)]).astype(jnp.int32)

    with jax.named_scope("state_rows"):
        (home,) = call(
            pack_kernel,
            "pack",
            [((NX, 6, B, W), BF)],
            [],
            where,
            left_basis,
            right_basis,
            moment1,
            moment2,
            left_stats,
            right_stats,
        )
        rows = exchange(home, "x")
        stats_mine = jnp.where(left_core, rows[:, 4], rows[:, 5])
        stats_send = jnp.where(left_core, rows[:, 5], rows[:, 4])
        stats_recv = swap_cores(stats_send)
        stats_rows = ordered(ci, stats_mine, stats_recv)
        pack = jnp.concatenate(
            [rows[:, :4].swapaxes(0, 1).reshape(16, B, W), stats_rows.reshape(8, B, W)], axis=0
        )
        pack = lax.all_gather(pack, "z", axis=0)

    with jax.named_scope("grad_sum"):
        feat_other = lax.dynamic_slice_in_dim(features, (1 - ci) * half, half, 1)
        feat_mine = lax.dynamic_slice_in_dim(features, ci * half, half, 1)
        norm_parts = norm_grads[0].reshape(NX, NZ, NC, 32)

        def partial(feat, core):
            grads = jnp.einsum("ti,tnc->nic", feat, out_grads, preferred_element_type=F32)
            norm = lax.dynamic_index_in_dim(norm_parts, core, 2, keepdims=False)
            norm = jnp.pad(norm.reshape(NX, 1, W), ((0, 0), (0, PAD - 1), (0, 0)))
            return grads, norm

        grads_o, norm_o = partial(feat_other, 1 - ci)
        sent = jnp.concatenate([grads_o.astype(BF), norm_o.astype(BF)], axis=1)
        got = swap_cores(sent)
        grads_s, norm_s = partial(feat_mine, ci)
        acc = jnp.concatenate([grads_s, norm_s], axis=1) + got.astype(F32)
        acc = exchange(acc.astype(BF), "x")
        acc, pack = lax.optimization_barrier((acc, pack))

    with jax.named_scope("state_all"):
        bases = lax.all_gather(pack[:, :8], "mp", axis=0)
        stats = pack[:, 16:]
        stats_all = [stats] + [
            lax.ppermute(stats, "mp", [(i, (i + s) % NM) for i in range(NM)]) for s in (1, 2, 3)
        ]
        bases_other = swap_cores(bases)
        left, right = call(
            prep_kernel, "prep", [((full, full), BF)] * 2, [], where, bases, bases_other
        )
        (power_old,) = call(
            old_power_kernel,
            "old_power",
            [((full, full), F32)],
            [((full, full), BF)],
            where,
            *stats_all,
            left,
            right,
        )

    with jax.named_scope("grad_sum"):
        acc = jnp.sum(acc.astype(F32), axis=0)
        norm_z = jnp.pad(acc[half].reshape(NZ, 1, 32), ((0, 0), (0, PAD - 1), (0, W - 32)))
        acc = jnp.concatenate([acc[:half].reshape(NZ, half // NZ, W), norm_z], axis=1)
        acc = exchange(acc.astype(BF), "z")
        acc = jnp.sum(acc.astype(F32), axis=0)
        grad_rows = acc[: half // NZ].astype(BF)
        norm_total = acc[half // NZ, :32]

    new_nm = 0.9 * norm_m + 0.1 * norm_total
    new_nv = 0.95 * norm_v + 0.05 * norm_total * norm_total
    norm_step = new_nm / FIX_ONE / (jnp.sqrt(new_nv / FIX_TWO) + 1e-08)

    with jax.named_scope("grad_all"):
        norm_row = jnp.pad(norm_step.astype(BF)[None], ((0, PAD - 1), (0, W - 32)))
        grad_z = everyone(jnp.concatenate([grad_rows, norm_row], axis=0), "z", NZ)
        norm_zs = grad_z[:, half // NZ, :32].reshape(1, W)
        grad_half = grad_z[:, : half // NZ].reshape(half, W)
        grad_half = everyone(grad_half, "mp", NM)
        grad_other = swap_cores(grad_half)

    with jax.named_scope("rotate"):
        grad, work, direction, rot_home = call(
            rotate_kernel,
            "rotate",
            [
                ((full, full), BF),
                ((full, full), BF),
                ((NM, half, W), BF),
                ((NX, B, W), BF),
            ],
            [((full, W), F32)],
            where,
            grad_half,
            grad_other,
            left,
            right,
            pack,
        )
        direction = exchange(direction, "mp")
    with jax.named_scope("power"):
        outer, basis = call(
            power_kernel,
            "power",
            [((NX, NC * B, W), BF)] * 2,
            [((full, full), F32), ((full, full), BF)],
            where,
            grad,
            work,
            power_old,
        )
    with jax.named_scope("update"):
        (back,) = call(back_kernel, "back", [((half, W), BF)], [], where, direction, right)
        back_other = swap_cores(back)
        norm_pad = jnp.pad(norm_zs, ((0, PAD - 1), (0, 0)))
        (sent,) = call(
            update_kernel,
            "update",
            [((NX, half + 5 * B + PAD, W), BF)],
            [((full, W), BF)],
            where,
            back,
            back_other,
            left,
            rot_home,
            outer,
            basis,
            norm_pad,
        )

    with jax.named_scope("home"):
        got = exchange(sent, "x")
        nb = NX * B
        own_slot, sent = call(
            relay_kernel,
            "relay",
            [((half, W), BF), ((half + 2 * nb + PAD, W), BF)],
            [],
            where,
            got,
        )
        recv = swap_cores(sent)
        state = ((NX, B, W), F32)
        outs = call(
            final_kernel,
            "final",
            [state] * 6 + [((1, full, W), BF)],
            [],
            where,
            got,
            own_slot,
            recv,
            moment1,
            moment2,
            left_stats,
            right_stats,
        )
        norm_xz = got[:, half + 5 * B]
        norm_all = ordered(ci, norm_xz, recv[half + 2 * nb : half + 2 * nb + NX])
        norm_all = norm_all.reshape(NC, NX, NZ, 32).transpose(1, 2, 0, 3).reshape(1, -1)
        norm_slot = jnp.where(mine_dp == owners[NX], norm_all.astype(F32), 0.0)
    return (*outs, new_nm, new_nv, norm_slot)


def solution(mesh):
    mesh = Mesh(mesh.devices.reshape(NX, NZ, NC, NM), ("x", "z", "c", "mp"))
    dp = ("x", "z", "c")
    state = P(None, dp, "mp")
    in_specs = (
        P(dp, None),
        P(dp, None, "mp"),
        P(dp, None),
        P(),
        state,
        state,
        state,
        state,
        state,
        state,
        P(dp),
        P(dp),
    )
    out_specs = (
        state,
        state,
        state,
        state,
        state,
        state,
        P(dp, None, "mp"),
        P(dp),
        P(dp),
        P(dp, None),
    )
    return jax.shard_map(shards, mesh=mesh, in_specs=in_specs, out_specs=out_specs, check_vma=False)
```

```python
import jax
import jax.numpy as jnp
from jax import lax
from jax.experimental import pallas as pl
from jax.experimental.pallas import tpu as pltpu
from jax.sharding import Mesh, PartitionSpec as P

FIX_ONE = 1.0 - 0.9**10
FIX_TWO = 1.0 - 0.95**10
F32 = jnp.float32
BF = jnp.bfloat16
NX, NZ, NC, NM = 4, 8, 2, 4
B = 16
W = 256
PAD = 16


def contract(left, right, left_dim, right_dim):
    return lax.dot_general(
        left, right, (((left_dim,), (right_dim,)), ((), ())), preferred_element_type=F32
    )


def swap_cores(value):
    return lax.ppermute(value, "c", [(0, 1), (1, 0)])


def exchange(value, axis):
    return lax.all_to_all(value, axis, 0, 0, tiled=True)


def everyone(value, axis, count):
    return exchange(jnp.broadcast_to(value[None], (count, *value.shape)), axis)


def ordered(core, mine, other):
    return jnp.where(core == 0, jnp.stack([mine, other]), jnp.stack([other, mine]))


VMEM = pl.BlockSpec(memory_space=pltpu.VMEM)
SMEM = pl.BlockSpec(memory_space=pltpu.SMEM)


COST = pl.CostEstimate(flops=6 * 10**9, bytes_accessed=24 * 10**6, transcendentals=0)


def dot_nn(a, b):
    return contract(a, b, 1, 0)


def dot_nt(a, b):
    return contract(a, b, 1, 1)


def dot_tn(a, b):
    return contract(a, b, 0, 0)


def call(kernel, name, outs, scratch, *args, cost=None):
    n_scalar = 1
    return pl.pallas_call(
        kernel,
        out_shape=[jax.ShapeDtypeStruct(s, d) for s, d in outs],
        in_specs=[SMEM] * n_scalar + [VMEM] * (len(args) - n_scalar),
        out_specs=[VMEM] * len(outs),
        scratch_shapes=[pltpu.VMEM(s, d) for s, d in scratch],
        compiler_params=pltpu.CompilerParams(vmem_limit_bytes=48 * 1024 * 1024),
        cost_estimate=cost,
        name=name,
    )(*args)


def pack_kernel(*refs):
    states, outs, (held, sems) = refs[:6], refs[6:10], refs[10:]
    x, c = lax.axis_index("x"), lax.axis_index("c")
    copies = [pltpu.make_async_copy(ref, held.at[k], sems.at[k]) for k, ref in enumerate(states)]
    for copy in copies:
        copy.start()
    for copy in copies:
        copy.wait()
    for shift, out in enumerate(outs):
        tile = lax.rem(x + shift, NX)
        for k in range(4):
            out[k] = held[k, tile].astype(BF)
        lefts, rights = held[4, tile], held[5, tile]
        out[4] = jnp.where(c == 0, lefts, rights).astype(BF)
        out[5] = jnp.where(c == 0, rights, lefts).astype(BF)


def shift_of(where, xp):
    return lax.rem(where[0] - xp + NX, NX)


def select_kernel(where, pack, bases, near, far):
    m = where[3]
    bases[...] = pack[:, 0:8]
    for out, steps in ((near, (0, 1)), (far, (0, 2))):
        for j, step in enumerate(steps):
            shift = shift_of(where, lax.rem(m + step, NM))
            for core in range(NC):
                out[:, 2 * core + j] = pack[:, 16 + NX * core + shift]


def block_start(index, size):
    return pl.multiple_of(index * size, size)


def prep_kernel(where, own, oth, left, right):
    c = where[2]

    def step(k, carry):
        z, shift = k // NX, k % NX
        xp = shift_of(where, shift)
        start = xp * (NZ * NC * B) + z * (NC * B)
        for ref, core in ((own, c), (oth, 1 - c)):
            row = pl.multiple_of(start + core * B, B)
            for arr, out in ((0, left), (1, right)):
                for m in range(NM):
                    out[pl.ds(row, B), m * W : (m + 1) * W] = ref[m, z, arr * NX + shift]
        return carry

    lax.fori_loop(0, NZ * NX, step, 0)


def old_power_kernel(where, pack, from1, from3, from2, left, right, out, block):
    c, m = where[2], where[3]

    def fill(n, piece):
        for z in range(NZ):
            for k, core in ((0, c), (1, 1 - c)):
                row = pl.multiple_of(z * (NC * B) + core * B, B)
                block[n, pl.ds(row, B), :] = piece(z, k)

    for u in range(NM):
        shift = shift_of(where, lax.rem(m + u, NM))
        fill(u, lambda z, k: pack[z, 16 + NX * k + shift])
    for n, ref in enumerate((from1, from3, from2)):
        for j in range(2):
            fill(4 + 2 * n + j, lambda z, k: ref[z, 2 * k + j])
    table = (
        ((0, 0), (1, 1), (2, 1), (3, 1)),
        ((1, 0), (6, 0), (7, 1), (5, 0)),
        ((2, 0), (7, 0), (8, 0), (9, 1)),
        ((3, 0), (5, 1), (9, 0), (4, 0)),
    )

    def product(basis):
        for u in range(NM):
            total = None
            for v in range(NM):
                rows = basis[pl.ds(block_start(lax.rem(m + v, NM), W), W), :]
                place, turned = table[u][v]
                part = (dot_tn if turned else dot_nn)(block[place], rows)
                total = part if total is None else total + part
            out[pl.ds(block_start(lax.rem(m + u, NM), W), W), :] = total

    @pl.when(c == 0)
    def _():
        product(left)

    @pl.when(c == 1)
    def _():
        product(right)


def rotate_kernel(where, own, oth, left, right, pack, grad, work, direct, rot_home, rot):
    z, c, m = where[1], where[2], where[3]
    half = own.shape[1]
    for ref, core in ((own, c), (oth, 1 - c)):
        r = pl.ds(block_start(core, half), half)
        for k in range(NM):
            grad[r, k * W : (k + 1) * W] = ref[k]
    col = pl.ds(block_start(m, W), W)

    @pl.when(c == 0)
    def _():
        def rows(i, carry):
            r = pl.ds(block_start(i, W), W)
            work[r, :] = dot_tn(left[:, r], grad[...]).astype(BF)
            rot[r, :] = dot_nn(work[r, :], right[:, col])
            return carry

        lax.fori_loop(0, NM, rows, 0)

    @pl.when(c == 1)
    def _():
        def rows(i, carry):
            r = pl.ds(block_start(i, W), W)
            work[r, :] = dot_nn(grad[r, :], right[...]).astype(BF)
            return carry

        lax.fori_loop(0, NM, rows, 0)

        def more(i, carry):
            r = pl.ds(block_start(i, W), W)
            rot[r, :] = dot_tn(left[:, r], work[:, col])
            return carry

        lax.fori_loop(0, NM, more, 0)

    def step(k, carry):
        xp, zp = k // NZ, k % NZ
        value = rot[pl.ds(pl.multiple_of(k * (NC * B) + c * B, B), B), :]
        one = 0.9 * pack[zp, 2 * NX + shift_of(where, xp)].astype(F32) + 0.1 * value
        two = 0.95 * pack[zp, 3 * NX + shift_of(where, xp)].astype(F32) + 0.05 * value * value
        value = (one / FIX_ONE / (jnp.sqrt(two / FIX_TWO) + 1e-08)).astype(BF)
        for copy in range(NM):
            direct[copy, pl.ds(block_start(k, B), B), :] = value
        return carry

    lax.fori_loop(0, NX * NZ, step, 0)
    for xp in range(NX):
        row = pl.multiple_of(xp * (NZ * NC * B) + z * (NC * B) + c * B, B)
        rot_home[xp] = rot[pl.ds(row, B), :].astype(BF)


def power_kernel(where, grad, work, old, outer, basis, power, iterate):
    z, c, m = where[1], where[2], where[3]
    col = pl.ds(block_start(m, W), W)
    total = NM * W

    def z_rows(xp):
        return pl.ds(pl.multiple_of(xp * (NZ * NC * B) + z * (NC * B), NC * B), NC * B)

    @pl.when(c == 0)
    def _():
        def rows(i, sums):
            r = pl.ds(block_start(i, W), W)
            value = 0.95 * old[r, :] + 0.05 * dot_nt(grad[r, :], work[...])
            power[r, :] = value
            return sums + jnp.sum(value * value, axis=0, keepdims=True)

        sums = lax.fori_loop(0, NM, rows, jnp.zeros((1, total), F32))
        scale = lax.rsqrt(sums + 1e-06)
        for i in range(NM):
            r = slice(i * W, (i + 1) * W)
            iterate[r, :] = (power[r, :] * scale).astype(BF)
        for xp in range(NX):
            outer[xp] = dot_nt(grad[z_rows(xp), :], grad[col, :]).astype(BF)

    @pl.when(c == 1)
    def _():
        def rows(i, sums):
            r = pl.ds(block_start(i, W), W)
            value = 0.95 * old[r, :] + 0.05 * dot_tn(grad[:, r], work[...])
            power[r, :] = value
            return sums + jnp.sum(value * value, axis=0, keepdims=True)

        sums = lax.fori_loop(0, NM, rows, jnp.zeros((1, total), F32))
        scale = lax.rsqrt(sums + 1e-06)
        for i in range(NM):
            r = slice(i * W, (i + 1) * W)
            iterate[r, :] = (power[r, :] * scale).astype(BF)

        def gram_rows(i, carry):
            r = pl.ds(block_start(i, W), W)
            power[r, 0:W] = dot_tn(grad[:, r], grad[:, col])
            return carry

        lax.fori_loop(0, NM, gram_rows, 0)
        for xp in range(NX):
            outer[xp] = power[z_rows(xp), 0:W].astype(BF)

    gram = dot_tn(iterate[:, col], iterate[...]).astype(BF)
    for xp in range(NX):
        here = iterate[z_rows(xp), :]
        value = 1.5 * iterate[z_rows(xp), col].astype(F32) - 0.5 * dot_nt(here, gram)
        basis[xp] = value.astype(BF)


def back_kernel(where, direct, right, back):
    m = where[3]
    rows = pl.ds(block_start(m, W), W)
    total = dot_nt(direct[0], right[rows, 0:W])
    for k in range(1, NM):
        total += dot_nt(direct[k], right[rows, k * W : (k + 1) * W])
    back[...] = total.astype(BF)


def update_kernel(where, own, oth, left, rot_home, outer, basis, norm, sent, back):
    c = where[2]
    half = own.shape[0]

    def step(k, carry):
        src = pl.ds(block_start(k, B), B)
        for ref, core in ((own, c), (oth, 1 - c)):
            back[pl.ds(pl.multiple_of(k * (NC * B) + core * B, B), B), :] = ref[src, :]
        return carry

    lax.fori_loop(0, NX * NZ, step, 0)
    value = dot_nn(left[pl.ds(block_start(c, half), half), :], back[...]).astype(BF)
    for xp in range(NX):
        sent[xp, :half] = value
        sent[xp, half : half + B] = rot_home[xp]
        sent[xp, half + B : half + 3 * B] = outer[xp]
        sent[xp, half + 3 * B : half + 5 * B] = basis[xp]
        sent[xp, half + 5 * B :] = norm[...]


def relay_kernel(where, got, own_slot, sent):
    c = where[2]
    half = own_slot.shape[0]

    def owned(hit, tile):
        value = got[tile, :half]
        return jnp.where(hit > 0, value.astype(F32), 0.0).astype(BF)

    own_slot[...] = owned(where[4], where[5])
    sent[:half] = owned(where[6], where[7])
    nb = NX * B
    for t in range(NX):
        row = pl.multiple_of((1 - c) * B, B)
        sent[half + t * B : half + (t + 1) * B] = got[t, pl.ds(half + B + row, B)]
        sent[half + nb + t * B : half + nb + (t + 1) * B] = got[
            t, pl.ds(half + 3 * B + row, B)
        ]
    sent[half + 2 * nb :] = got[0, half + 5 * B :]
    for t in range(NX):
        row = half + 2 * nb + 2 * t
        sent[row : row + 2] = got[t, half + 5 * B : half + 5 * B + 2]


def final_kernel(
    where, got, own_slot, recv, m1, m2, sl, sr, o1, o2, osl, osr, obl, obr, slot, norm
):
    c = where[2]
    half = own_slot.shape[0]
    nb = NX * B
    slot[0, pl.ds(block_start(c, half), half)] = own_slot[...]
    slot[0, pl.ds(block_start(1 - c, half), half)] = recv[:half]
    row = pl.multiple_of(c * B, B)
    norm_oth = recv[half + 2 * nb :].astype(F32)
    for t in range(NX):
        norm_own = got[t, half + 5 * B :].astype(F32)
        value = norm_own[0:2] + norm_oth[2 * t : 2 * t + 2]
        norm[2 * t : 2 * t + 2] = jnp.where(where[8] > 0, value, 0.0)
        rot = got[t, half : half + B].astype(F32)
        o1[t] = 0.9 * m1[t] + 0.1 * rot
        o2[t] = 0.95 * m2[t] + 0.05 * rot * rot
        outer_own = got[t, pl.ds(half + B + row, B)].astype(F32)
        outer_oth = recv[half + t * B : half + (t + 1) * B].astype(F32)
        basis_own = got[t, pl.ds(half + 3 * B + row, B)].astype(F32)
        basis_oth = recv[half + nb + t * B : half + nb + (t + 1) * B].astype(F32)
        osl[t] = 0.95 * sl[t] + 0.05 * jnp.where(c == 0, outer_own, outer_oth)
        osr[t] = 0.95 * sr[t] + 0.05 * jnp.where(c == 0, outer_oth, outer_own)
        obl[t] = jnp.where(c == 0, basis_own, basis_oth)
        obr[t] = jnp.where(c == 0, basis_oth, basis_own)


def shards(
    features,
    out_grads,
    norm_grads,
    owners,
    moment1,
    moment2,
    left_stats,
    right_stats,
    left_basis,
    right_basis,
    norm_m,
    norm_v,
):
    xi = lax.axis_index("x")
    zi = lax.axis_index("z")
    ci = lax.axis_index("c")
    mi = lax.axis_index("mp")
    mine_dp = (xi * NZ + zi) * NC + ci
    other_dp = (xi * NZ + zi) * NC + (1 - ci)
    left_core = ci == 0
    half = features.shape[1] // 2
    full = 2 * half
    tile_owner = owners[:NX]

    def owned(index):
        hit = tile_owner == index
        which = jnp.sum(jnp.where(hit, jnp.arange(NX, dtype=jnp.int32), 0))
        return [jnp.any(hit).astype(jnp.int32), which]

    where = jnp.stack([xi, zi, ci, mi, *owned(mine_dp), *owned(other_dp), mine_dp == owners[NX]])
    where = where.astype(jnp.int32)

    with jax.named_scope("state_rows"):
        home = pl.pallas_call(
            pack_kernel,
            out_shape=[jax.ShapeDtypeStruct((6, B, W), BF)] * NX,
            in_specs=[pl.BlockSpec(memory_space=pl.ANY)] * 6,
            out_specs=[VMEM] * NX,
            scratch_shapes=[pltpu.VMEM((6, NX, B, W), F32), pltpu.SemaphoreType.DMA((6,))],
            name="pack",
        )(left_basis, right_basis, moment1, moment2, left_stats, right_stats)
        rows = [home[0]] + [
            lax.ppermute(home[s], "x", [(i, (i + s) % NX) for i in range(NX)]) for s in (1, 2, 3)
        ]
        stats_recv = swap_cores(jnp.stack([r[5] for r in rows]))
        pack = jnp.stack([r[:5] for r in rows], axis=1).reshape(5 * NX, B, W)
        pack = jnp.concatenate([pack, stats_recv], axis=0)
        pack = lax.all_gather(pack, "z", axis=0)

    with jax.named_scope("grad_sum"):
        feat_other = lax.dynamic_slice_in_dim(features, (1 - ci) * half, half, 1)
        feat_mine = lax.dynamic_slice_in_dim(features, ci * half, half, 1)
        norm_parts = norm_grads[0].reshape(NX, NZ, NC, 32)

        def partial(feat, core):
            grads = jnp.einsum("ti,tnc->nic", feat, out_grads, preferred_element_type=F32)
            norm = lax.dynamic_index_in_dim(norm_parts, core, 2, keepdims=False)
            norm = jnp.pad(norm.reshape(NX, 1, W), ((0, 0), (0, PAD - 1), (0, 0)))
            return grads, norm

        grads_o, norm_o = partial(feat_other, 1 - ci)
        sent = jnp.concatenate([grads_o.astype(BF), norm_o.astype(BF)], axis=1)
        got = swap_cores(sent)
        grads_s, norm_s = partial(feat_mine, ci)
        acc = jnp.concatenate([grads_s, norm_s], axis=1) + got.astype(F32)
        acc = exchange(acc.astype(BF), "x")

    with jax.named_scope("grad_sum"):
        acc = jnp.sum(acc.astype(F32), axis=0)
        norm_z = jnp.pad(acc[half].reshape(NZ, 1, 32), ((0, 0), (0, PAD - 1), (0, W - 32)))
        acc = jnp.concatenate([acc[:half].reshape(NZ, half // NZ, W), norm_z], axis=1)
        acc = exchange(acc.astype(BF), "z")
        acc, pack = lax.optimization_barrier((acc, pack))
        acc = jnp.sum(acc.astype(F32), axis=0)
        grad_rows = acc[: half // NZ].astype(BF)
        norm_total = acc[half // NZ, :32]

    with jax.named_scope("state_all"):
        piece = (NZ, 4, B, W)
        bases, near, far = call(
            select_kernel,
            "select",
            [((NZ, 8, B, W), BF), (piece, BF), (piece, BF)],
            [],
            where,
            pack,
        )
        bases = lax.all_gather(bases, "mp", axis=0)

        def turn(value, s):
            return lax.ppermute(value, "mp", [(i, (i + s) % NM) for i in range(NM)])

        stats = [turn(far, 1), turn(near, 3), turn(near, 2)]

    new_nm = 0.9 * norm_m + 0.1 * norm_total
    new_nv = 0.95 * norm_v + 0.05 * norm_total * norm_total
    norm_step = new_nm / FIX_ONE / (jnp.sqrt(new_nv / FIX_TWO) + 1e-08)

    with jax.named_scope("grad_all"):
        norm_row = jnp.pad(norm_step.astype(BF)[None], ((0, PAD - 1), (0, W - 32)))
        grad_z = everyone(jnp.concatenate([grad_rows, norm_row], axis=0), "z", NZ)
        norm_zs = grad_z[:, half // NZ, None, :32]
        norm_zs = jnp.where(jnp.arange(NC)[None, :, None] == ci, norm_zs, 0).reshape(2, W)
        grad_half = grad_z[:, : half // NZ].reshape(half, W)
        grad_half, *stats = lax.optimization_barrier((grad_half, *stats))
        grad_half = everyone(grad_half, "mp", NM)
        grad_half, bases = lax.optimization_barrier((grad_half, bases))
        grad_other = swap_cores(grad_half)
        bases_other = swap_cores(bases)
        left, right = call(
            prep_kernel, "prep", [((full, full), BF)] * 2, [], where, bases, bases_other
        )

    with jax.named_scope("rotate"):
        grad, work, direction, rot_home = call(
            rotate_kernel,
            "rotate",
            [
                ((full, full), BF),
                ((full, full), BF),
                ((NM, half, W), BF),
                ((NX, B, W), BF),
            ],
            [((full, W), F32)],
            where,
            grad_half,
            grad_other,
            left,
            right,
            pack,
        )
        direction = exchange(direction, "mp")
    with jax.named_scope("power"):
        (power_old,) = call(
            old_power_kernel,
            "old_power",
            [((full, full), F32)],
            [((10, W, W), BF)],
            where,
            pack,
            *stats,
            left,
            right,
            cost=COST,
        )
        outer, basis = call(
            power_kernel,
            "power",
            [((NX, NC * B, W), BF)] * 2,
            [((full, full), F32), ((full, full), BF)],
            where,
            grad,
            work,
            power_old,
            cost=COST,
        )
        direction, outer, basis = lax.optimization_barrier((direction, outer, basis))
    with jax.named_scope("update"):
        (back,) = call(back_kernel, "back", [((half, W), BF)], [], where, direction, right)
        back_other = swap_cores(back)
        norm_pad = jnp.pad(norm_zs, ((0, PAD - 2), (0, 0)))
        (sent,) = call(
            update_kernel,
            "update",
            [((NX, half + 5 * B + PAD, W), BF)],
            [((full, W), BF)],
            where,
            back,
            back_other,
            left,
            rot_home,
            outer,
            basis,
            norm_pad,
        )

    with jax.named_scope("home"):
        got = exchange(sent, "x")
        nb = NX * B
        own_slot, sent = call(
            relay_kernel,
            "relay",
            [((half, W), BF), ((half + 2 * nb + PAD, W), BF)],
            [],
            where,
            got,
        )
        recv = swap_cores(sent)
        state = ((NX, B, W), F32)
        outs = call(
            final_kernel,
            "final",
            [state] * 6 + [((1, full, W), BF), ((2 * NX, W), F32)],
            [],
            where,
            got,
            own_slot,
            recv,
            moment1,
            moment2,
            left_stats,
            right_stats,
        )
    *outs, norm_slot = outs
    return (*outs, new_nm, new_nv, norm_slot.reshape(1, -1))


def solution(mesh):
    mesh = Mesh(mesh.devices.reshape(NX, NZ, NC, NM), ("x", "z", "c", "mp"))
    dp = ("x", "z", "c")
    state = P(None, dp, "mp")
    in_specs = (
        P(dp, None),
        P(dp, None, "mp"),
        P(dp, None),
        P(),
        state,
        state,
        state,
        state,
        state,
        state,
        P(dp),
        P(dp),
    )
    out_specs = (
        state,
        state,
        state,
        state,
        state,
        state,
        P(dp, None, "mp"),
        P(dp),
        P(dp),
        P(dp, None),
    )
    return jax.shard_map(shards, mesh=mesh, in_specs=in_specs, out_specs=out_specs, check_vma=False)
```

```python
import jax
import jax.numpy as jnp
from jax import lax
from jax.experimental import pallas as pl
from jax.experimental.pallas import tpu as pltpu
from jax.sharding import Mesh, PartitionSpec as P

FIX_ONE = 1.0 - 0.9**10
FIX_TWO = 1.0 - 0.95**10
F32 = jnp.float32
BF = jnp.bfloat16
NX, NZ, NC, NM = 4, 8, 2, 4
B = 16
W = 256
PAD = 16


def contract(left, right, left_dim, right_dim):
    return lax.dot_general(
        left, right, (((left_dim,), (right_dim,)), ((), ())), preferred_element_type=F32
    )


def swap_cores(value):
    return lax.ppermute(value, "c", [(0, 1), (1, 0)])


def exchange(value, axis):
    return lax.all_to_all(value, axis, 0, 0, tiled=True)


def turn(value, s):
    return lax.ppermute(value, "mp", [(i, (i + s) % NM) for i in range(NM)])


def everyone(value, axis, count):
    return exchange(jnp.broadcast_to(value[None], (count, *value.shape)), axis)


def ordered(core, mine, other):
    return jnp.where(core == 0, jnp.stack([mine, other]), jnp.stack([other, mine]))


VMEM = pl.BlockSpec(memory_space=pltpu.VMEM)
SMEM = pl.BlockSpec(memory_space=pltpu.SMEM)


COST = pl.CostEstimate(flops=6 * 10**9, bytes_accessed=24 * 10**6, transcendentals=0)


def dot_nn(a, b):
    return contract(a, b, 1, 0)


def dot_nt(a, b):
    return contract(a, b, 1, 1)


def dot_tn(a, b):
    return contract(a, b, 0, 0)


def call(kernel, name, outs, scratch, *args, cost=None):
    n_scalar = 1
    return pl.pallas_call(
        kernel,
        out_shape=[jax.ShapeDtypeStruct(s, d) for s, d in outs],
        in_specs=[SMEM] * n_scalar + [VMEM] * (len(args) - n_scalar),
        out_specs=[VMEM] * len(outs),
        scratch_shapes=[pltpu.VMEM(s, d) for s, d in scratch],
        compiler_params=pltpu.CompilerParams(vmem_limit_bytes=48 * 1024 * 1024),
        cost_estimate=cost,
        name=name,
    )(*args)


def pack_kernel(*refs):
    states, outs, (held, sems) = refs[:6], refs[6:10], refs[10:]
    x, c = lax.axis_index("x"), lax.axis_index("c")
    copies = [pltpu.make_async_copy(ref, held.at[k], sems.at[k]) for k, ref in enumerate(states)]
    for copy in copies:
        copy.start()
    for copy in copies:
        copy.wait()
    for shift, out in enumerate(outs):
        tile = lax.rem(x + shift, NX)
        for k in range(4):
            out[k] = held[k, tile].astype(BF)
        lefts, rights = held[4, tile], held[5, tile]
        out[4] = jnp.where(c == 0, lefts, rights).astype(BF)
        out[5] = jnp.where(c == 0, rights, lefts).astype(BF)


def join_kernel(*refs):
    *parts, out = refs
    start = 0
    for part in parts:
        out[start : start + part.shape[0]] = part[...]
        start += part.shape[0]


def join(*parts):
    shape = (sum(p.shape[0] for p in parts), *parts[0].shape[1:])
    return pl.pallas_call(
        join_kernel,
        out_shape=jax.ShapeDtypeStruct(shape, parts[0].dtype),
        in_specs=[VMEM] * len(parts),
        out_specs=VMEM,
        name="join",
    )(*parts)


def spread_kernel(r0, r1, r2, r3, other, bases, moments, stats, near, far):
    rows = (r0, r1, r2, r3)
    x, m = lax.axis_index("x"), lax.axis_index("mp")
    for s, ref in enumerate(rows):
        for k in range(2):
            bases[NX * k + s] = ref[k]
            moments[NX * k + s] = ref[2 + k]
        stats[s] = ref[4]
        stats[NX + s] = other[s]
    for out, steps in ((near, (0, 1)), (far, (0, 2))):
        for j, step in enumerate(steps):
            shift = lax.rem(x - lax.rem(m + step, NM) + NX, NX)
            for core in range(NC):
                out[2 * core + j] = stats[NX * core + shift]


def block_start(index, size):
    return pl.multiple_of(index * size, size)


def shift_of(where, xp):
    return lax.rem(where[0] - xp + NX, NX)


def prep_kernel(where, own, oth, left, right):
    c, m = where[2], where[3]

    def step(k, carry):
        z, shift = k // NX, k % NX
        start = shift_of(where, shift) * (NZ * NC * B) + z * (NC * B)
        for ref, core in ((own, c), (oth, 1 - c)):
            row = pl.multiple_of(start + core * B, B)
            for t in range(NM):
                col = block_start(lax.rem(m - t + NM, NM), W)
                left[pl.ds(row, B), pl.ds(col, W)] = ref[z, 2 * NX * t + shift]
                right[pl.ds(row, B), pl.ds(col, W)] = ref[z, 2 * NX * t + NX + shift]
        return carry

    lax.fori_loop(0, NZ * NX, step, 0)


def old_power_kernel(where, pack, left, right, out, block):
    c, m = where[2], where[3]

    def fill(n, piece):
        for z in range(NZ):
            for k, core in ((0, c), (1, 1 - c)):
                row = pl.multiple_of(z * (NC * B) + core * B, B)
                block[n, pl.ds(row, B), :] = piece(z, k)

    for u in range(NM):
        shift = shift_of(where, lax.rem(m + u, NM))
        fill(u, lambda z, k: pack[z, NX * k + shift])
    for n in range(3):
        for j in range(2):
            fill(4 + 2 * n + j, lambda z, k: pack[z, 8 + 4 * n + 2 * k + j])
    table = (
        ((0, 0), (1, 1), (2, 1), (3, 1)),
        ((1, 0), (6, 0), (7, 1), (5, 0)),
        ((2, 0), (7, 0), (8, 0), (9, 1)),
        ((3, 0), (5, 1), (9, 0), (4, 0)),
    )

    def product(basis):
        for u in range(NM):
            total = None
            for v in range(NM):
                rows = basis[pl.ds(block_start(lax.rem(m + v, NM), W), W), :]
                place, turned = table[u][v]
                part = (dot_tn if turned else dot_nn)(block[place], rows)
                total = part if total is None else total + part
            out[pl.ds(block_start(lax.rem(m + u, NM), W), W), :] = total

    @pl.when(c == 0)
    def _():
        product(left)

    @pl.when(c == 1)
    def _():
        product(right)


def rotate_kernel(where, own, oth, left, right, pack, grad, work, direct, rot_home, rot):
    z, c, m = where[1], where[2], where[3]
    half = own.shape[1]
    for ref, core in ((own, c), (oth, 1 - c)):
        r = pl.ds(block_start(core, half), half)
        for k in range(NM):
            grad[r, k * W : (k + 1) * W] = ref[k]
    col = pl.ds(block_start(m, W), W)

    @pl.when(c == 0)
    def _():
        def rows(i, carry):
            r = pl.ds(block_start(i, W), W)
            work[r, :] = dot_tn(left[:, r], grad[...]).astype(BF)
            rot[r, :] = dot_nn(work[r, :], right[:, col])
            return carry

        lax.fori_loop(0, NM, rows, 0)

    @pl.when(c == 1)
    def _():
        def rows(i, carry):
            r = pl.ds(block_start(i, W), W)
            work[r, :] = dot_nn(grad[r, :], right[...]).astype(BF)
            return carry

        lax.fori_loop(0, NM, rows, 0)

        def more(i, carry):
            r = pl.ds(block_start(i, W), W)
            rot[r, :] = dot_tn(left[:, r], work[:, col])
            return carry

        lax.fori_loop(0, NM, more, 0)

    def step(k, carry):
        xp, zp = k // NZ, k % NZ
        value = rot[pl.ds(pl.multiple_of(k * (NC * B) + c * B, B), B), :]
        one = 0.9 * pack[zp, 8 * NX + shift_of(where, xp)].astype(F32) + 0.1 * value
        two = 0.95 * pack[zp, 9 * NX + shift_of(where, xp)].astype(F32) + 0.05 * value * value
        value = (one / FIX_ONE / (jnp.sqrt(two / FIX_TWO) + 1e-08)).astype(BF)
        for copy in range(NM):
            direct[copy, pl.ds(block_start(k, B), B), :] = value
        return carry

    lax.fori_loop(0, NX * NZ, step, 0)
    for xp in range(NX):
        row = pl.multiple_of(xp * (NZ * NC * B) + z * (NC * B) + c * B, B)
        rot_home[xp] = rot[pl.ds(row, B), :].astype(BF)


def power_kernel(where, grad, work, old, outer, basis, power, iterate):
    z, c, m = where[1], where[2], where[3]
    col = pl.ds(block_start(m, W), W)
    total = NM * W

    def z_rows(xp):
        return pl.ds(pl.multiple_of(xp * (NZ * NC * B) + z * (NC * B), NC * B), NC * B)

    @pl.when(c == 0)
    def _():
        def rows(i, sums):
            r = pl.ds(block_start(i, W), W)
            value = 0.95 * old[r, :] + 0.05 * dot_nt(grad[r, :], work[...])
            power[r, :] = value
            return sums + jnp.sum(value * value, axis=0, keepdims=True)

        sums = lax.fori_loop(0, NM, rows, jnp.zeros((1, total), F32))
        scale = lax.rsqrt(sums + 1e-06)
        for i in range(NM):
            r = slice(i * W, (i + 1) * W)
            iterate[r, :] = (power[r, :] * scale).astype(BF)
        for xp in range(NX):
            outer[xp] = dot_nt(grad[z_rows(xp), :], grad[col, :]).astype(BF)

    @pl.when(c == 1)
    def _():
        def rows(i, sums):
            r = pl.ds(block_start(i, W), W)
            value = 0.95 * old[r, :] + 0.05 * dot_tn(grad[:, r], work[...])
            power[r, :] = value
            return sums + jnp.sum(value * value, axis=0, keepdims=True)

        sums = lax.fori_loop(0, NM, rows, jnp.zeros((1, total), F32))
        scale = lax.rsqrt(sums + 1e-06)
        for i in range(NM):
            r = slice(i * W, (i + 1) * W)
            iterate[r, :] = (power[r, :] * scale).astype(BF)

        def gram_rows(i, carry):
            r = pl.ds(block_start(i, W), W)
            power[r, 0:W] = dot_tn(grad[:, r], grad[:, col])
            return carry

        lax.fori_loop(0, NM, gram_rows, 0)
        for xp in range(NX):
            outer[xp] = power[z_rows(xp), 0:W].astype(BF)

    gram = dot_tn(iterate[:, col], iterate[...]).astype(BF)
    for xp in range(NX):
        here = iterate[z_rows(xp), :]
        value = 1.5 * iterate[z_rows(xp), col].astype(F32) - 0.5 * dot_nt(here, gram)
        basis[xp] = value.astype(BF)


def back_kernel(where, direct, right, back):
    m = where[3]
    rows = pl.ds(block_start(m, W), W)
    total = dot_nt(direct[0], right[rows, 0:W])
    for k in range(1, NM):
        total += dot_nt(direct[k], right[rows, k * W : (k + 1) * W])
    back[...] = total.astype(BF)


def update_kernel(where, own, oth, left, rot_home, outer, basis, norm, sent, back):
    c = where[2]
    half = own.shape[0]

    def step(k, carry):
        src = pl.ds(block_start(k, B), B)
        for ref, core in ((own, c), (oth, 1 - c)):
            back[pl.ds(pl.multiple_of(k * (NC * B) + core * B, B), B), :] = ref[src, :]
        return carry

    lax.fori_loop(0, NX * NZ, step, 0)
    value = dot_nn(left[pl.ds(block_start(c, half), half), :], back[...]).astype(BF)
    for xp in range(NX):
        sent[xp, :half] = value
        sent[xp, half : half + B] = rot_home[xp]
        sent[xp, half + B : half + 3 * B] = outer[xp]
        sent[xp, half + 3 * B : half + 5 * B] = basis[xp]
        sent[xp, half + 5 * B :] = norm[...]


def relay_kernel(where, got, own_slot, sent):
    c = where[2]
    half = own_slot.shape[0]

    def owned(hit, tile):
        value = got[tile, :half]
        return jnp.where(hit > 0, value.astype(F32), 0.0).astype(BF)

    own_slot[...] = owned(where[4], where[5])
    sent[:half] = owned(where[6], where[7])
    nb = NX * B
    for t in range(NX):
        row = pl.multiple_of((1 - c) * B, B)
        sent[half + t * B : half + (t + 1) * B] = got[t, pl.ds(half + B + row, B)]
        sent[half + nb + t * B : half + nb + (t + 1) * B] = got[
            t, pl.ds(half + 3 * B + row, B)
        ]
    sent[half + 2 * nb :] = got[0, half + 5 * B :]
    for t in range(NX):
        row = half + 2 * nb + 2 * t
        sent[row : row + 2] = got[t, half + 5 * B : half + 5 * B + 2]


def final_kernel(
    where, got, own_slot, recv, m1, m2, sl, sr, o1, o2, osl, osr, obl, obr, slot, norm
):
    c = where[2]
    half = own_slot.shape[0]
    nb = NX * B
    slot[0, pl.ds(block_start(c, half), half)] = own_slot[...]
    slot[0, pl.ds(block_start(1 - c, half), half)] = recv[:half]
    row = pl.multiple_of(c * B, B)
    norm_oth = recv[half + 2 * nb :].astype(F32)
    for t in range(NX):
        norm_own = got[t, half + 5 * B :].astype(F32)
        value = norm_own[0:2] + norm_oth[2 * t : 2 * t + 2]
        norm[2 * t : 2 * t + 2] = jnp.where(where[8] > 0, value, 0.0)
        rot = got[t, half : half + B].astype(F32)
        o1[t] = 0.9 * m1[t] + 0.1 * rot
        o2[t] = 0.95 * m2[t] + 0.05 * rot * rot
        outer_own = got[t, pl.ds(half + B + row, B)].astype(F32)
        outer_oth = recv[half + t * B : half + (t + 1) * B].astype(F32)
        basis_own = got[t, pl.ds(half + 3 * B + row, B)].astype(F32)
        basis_oth = recv[half + nb + t * B : half + nb + (t + 1) * B].astype(F32)
        osl[t] = 0.95 * sl[t] + 0.05 * jnp.where(c == 0, outer_own, outer_oth)
        osr[t] = 0.95 * sr[t] + 0.05 * jnp.where(c == 0, outer_oth, outer_own)
        obl[t] = jnp.where(c == 0, basis_own, basis_oth)
        obr[t] = jnp.where(c == 0, basis_oth, basis_own)


def shards(
    features,
    out_grads,
    norm_grads,
    owners,
    moment1,
    moment2,
    left_stats,
    right_stats,
    left_basis,
    right_basis,
    norm_m,
    norm_v,
):
    xi = lax.axis_index("x")
    zi = lax.axis_index("z")
    ci = lax.axis_index("c")
    mi = lax.axis_index("mp")
    mine_dp = (xi * NZ + zi) * NC + ci
    other_dp = (xi * NZ + zi) * NC + (1 - ci)
    left_core = ci == 0
    half = features.shape[1] // 2
    full = 2 * half
    tile_owner = owners[:NX]

    def owned(index):
        hit = tile_owner == index
        which = jnp.sum(jnp.where(hit, jnp.arange(NX, dtype=jnp.int32), 0))
        return [jnp.any(hit).astype(jnp.int32), which]

    where = jnp.stack([xi, zi, ci, mi, *owned(mine_dp), *owned(other_dp), mine_dp == owners[NX]])
    where = where.astype(jnp.int32)

    with jax.named_scope("state_rows"):
        home = pl.pallas_call(
            pack_kernel,
            out_shape=[jax.ShapeDtypeStruct((6, B, W), BF)] * NX,
            in_specs=[pl.BlockSpec(memory_space=pl.ANY)] * 6,
            out_specs=[VMEM] * NX,
            scratch_shapes=[pltpu.VMEM((6, NX, B, W), F32), pltpu.SemaphoreType.DMA((6,))],
            name="pack",
        )(left_basis, right_basis, moment1, moment2, left_stats, right_stats)
        rows = [home[0]] + [
            lax.ppermute(home[s], "x", [(i, (i + s) % NX) for i in range(NX)]) for s in (1, 2, 3)
        ]
    with jax.named_scope("grad_sum"):
        feat_other = lax.dynamic_slice_in_dim(features, (1 - ci) * half, half, 1)
        feat_mine = lax.dynamic_slice_in_dim(features, ci * half, half, 1)
        norm_parts = norm_grads[0].reshape(NX, NZ, NC, 32)

        def partial(feat, core):
            grads = jnp.einsum("ti,tnc->nic", feat, out_grads, preferred_element_type=F32)
            norm = lax.dynamic_index_in_dim(norm_parts, core, 2, keepdims=False)
            norm = jnp.pad(norm.reshape(NX, 1, W), ((0, 0), (0, PAD - 1), (0, 0)))
            return grads, norm

        grads_o, norm_o = partial(feat_other, 1 - ci)
        sent = jnp.concatenate([grads_o.astype(BF), norm_o.astype(BF)], axis=1)
        *rows, sent = lax.optimization_barrier((*rows, sent))
        got = swap_cores(sent)
        stats_recv = swap_cores(jnp.stack([r[5] for r in rows]))
        rows_of_z = lambda n: jax.ShapeDtypeStruct((n, B, W), BF)
        bases, moments, stats, near, far = pl.pallas_call(
            spread_kernel,
            out_shape=[rows_of_z(n) for n in (8, 8, 8, 4, 4)],
            in_specs=[VMEM] * 5,
            out_specs=[VMEM] * 5,
            name="spread",
        )(*rows, stats_recv)
        turned = [turn(bases, s) for s in (1, 2, 3)]
        grads_s, norm_s = partial(feat_mine, ci)
        acc = jnp.concatenate([grads_s, norm_s], axis=1) + got.astype(F32)
        acc, *turned = lax.optimization_barrier((acc.astype(BF), *turned))
        pack = lax.all_gather(join(bases, *turned, moments), "z", axis=0)
        acc = exchange(acc, "x")
        stats = join(stats, turn(far, 1), turn(near, 3), turn(near, 2))

    with jax.named_scope("grad_sum"):
        acc = jnp.sum(acc.astype(F32), axis=0)
        norm_z = jnp.pad(acc[half].reshape(NZ, 1, 32), ((0, 0), (0, PAD - 1), (0, W - 32)))
        acc = jnp.concatenate([acc[:half].reshape(NZ, half // NZ, W), norm_z], axis=1)
        acc = exchange(acc.astype(BF), "z")
        acc = jnp.sum(acc.astype(F32), axis=0)
        grad_rows = acc[: half // NZ].astype(BF)
        norm_total = acc[half // NZ, :32]

    new_nm = 0.9 * norm_m + 0.1 * norm_total
    new_nv = 0.95 * norm_v + 0.05 * norm_total * norm_total
    norm_step = new_nm / FIX_ONE / (jnp.sqrt(new_nv / FIX_TWO) + 1e-08)

    with jax.named_scope("grad_all"):
        norm_row = jnp.pad(norm_step.astype(BF)[None], ((0, PAD - 1), (0, W - 32)))
        grad_z = everyone(jnp.concatenate([grad_rows, norm_row], axis=0), "z", NZ)
        norm_zs = grad_z[:, half // NZ, None, :32]
        norm_zs = jnp.where(jnp.arange(NC)[None, :, None] == ci, norm_zs, 0).reshape(2, W)
        grad_half = grad_z[:, : half // NZ].reshape(half, W)
        pack, norm_zs, stats = lax.optimization_barrier((pack, norm_zs, stats))
        stats = lax.all_gather(stats, "z", axis=0)
        pack_other = swap_cores(pack)
        left, right = call(
            prep_kernel,
            "prep",
            [((full, full), BF)] * 2,
            [],
            where,
            pack,
            pack_other,
            cost=COST,
        )
        grad_half = everyone(grad_half, "mp", NM)
        grad_half, left, right = lax.optimization_barrier((grad_half, left, right))
        grad_other = swap_cores(grad_half)

    with jax.named_scope("rotate"):
        grad, work, direction, rot_home = call(
            rotate_kernel,
            "rotate",
            [
                ((full, full), BF),
                ((full, full), BF),
                ((NM, half, W), BF),
                ((NX, B, W), BF),
            ],
            [((full, W), F32)],
            where,
            grad_half,
            grad_other,
            left,
            right,
            pack,
        )
        stats, rot_home = lax.optimization_barrier((stats, rot_home))
        direction = exchange(direction, "mp")
    with jax.named_scope("power"):
        (power_old,) = call(
            old_power_kernel,
            "old_power",
            [((full, full), F32)],
            [((10, W, W), BF)],
            where,
            stats,
            left,
            right,
            cost=COST,
        )
        outer, basis = call(
            power_kernel,
            "power",
            [((NX, NC * B, W), BF)] * 2,
            [((full, full), F32), ((full, full), BF)],
            where,
            grad,
            work,
            power_old,
            cost=COST,
        )
        direction, outer, basis = lax.optimization_barrier((direction, outer, basis))
    with jax.named_scope("update"):
        (back,) = call(back_kernel, "back", [((half, W), BF)], [], where, direction, right)
        back_other = swap_cores(back)
        norm_pad = jnp.pad(norm_zs, ((0, PAD - 2), (0, 0)))
        (sent,) = call(
            update_kernel,
            "update",
            [((NX, half + 5 * B + PAD, W), BF)],
            [((full, W), BF)],
            where,
            back,
            back_other,
            left,
            rot_home,
            outer,
            basis,
            norm_pad,
        )

    with jax.named_scope("home"):
        got = exchange(sent, "x")
        nb = NX * B
        own_slot, sent = call(
            relay_kernel,
            "relay",
            [((half, W), BF), ((half + 2 * nb + PAD, W), BF)],
            [],
            where,
            got,
        )
        recv = swap_cores(sent)
        state = ((NX, B, W), F32)
        outs = call(
            final_kernel,
            "final",
            [state] * 6 + [((1, full, W), BF), ((2 * NX, W), F32)],
            [],
            where,
            got,
            own_slot,
            recv,
            moment1,
            moment2,
            left_stats,
            right_stats,
        )
    *outs, norm_slot = outs
    return (*outs, new_nm, new_nv, norm_slot.reshape(1, -1))


def solution(mesh):
    mesh = Mesh(mesh.devices.reshape(NX, NZ, NC, NM), ("x", "z", "c", "mp"))
    dp = ("x", "z", "c")
    state = P(None, dp, "mp")
    in_specs = (
        P(dp, None),
        P(dp, None, "mp"),
        P(dp, None),
        P(),
        state,
        state,
        state,
        state,
        state,
        state,
        P(dp),
        P(dp),
    )
    out_specs = (
        state,
        state,
        state,
        state,
        state,
        state,
        P(dp, None, "mp"),
        P(dp),
        P(dp),
        P(dp, None),
    )
    return jax.shard_map(shards, mesh=mesh, in_specs=in_specs, out_specs=out_specs, check_vma=False)
```

```python
import jax
import jax.numpy as jnp
from jax import lax
from jax.experimental import pallas as pl
from jax.experimental.pallas import tpu as pltpu
from jax.sharding import Mesh, PartitionSpec as P

FIX_ONE = 1.0 - 0.9**10
FIX_TWO = 1.0 - 0.95**10
F32 = jnp.float32
BF = jnp.bfloat16
NX, NZ, NC, NM = 4, 8, 2, 4
B = 16
W = 256
PAD = 16


def contract(left, right, left_dim, right_dim):
    return lax.dot_general(
        left, right, (((left_dim,), (right_dim,)), ((), ())), preferred_element_type=F32
    )


def swap_cores(value):
    return lax.ppermute(value, "c", [(0, 1), (1, 0)])


def exchange(value, axis):
    return lax.all_to_all(value, axis, 0, 0, tiled=True)


def turn(value, s):
    return lax.ppermute(value, "mp", [(i, (i + s) % NM) for i in range(NM)])


def everyone(value, axis, count):
    return exchange(jnp.broadcast_to(value[None], (count, *value.shape)), axis)


def ordered(core, mine, other):
    return jnp.where(core == 0, jnp.stack([mine, other]), jnp.stack([other, mine]))


VMEM = pl.BlockSpec(memory_space=pltpu.VMEM)
SMEM = pl.BlockSpec(memory_space=pltpu.SMEM)


COST = pl.CostEstimate(flops=6 * 10**9, bytes_accessed=24 * 10**6, transcendentals=0)


def dot_nn(a, b):
    return contract(a, b, 1, 0)


def dot_nt(a, b):
    return contract(a, b, 1, 1)


def dot_tn(a, b):
    return contract(a, b, 0, 0)


def call(kernel, name, outs, scratch, *args, cost=None):
    n_scalar = 1
    return pl.pallas_call(
        kernel,
        out_shape=[jax.ShapeDtypeStruct(s, d) for s, d in outs],
        in_specs=[SMEM] * n_scalar + [VMEM] * (len(args) - n_scalar),
        out_specs=[VMEM] * len(outs),
        scratch_shapes=[pltpu.VMEM(s, d) for s, d in scratch],
        compiler_params=pltpu.CompilerParams(vmem_limit_bytes=16 * 1024 * 1024),
        cost_estimate=cost,
        name=name,
    )(*args)


def pack_kernel(*refs):
    states, outs, (held, sems) = refs[:6], refs[6:10], refs[10:]
    x, c = lax.axis_index("x"), lax.axis_index("c")
    copies = [pltpu.make_async_copy(ref, held.at[k], sems.at[k]) for k, ref in enumerate(states)]
    for copy in copies:
        copy.start()
    for copy in copies:
        copy.wait()
    for shift, out in enumerate(outs):
        tile = lax.rem(x + shift, NX)
        for k in range(4):
            out[k] = held[k, tile].astype(BF)
        lefts, rights = held[4, tile], held[5, tile]
        out[4] = jnp.where(c == 0, lefts, rights).astype(BF)
        out[5] = jnp.where(c == 0, rights, lefts).astype(BF)


def join_kernel(*refs):
    *parts, out = refs
    start = 0
    for part in parts:
        out[start : start + part.shape[0]] = part[...]
        start += part.shape[0]


def join(*parts):
    shape = (sum(p.shape[0] for p in parts), *parts[0].shape[1:])
    return pl.pallas_call(
        join_kernel,
        out_shape=jax.ShapeDtypeStruct(shape, parts[0].dtype),
        in_specs=[VMEM] * len(parts),
        out_specs=VMEM,
        name="join",
    )(*parts)


def spread_kernel(r0, r1, r2, r3, trigger, bases, moments, keep, send):
    for s, ref in enumerate((r0, r1, r2, r3)):
        for k in range(2):
            bases[NX * k + s] = ref[k]
            moments[NX * k + s] = ref[2 + k]
        keep[s] = ref[4]
        send[s] = ref[5]


def choose_kernel(keep, other, trigger, stats, near, far):
    x, m = lax.axis_index("x"), lax.axis_index("mp")
    stats[:NX] = keep[...]
    stats[NX:] = other[...]
    for out, steps in ((near, (0, 1)), (far, (0, 2))):
        for j, step in enumerate(steps):
            shift = lax.rem(x - lax.rem(m + step, NM) + NX, NX)
            out[j] = keep[shift]
            out[2 + j] = other[shift]


def small(kernel, name, counts, *args):
    return pl.pallas_call(
        kernel,
        out_shape=[jax.ShapeDtypeStruct((n, B, W), BF) for n in counts],
        in_specs=[VMEM] * (len(args) - 1) + [pl.BlockSpec(memory_space=pl.ANY)],
        out_specs=[VMEM] * len(counts),
        name=name,
    )(*args)


def block_start(index, size):
    return pl.multiple_of(index * size, size)


def shift_of(where, xp):
    return lax.rem(where[0] - xp + NX, NX)


def prep_kernel(where, own, oth, left, right):
    c, m = where[2], where[3]
    for shift in range(NX):
        start = shift_of(where, shift) * (NZ * NC * B)
        for t in range(NM):
            col = block_start(lax.rem(m - t + NM, NM), W)
            for z in range(NZ):
                for ref, core in ((own, c), (oth, 1 - c)):
                    row = pl.multiple_of(start + z * (NC * B) + core * B, B)
                    left[pl.ds(row, B), pl.ds(col, W)] = ref[z, 2 * NX * t + shift]
                    right[pl.ds(row, B), pl.ds(col, W)] = ref[z, 2 * NX * t + NX + shift]


def old_power_kernel(where, pack, left, right, out, block):
    c, m = where[2], where[3]

    def fill(n, piece):
        for z in range(NZ):
            for k, core in ((0, c), (1, 1 - c)):
                row = pl.multiple_of(z * (NC * B) + core * B, B)
                block[n, pl.ds(row, B), :] = piece(z, k)

    for u in range(NM):
        shift = shift_of(where, lax.rem(m + u, NM))
        fill(u, lambda z, k: pack[z, NX * k + shift])
    for n in range(3):
        for j in range(2):
            fill(4 + 2 * n + j, lambda z, k: pack[z, 8 + 4 * n + 2 * k + j])
    table = (
        ((0, 0), (1, 1), (2, 1), (3, 1)),
        ((1, 0), (6, 0), (7, 1), (5, 0)),
        ((2, 0), (7, 0), (8, 0), (9, 1)),
        ((3, 0), (5, 1), (9, 0), (4, 0)),
    )

    def product(basis):
        for u in range(NM):
            total = None
            for v in range(NM):
                rows = basis[pl.ds(block_start(lax.rem(m + v, NM), W), W), :]
                place, turned = table[u][v]
                part = (dot_tn if turned else dot_nn)(block[place], rows)
                total = part if total is None else total + part
            out[pl.ds(block_start(lax.rem(m + u, NM), W), W), :] = total

    @pl.when(c == 0)
    def _():
        product(left)

    @pl.when(c == 1)
    def _():
        product(right)


def rotate_kernel(where, own, oth, left, right, pack, grad, work, direct, rot_home, rot):
    z, c, m = where[1], where[2], where[3]
    half = own.shape[1]
    for ref, core in ((own, c), (oth, 1 - c)):
        r = pl.ds(block_start(core, half), half)
        for k in range(NM):
            grad[r, k * W : (k + 1) * W] = ref[k]
    col = pl.ds(block_start(m, W), W)

    @pl.when(c == 0)
    def _():
        work[...] = dot_tn(left[...], grad[...]).astype(BF)
        rot[...] = dot_nn(work[...], right[:, col])

    @pl.when(c == 1)
    def _():
        work[...] = dot_nn(grad[...], right[...]).astype(BF)
        rot[...] = dot_tn(left[...], work[:, col])

    for xp in range(NX):
        shift = shift_of(where, xp)
        for zp in range(NZ):
            k = xp * NZ + zp
            value = rot[pl.ds(pl.multiple_of(k * (NC * B) + c * B, B), B), :]
            one = 0.9 * pack[zp, 8 * NX + shift].astype(F32) + 0.1 * value
            two = 0.95 * pack[zp, 9 * NX + shift].astype(F32) + 0.05 * value * value
            value = (one / FIX_ONE / (jnp.sqrt(two / FIX_TWO) + 1e-08)).astype(BF)
            for copy in range(NM):
                direct[copy, k * B : (k + 1) * B, :] = value
    for xp in range(NX):
        row = pl.multiple_of(xp * (NZ * NC * B) + z * (NC * B) + c * B, B)
        rot_home[xp] = rot[pl.ds(row, B), :].astype(BF)


def power_kernel(where, grad, work, old, outer, basis, power, iterate):
    z, c, m = where[1], where[2], where[3]
    col = pl.ds(block_start(m, W), W)
    total = NM * W

    def z_rows(xp):
        return pl.ds(pl.multiple_of(xp * (NZ * NC * B) + z * (NC * B), NC * B), NC * B)

    @pl.when(c == 0)
    def _():
        def rows(i, sums):
            r = pl.ds(block_start(i, W), W)
            value = 0.95 * old[r, :] + 0.05 * dot_nt(grad[r, :], work[...])
            power[r, :] = value
            return sums + jnp.sum(value * value, axis=0, keepdims=True)

        sums = lax.fori_loop(0, NM, rows, jnp.zeros((1, total), F32))
        scale = lax.rsqrt(sums + 1e-06)
        for i in range(NM):
            r = slice(i * W, (i + 1) * W)
            iterate[r, :] = (power[r, :] * scale).astype(BF)
        for xp in range(NX):
            outer[xp] = dot_nt(grad[z_rows(xp), :], grad[col, :]).astype(BF)

    @pl.when(c == 1)
    def _():
        def rows(i, sums):
            r = pl.ds(block_start(i, W), W)
            value = 0.95 * old[r, :] + 0.05 * dot_tn(grad[:, r], work[...])
            power[r, :] = value
            return sums + jnp.sum(value * value, axis=0, keepdims=True)

        sums = lax.fori_loop(0, NM, rows, jnp.zeros((1, total), F32))
        scale = lax.rsqrt(sums + 1e-06)
        for i in range(NM):
            r = slice(i * W, (i + 1) * W)
            iterate[r, :] = (power[r, :] * scale).astype(BF)

        def gram_rows(i, carry):
            r = pl.ds(block_start(i, W), W)
            power[r, 0:W] = dot_tn(grad[:, r], grad[:, col])
            return carry

        lax.fori_loop(0, NM, gram_rows, 0)
        for xp in range(NX):
            outer[xp] = power[z_rows(xp), 0:W].astype(BF)

    gram = dot_tn(iterate[:, col], iterate[...]).astype(BF)
    for xp in range(NX):
        here = iterate[z_rows(xp), :]
        value = 1.5 * iterate[z_rows(xp), col].astype(F32) - 0.5 * dot_nt(here, gram)
        basis[xp] = value.astype(BF)


def back_kernel(where, direct, right, back):
    m = where[3]
    rows = pl.ds(block_start(m, W), W)
    total = dot_nt(direct[0], right[rows, 0:W])
    for k in range(1, NM):
        total += dot_nt(direct[k], right[rows, k * W : (k + 1) * W])
    back[...] = total.astype(BF)


def update_kernel(where, own, oth, left, rot_home, outer, basis, norm, sent, back):
    c = where[2]
    half = own.shape[0]

    def step(k, carry):
        src = pl.ds(block_start(k, B), B)
        for ref, core in ((own, c), (oth, 1 - c)):
            back[pl.ds(pl.multiple_of(k * (NC * B) + core * B, B), B), :] = ref[src, :]
        return carry

    lax.fori_loop(0, NX * NZ, step, 0)
    value = dot_nn(left[pl.ds(block_start(c, half), half), :], back[...]).astype(BF)
    for xp in range(NX):
        sent[xp, :half] = value
        sent[xp, half : half + B] = rot_home[xp]
        sent[xp, half + B : half + 3 * B] = outer[xp]
        sent[xp, half + 3 * B : half + 5 * B] = basis[xp]
        sent[xp, half + 5 * B :] = norm[...]


def relay_kernel(where, got, own_slot, sent):
    c = where[2]
    half = own_slot.shape[0]

    def owned(hit, tile):
        value = got[tile, :half]
        return jnp.where(hit > 0, value.astype(F32), 0.0).astype(BF)

    own_slot[...] = owned(where[4], where[5])
    sent[:half] = owned(where[6], where[7])
    nb = NX * B
    for t in range(NX):
        row = pl.multiple_of((1 - c) * B, B)
        sent[half + t * B : half + (t + 1) * B] = got[t, pl.ds(half + B + row, B)]
        sent[half + nb + t * B : half + nb + (t + 1) * B] = got[
            t, pl.ds(half + 3 * B + row, B)
        ]
    sent[half + 2 * nb :] = got[0, half + 5 * B :]
    for t in range(NX):
        row = half + 2 * nb + 2 * t
        sent[row : row + 2] = got[t, half + 5 * B : half + 5 * B + 2]


def final_kernel(
    where, got, own_slot, recv, m1, m2, sl, sr, o1, o2, osl, osr, obl, obr, slot, norm
):
    c = where[2]
    half = own_slot.shape[0]
    nb = NX * B
    slot[0, pl.ds(block_start(c, half), half)] = own_slot[...]
    slot[0, pl.ds(block_start(1 - c, half), half)] = recv[:half]
    row = pl.multiple_of(c * B, B)
    norm_oth = recv[half + 2 * nb :].astype(F32)
    for t in range(NX):
        norm_own = got[t, half + 5 * B :].astype(F32)
        value = norm_own[0:2] + norm_oth[2 * t : 2 * t + 2]
        norm[2 * t : 2 * t + 2] = jnp.where(where[8] > 0, value, 0.0)
        rot = got[t, half : half + B].astype(F32)
        o1[t] = 0.9 * m1[t] + 0.1 * rot
        o2[t] = 0.95 * m2[t] + 0.05 * rot * rot
        outer_own = got[t, pl.ds(half + B + row, B)].astype(F32)
        outer_oth = recv[half + t * B : half + (t + 1) * B].astype(F32)
        basis_own = got[t, pl.ds(half + 3 * B + row, B)].astype(F32)
        basis_oth = recv[half + nb + t * B : half + nb + (t + 1) * B].astype(F32)
        osl[t] = 0.95 * sl[t] + 0.05 * jnp.where(c == 0, outer_own, outer_oth)
        osr[t] = 0.95 * sr[t] + 0.05 * jnp.where(c == 0, outer_oth, outer_own)
        obl[t] = jnp.where(c == 0, basis_own, basis_oth)
        obr[t] = jnp.where(c == 0, basis_oth, basis_own)


def shards(
    features,
    out_grads,
    norm_grads,
    owners,
    moment1,
    moment2,
    left_stats,
    right_stats,
    left_basis,
    right_basis,
    norm_m,
    norm_v,
):
    xi = lax.axis_index("x")
    zi = lax.axis_index("z")
    ci = lax.axis_index("c")
    mi = lax.axis_index("mp")
    mine_dp = (xi * NZ + zi) * NC + ci
    other_dp = (xi * NZ + zi) * NC + (1 - ci)
    left_core = ci == 0
    half = features.shape[1] // 2
    full = 2 * half
    tile_owner = owners[:NX]

    def owned(index):
        hit = tile_owner == index
        which = jnp.sum(jnp.where(hit, jnp.arange(NX, dtype=jnp.int32), 0))
        return [jnp.any(hit).astype(jnp.int32), which]

    where = jnp.stack([xi, zi, ci, mi, *owned(mine_dp), *owned(other_dp), mine_dp == owners[NX]])
    where = where.astype(jnp.int32)

    with jax.named_scope("state_rows"):
        home = pl.pallas_call(
            pack_kernel,
            out_shape=[jax.ShapeDtypeStruct((6, B, W), BF)] * NX,
            in_specs=[pl.BlockSpec(memory_space=pl.ANY)] * 6,
            out_specs=[VMEM] * NX,
            scratch_shapes=[pltpu.VMEM((6, NX, B, W), F32), pltpu.SemaphoreType.DMA((6,))],
            name="pack",
        )(left_basis, right_basis, moment1, moment2, left_stats, right_stats)
        rows = [home[0]] + [
            lax.ppermute(home[s], "x", [(i, (i + s) % NX) for i in range(NX)]) for s in (1, 2, 3)
        ]
    with jax.named_scope("grad_sum"):
        feat_other = lax.dynamic_slice_in_dim(features, (1 - ci) * half, half, 1)
        feat_mine = lax.dynamic_slice_in_dim(features, ci * half, half, 1)
        norm = jnp.pad(norm_grads.reshape(NX, 2, W), ((0, 0), (0, PAD - 2), (0, 0)))

        def partial(feat):
            return jnp.einsum("ti,tnc->nic", feat, out_grads, preferred_element_type=F32)

        sent = jnp.concatenate([partial(feat_other).astype(BF), norm.astype(BF)], axis=1)
        *rows, sent = lax.optimization_barrier((*rows, sent))
        got = swap_cores(sent)
        acc = jnp.concatenate([partial(feat_mine), norm], axis=1) + got.astype(F32)
        acc = acc.astype(BF)
        bases, moments, keep, send = small(spread_kernel, "spread", (8, 8, 4, 4), *rows, acc)
        turned = [turn(bases, s) for s in (1, 2, 3)]
        pack = lax.all_gather(join(bases, *turned, moments), "z", axis=0)
        tile = lambda s: lax.dynamic_index_in_dim(acc, lax.rem(xi + s, NX), 0, keepdims=False)
        acc = [tile(0)] + [
            lax.ppermute(tile(s), "x", [(i, (i + s) % NX) for i in range(NX)]) for s in (2, 1, 3)
        ]

    with jax.named_scope("grad_sum"):
        acc = sum(a.astype(F32) for a in acc)
        norm_z = acc[half : half + 2].reshape(NZ, 1, 64)
        norm_z = jnp.pad(norm_z, ((0, 0), (0, PAD - 1), (0, W - 64)))
        acc = jnp.concatenate([acc[:half].reshape(NZ, half // NZ, W), norm_z], axis=1)
        acc = acc.astype(BF)
        stats, near, far = small(choose_kernel, "choose", (8, 4, 4), keep, swap_cores(send), acc)
        stats = join(stats, turn(far, 1), turn(near, 3), turn(near, 2))
        acc = exchange(acc, "z")
        acc = jnp.sum(acc.astype(F32), axis=0)
        grad_rows = acc[: half // NZ].astype(BF)
        norm_total = jnp.where(ci == 0, acc[half // NZ, :32], acc[half // NZ, 32:64])

    new_nm = 0.9 * norm_m + 0.1 * norm_total
    new_nv = 0.95 * norm_v + 0.05 * norm_total * norm_total
    norm_step = new_nm / FIX_ONE / (jnp.sqrt(new_nv / FIX_TWO) + 1e-08)

    with jax.named_scope("grad_all"):
        norm_row = jnp.pad(norm_step.astype(BF)[None], ((0, PAD - 1), (0, W - 32)))
        grad_z = everyone(jnp.concatenate([grad_rows, norm_row], axis=0), "z", NZ)
        norm_zs = grad_z[:, half // NZ, None, :32]
        norm_zs = jnp.where(jnp.arange(NC)[None, :, None] == ci, norm_zs, 0).reshape(2, W)
        grad_half = grad_z[:, : half // NZ].reshape(half, W)
        pack, norm_zs, stats = lax.optimization_barrier((pack, norm_zs, stats))
        stats = lax.all_gather(stats, "z", axis=0)
        pack_other = swap_cores(pack)
        left, right = call(
            prep_kernel,
            "prep",
            [((full, full), BF)] * 2,
            [],
            where,
            pack,
            pack_other,
            cost=COST,
        )
        grad_half = everyone(grad_half, "mp", NM)
        grad_half, left, right = lax.optimization_barrier((grad_half, left, right))
        grad_other = swap_cores(grad_half)

    with jax.named_scope("rotate"):
        grad, work, direction, rot_home = call(
            rotate_kernel,
            "rotate",
            [
                ((full, full), BF),
                ((full, full), BF),
                ((NM, half, W), BF),
                ((NX, B, W), BF),
            ],
            [((full, W), F32)],
            where,
            grad_half,
            grad_other,
            left,
            right,
            pack,
        )
        stats, rot_home = lax.optimization_barrier((stats, rot_home))
        direction = exchange(direction, "mp")
    with jax.named_scope("power"):
        (power_old,) = call(
            old_power_kernel,
            "old_power",
            [((full, full), F32)],
            [((10, W, W), BF)],
            where,
            stats,
            left,
            right,
            cost=COST,
        )
        outer, basis = call(
            power_kernel,
            "power",
            [((NX, NC * B, W), BF)] * 2,
            [((full, full), F32), ((full, full), BF)],
            where,
            grad,
            work,
            power_old,
            cost=COST,
        )
        direction, outer, basis = lax.optimization_barrier((direction, outer, basis))
    with jax.named_scope("update"):
        (back,) = call(back_kernel, "back", [((half, W), BF)], [], where, direction, right)
        back_other = swap_cores(back)
        norm_pad = jnp.pad(norm_zs, ((0, PAD - 2), (0, 0)))
        (sent,) = call(
            update_kernel,
            "update",
            [((NX, half + 5 * B + PAD, W), BF)],
            [((full, W), BF)],
            where,
            back,
            back_other,
            left,
            rot_home,
            outer,
            basis,
            norm_pad,
        )

    with jax.named_scope("home"):
        got = exchange(sent, "x")
        nb = NX * B
        own_slot, sent = call(
            relay_kernel,
            "relay",
            [((half, W), BF), ((half + 2 * nb + PAD, W), BF)],
            [],
            where,
            got,
        )
        recv = swap_cores(sent)
        state = ((NX, B, W), F32)
        outs = call(
            final_kernel,
            "final",
            [state] * 6 + [((1, full, W), BF), ((2 * NX, W), F32)],
            [],
            where,
            got,
            own_slot,
            recv,
            moment1,
            moment2,
            left_stats,
            right_stats,
        )
    *outs, norm_slot = outs
    return (*outs, new_nm, new_nv, norm_slot.reshape(1, -1))


def solution(mesh):
    mesh = Mesh(mesh.devices.reshape(NX, NZ, NC, NM), ("x", "z", "c", "mp"))
    dp = ("x", "z", "c")
    state = P(None, dp, "mp")
    in_specs = (
        P(dp, None),
        P(dp, None, "mp"),
        P(dp, None),
        P(),
        state,
        state,
        state,
        state,
        state,
        state,
        P(dp),
        P(dp),
    )
    out_specs = (
        state,
        state,
        state,
        state,
        state,
        state,
        P(dp, None, "mp"),
        P(dp),
        P(dp),
        P(dp, None),
    )
    return jax.shard_map(shards, mesh=mesh, in_specs=in_specs, out_specs=out_specs, check_vma=False)
```

```python
import jax
import jax.numpy as jnp
from jax import lax
from jax.experimental import pallas as pl
from jax.experimental.pallas import tpu as pltpu
from jax.sharding import Mesh, PartitionSpec as P

FIX_ONE = 1.0 - 0.9**10
FIX_TWO = 1.0 - 0.95**10
F32 = jnp.float32
BF = jnp.bfloat16
NX, NZ, NC, NM = 4, 8, 2, 4
B = 16
W = 256
PAD = 16


def contract(left, right, left_dim, right_dim):
    return lax.dot_general(
        left, right, (((left_dim,), (right_dim,)), ((), ())), preferred_element_type=F32
    )


def swap_cores(value):
    return lax.ppermute(value, "c", [(0, 1), (1, 0)])


def exchange(value, axis):
    return lax.all_to_all(value, axis, 0, 0, tiled=True)


def turn(value, s):
    return lax.ppermute(value, "mp", [(i, (i + s) % NM) for i in range(NM)])


def turn_x(value, s):
    return lax.ppermute(value, "x", [(i, (i + s) % NX) for i in range(NX)])


def all_turns(value, turn_by):
    far = turn_by(value, 2)
    return [value, turn_by(value, 1), far, turn_by(value, 3)]


def everyone(value, axis, count):
    return exchange(jnp.broadcast_to(value[None], (count, *value.shape)), axis)


def ordered(core, mine, other):
    return jnp.where(core == 0, jnp.stack([mine, other]), jnp.stack([other, mine]))


VMEM = pl.BlockSpec(memory_space=pltpu.VMEM)
SMEM = pl.BlockSpec(memory_space=pltpu.SMEM)


COST = pl.CostEstimate(flops=6 * 10**9, bytes_accessed=24 * 10**6, transcendentals=0)


def dot_nn(a, b):
    return contract(a, b, 1, 0)


def dot_nt(a, b):
    return contract(a, b, 1, 1)


def dot_tn(a, b):
    return contract(a, b, 0, 0)


def call(kernel, name, outs, scratch, *args, cost=None):
    n_scalar = 1
    return pl.pallas_call(
        kernel,
        out_shape=[jax.ShapeDtypeStruct(s, d) for s, d in outs],
        in_specs=[SMEM] * n_scalar + [VMEM] * (len(args) - n_scalar),
        out_specs=[VMEM] * len(outs),
        scratch_shapes=[pltpu.VMEM(s, d) for s, d in scratch],
        compiler_params=pltpu.CompilerParams(vmem_limit_bytes=16 * 1024 * 1024),
        cost_estimate=cost,
        name=name,
    )(*args)


def pack_kernel(*refs):
    states, outs, (held, sems) = refs[:6], refs[6:10], refs[10:]
    x, c = lax.axis_index("x"), lax.axis_index("c")
    copies = [pltpu.make_async_copy(ref, held.at[k], sems.at[k]) for k, ref in enumerate(states)]
    for copy in copies:
        copy.start()
    for copy in copies:
        copy.wait()
    for shift, out in enumerate(outs):
        tile = lax.rem(x + shift, NX)
        for k in range(4):
            out[k] = held[k, tile].astype(BF)
        lefts, rights = held[4, tile], held[5, tile]
        out[4] = jnp.where(c == 0, lefts, rights).astype(BF)
        out[5] = jnp.where(c == 0, rights, lefts).astype(BF)


def join_kernel(*refs):
    *parts, out = refs
    start = 0
    for part in parts:
        out[start : start + part.shape[0]] = part[...]
        start += part.shape[0]


def join(*parts):
    shape = (sum(p.shape[0] for p in parts), *parts[0].shape[1:])
    return pl.pallas_call(
        join_kernel,
        out_shape=jax.ShapeDtypeStruct(shape, parts[0].dtype),
        in_specs=[VMEM] * len(parts),
        out_specs=VMEM,
        name="join",
    )(*parts)


def spread_kernel(r0, r1, r2, r3, trigger, bases, moments, keep, send):
    for s, ref in enumerate((r0, r1, r2, r3)):
        for k in range(2):
            bases[NX * k + s] = ref[k]
            moments[NX * k + s] = ref[2 + k]
        keep[s] = ref[4]
        send[s] = ref[5]


def choose_kernel(keep, other, trigger, stats, near, far):
    x, m = lax.axis_index("x"), lax.axis_index("mp")
    stats[:NX] = keep[...]
    stats[NX:] = other[...]
    for out, steps in ((near, (0, 1)), (far, (0, 2))):
        for j, step in enumerate(steps):
            shift = lax.rem(x - lax.rem(m + step, NM) + NX, NX)
            out[j] = keep[shift]
            out[2 + j] = other[shift]


def small(kernel, name, counts, *args):
    return pl.pallas_call(
        kernel,
        out_shape=[jax.ShapeDtypeStruct((n, B, W), BF) for n in counts],
        in_specs=[VMEM] * (len(args) - 1) + [pl.BlockSpec(memory_space=pl.ANY)],
        out_specs=[VMEM] * len(counts),
        name=name,
    )(*args)


def block_start(index, size):
    return pl.multiple_of(index * size, size)


def shift_of(where, xp):
    return lax.rem(where[0] - xp + NX, NX)


def prep_kernel(where, own, oth, left, right):
    c, m = where[2], where[3]
    for shift in range(NX):
        start = shift_of(where, shift) * (NZ * NC * B)
        for t in range(NM):
            col = block_start(lax.rem(m - t + NM, NM), W)
            for z in range(NZ):
                for ref, core in ((own, c), (oth, 1 - c)):
                    row = pl.multiple_of(start + z * (NC * B) + core * B, B)
                    left[pl.ds(row, B), pl.ds(col, W)] = ref[z, 2 * NX * t + shift]
                    right[pl.ds(row, B), pl.ds(col, W)] = ref[z, 2 * NX * t + NX + shift]


def old_power_kernel(where, pack, left, right, out, block):
    c, m = where[2], where[3]

    def fill(n, piece):
        for z in range(NZ):
            for k, core in ((0, c), (1, 1 - c)):
                row = pl.multiple_of(z * (NC * B) + core * B, B)
                block[n, pl.ds(row, B), :] = piece(z, k)

    for u in range(NM):
        shift = shift_of(where, lax.rem(m + u, NM))
        fill(u, lambda z, k: pack[z, NX * k + shift])
    for n in range(3):
        for j in range(2):
            fill(4 + 2 * n + j, lambda z, k: pack[z, 8 + 4 * n + 2 * k + j])
    table = (
        ((0, 0), (1, 1), (2, 1), (3, 1)),
        ((1, 0), (6, 0), (7, 1), (5, 0)),
        ((2, 0), (7, 0), (8, 0), (9, 1)),
        ((3, 0), (5, 1), (9, 0), (4, 0)),
    )

    def product(basis):
        for u in range(NM):
            total = None
            for v in range(NM):
                rows = basis[pl.ds(block_start(lax.rem(m + v, NM), W), W), :]
                place, turned = table[u][v]
                part = (dot_tn if turned else dot_nn)(block[place], rows)
                total = part if total is None else total + part
            out[pl.ds(block_start(lax.rem(m + u, NM), W), W), :] = total

    @pl.when(c == 0)
    def _():
        product(left)

    @pl.when(c == 1)
    def _():
        product(right)


def rotate_kernel(where, *refs):
    own, oth = refs[:NM], refs[NM : 2 * NM]
    left, right, pack, grad, work, direct, rot_home, rot = refs[2 * NM :]
    z, c, m = where[1], where[2], where[3]
    half = own[0].shape[0]
    for pieces, core in ((own, c), (oth, 1 - c)):
        r = pl.ds(block_start(core, half), half)
        for s in range(NM):
            grad[r, pl.ds(block_start(lax.rem(m - s + NM, NM), W), W)] = pieces[s][...]
    col = pl.ds(block_start(m, W), W)

    @pl.when(c == 0)
    def _():
        work[...] = dot_tn(left[...], grad[...]).astype(BF)
        rot[...] = dot_nn(work[...], right[:, col])

    @pl.when(c == 1)
    def _():
        work[...] = dot_nn(grad[...], right[...]).astype(BF)
        rot[...] = dot_tn(left[...], work[:, col])

    for xp in range(NX):
        shift = shift_of(where, xp)
        for zp in range(NZ):
            k = xp * NZ + zp
            value = rot[pl.ds(pl.multiple_of(k * (NC * B) + c * B, B), B), :]
            one = 0.9 * pack[zp, 8 * NX + shift].astype(F32) + 0.1 * value
            two = 0.95 * pack[zp, 9 * NX + shift].astype(F32) + 0.05 * value * value
            value = (one / FIX_ONE / (jnp.sqrt(two / FIX_TWO) + 1e-08)).astype(BF)
            direct[k * B : (k + 1) * B, :] = value
    for xp in range(NX):
        row = pl.multiple_of(xp * (NZ * NC * B) + z * (NC * B) + c * B, B)
        rot_home[xp] = rot[pl.ds(row, B), :].astype(BF)


def power_kernel(where, grad, work, old, outer, basis, power, iterate):
    z, c, m = where[1], where[2], where[3]
    col = pl.ds(block_start(m, W), W)
    total = NM * W

    def z_rows(xp):
        return pl.ds(pl.multiple_of(xp * (NZ * NC * B) + z * (NC * B), NC * B), NC * B)

    @pl.when(c == 0)
    def _():
        def rows(i, sums):
            r = pl.ds(block_start(i, W), W)
            value = 0.95 * old[r, :] + 0.05 * dot_nt(grad[r, :], work[...])
            power[r, :] = value
            return sums + jnp.sum(value * value, axis=0, keepdims=True)

        sums = lax.fori_loop(0, NM, rows, jnp.zeros((1, total), F32))
        scale = lax.rsqrt(sums + 1e-06)
        for i in range(NM):
            r = slice(i * W, (i + 1) * W)
            iterate[r, :] = (power[r, :] * scale).astype(BF)
        for xp in range(NX):
            outer[xp] = dot_nt(grad[z_rows(xp), :], grad[col, :]).astype(BF)

    @pl.when(c == 1)
    def _():
        def rows(i, sums):
            r = pl.ds(block_start(i, W), W)
            value = 0.95 * old[r, :] + 0.05 * dot_tn(grad[:, r], work[...])
            power[r, :] = value
            return sums + jnp.sum(value * value, axis=0, keepdims=True)

        sums = lax.fori_loop(0, NM, rows, jnp.zeros((1, total), F32))
        scale = lax.rsqrt(sums + 1e-06)
        for i in range(NM):
            r = slice(i * W, (i + 1) * W)
            iterate[r, :] = (power[r, :] * scale).astype(BF)

        def gram_rows(i, carry):
            r = pl.ds(block_start(i, W), W)
            power[r, 0:W] = dot_tn(grad[:, r], grad[:, col])
            return carry

        lax.fori_loop(0, NM, gram_rows, 0)
        for xp in range(NX):
            outer[xp] = power[z_rows(xp), 0:W].astype(BF)

    gram = dot_tn(iterate[:, col], iterate[...]).astype(BF)
    for xp in range(NX):
        here = iterate[z_rows(xp), :]
        value = 1.5 * iterate[z_rows(xp), col].astype(F32) - 0.5 * dot_nt(here, gram)
        basis[xp] = value.astype(BF)


def back_kernel(where, d0, d1, d2, d3, right, back):
    m = where[3]
    rows = pl.ds(block_start(m, W), W)
    total = None
    for k, ref in enumerate((d0, d1, d2, d3)):
        col = pl.ds(block_start(lax.rem(m - k + NM, NM), W), W)
        part = dot_nt(ref[...], right[rows, col])
        total = part if total is None else total + part
    back[...] = total.astype(BF)


def update_kernel(where, own, oth, left, sent, back):
    c = where[2]
    half = own.shape[0]

    def step(k, carry):
        src = pl.ds(block_start(k, B), B)
        for ref, core in ((own, c), (oth, 1 - c)):
            back[pl.ds(pl.multiple_of(k * (NC * B) + core * B, B), B), :] = ref[src, :]
        return carry

    lax.fori_loop(0, NX * NZ, step, 0)
    value = dot_nn(left[pl.ds(block_start(c, half), half), :], back[...]).astype(BF)
    sent[...] = value


def rest_kernel(rot_home, outer, basis, norm, out):
    for xp in range(NX):
        out[xp, :B] = rot_home[xp]
        out[xp, B : 3 * B] = outer[xp]
        out[xp, 3 * B : 5 * B] = basis[xp]
        out[xp, 5 * B :] = norm[...]


def relay_kernel(where, u0, u1, u2, u3, h0, h1, h2, h3, own_slot, sent):
    c = where[2]
    half = own_slot.shape[0]
    nb = NX * B
    for out, hit, tile in ((own_slot, where[4], where[5]), (sent, where[6], where[7])):
        place = shift_of(where, tile)

        @pl.when(hit == 0)
        def _():
            out[:half] = jnp.zeros((half, W), BF)

        for s, ref in enumerate((u0, u1, u2, u3)):

            @pl.when((hit > 0) & (place == s))
            def _():
                out[:half] = ref[...]

    row = pl.multiple_of((1 - c) * B, B)
    for s, ref in enumerate((h0, h1, h2, h3)):
        sent[half + s * B : half + (s + 1) * B] = ref[pl.ds(B + row, B)]
        sent[half + nb + s * B : half + nb + (s + 1) * B] = ref[pl.ds(3 * B + row, B)]
        sent[half + 2 * nb + s * PAD : half + 2 * nb + (s + 1) * PAD] = ref[5 * B :]


def final_kernel(
    where,
    h0,
    h1,
    h2,
    h3,
    own_slot,
    recv,
    m1,
    m2,
    sl,
    sr,
    o1,
    o2,
    osl,
    osr,
    obl,
    obr,
    slot,
    norm,
):
    c = where[2]
    half = own_slot.shape[0]
    nb = NX * B
    slot[0, pl.ds(block_start(c, half), half)] = own_slot[...]
    slot[0, pl.ds(block_start(1 - c, half), half)] = recv[:half]
    row = pl.multiple_of(c * B, B)
    for s, ref in enumerate((h0, h1, h2, h3)):
        t = shift_of(where, s)
        other = recv[half + 2 * nb + s * PAD : half + 2 * nb + (s + 1) * PAD].astype(F32)
        value = (ref[5 * B :].astype(F32) + other)[0:2]
        norm[t] = jnp.where(where[8] > 0, value, 0.0)
        rot = ref[:B].astype(F32)
        o1[t] = 0.9 * m1[t] + 0.1 * rot
        o2[t] = 0.95 * m2[t] + 0.05 * rot * rot
        outer_own = ref[pl.ds(B + row, B)].astype(F32)
        outer_oth = recv[half + s * B : half + (s + 1) * B].astype(F32)
        basis_own = ref[pl.ds(3 * B + row, B)].astype(F32)
        basis_oth = recv[half + nb + s * B : half + nb + (s + 1) * B].astype(F32)
        osl[t] = 0.95 * sl[t] + 0.05 * jnp.where(c == 0, outer_own, outer_oth)
        osr[t] = 0.95 * sr[t] + 0.05 * jnp.where(c == 0, outer_oth, outer_own)
        obl[t] = jnp.where(c == 0, basis_own, basis_oth)
        obr[t] = jnp.where(c == 0, basis_oth, basis_own)


def shards(
    features,
    out_grads,
    norm_grads,
    owners,
    moment1,
    moment2,
    left_stats,
    right_stats,
    left_basis,
    right_basis,
    norm_m,
    norm_v,
):
    xi = lax.axis_index("x")
    zi = lax.axis_index("z")
    ci = lax.axis_index("c")
    mi = lax.axis_index("mp")
    mine_dp = (xi * NZ + zi) * NC + ci
    other_dp = (xi * NZ + zi) * NC + (1 - ci)
    left_core = ci == 0
    half = features.shape[1] // 2
    full = 2 * half
    tile_owner = owners[:NX]

    def owned(index):
        hit = tile_owner == index
        which = jnp.sum(jnp.where(hit, jnp.arange(NX, dtype=jnp.int32), 0))
        return [jnp.any(hit).astype(jnp.int32), which]

    where = jnp.stack([xi, zi, ci, mi, *owned(mine_dp), *owned(other_dp), mine_dp == owners[NX]])
    where = where.astype(jnp.int32)

    with jax.named_scope("state_rows"):
        home = pl.pallas_call(
            pack_kernel,
            out_shape=[jax.ShapeDtypeStruct((6, B, W), BF)] * NX,
            in_specs=[pl.BlockSpec(memory_space=pl.ANY)] * 6,
            out_specs=[VMEM] * NX,
            scratch_shapes=[pltpu.VMEM((6, NX, B, W), F32), pltpu.SemaphoreType.DMA((6,))],
            name="pack",
        )(left_basis, right_basis, moment1, moment2, left_stats, right_stats)
        rows = [home[0]] + [
            lax.ppermute(home[s], "x", [(i, (i + s) % NX) for i in range(NX)]) for s in (1, 2, 3)
        ]
    with jax.named_scope("grad_sum"):
        feat_other = lax.dynamic_slice_in_dim(features, (1 - ci) * half, half, 1)
        feat_mine = lax.dynamic_slice_in_dim(features, ci * half, half, 1)
        norm = jnp.pad(norm_grads.reshape(NX, 2, W), ((0, 0), (0, PAD - 2), (0, 0)))

        def partial(feat):
            return jnp.einsum("ti,tnc->nic", feat, out_grads, preferred_element_type=F32)

        sent = jnp.concatenate([partial(feat_other).astype(BF), norm.astype(BF)], axis=1)
        *rows, sent = lax.optimization_barrier((*rows, sent))
        got = swap_cores(sent)
        acc = jnp.concatenate([partial(feat_mine), norm], axis=1) + got.astype(F32)
        acc = acc.astype(BF)
        bases, moments, keep, send = small(spread_kernel, "spread", (8, 8, 4, 4), *rows, acc)
        turned = [turn(bases, s) for s in (1, 2, 3)]
        pack = join(bases, *turned, moments)
        stats, near, far = small(choose_kernel, "choose", (8, 4, 4), keep, swap_cores(send), pack)
        stats = join(stats, turn(far, 1), turn(near, 3), turn(near, 2))
        pack = lax.all_gather(pack, "z", axis=0)
        tile = lambda s: lax.dynamic_index_in_dim(acc, lax.rem(xi + s, NX), 0, keepdims=False)
        acc = [tile(0)] + [
            lax.ppermute(tile(s), "x", [(i, (i + s) % NX) for i in range(NX)]) for s in (2, 1, 3)
        ]

    with jax.named_scope("grad_sum"):
        acc = sum(a.astype(F32) for a in acc)
        norm_z = acc[half : half + 2].reshape(NZ, 1, 64)
        norm_z = jnp.pad(norm_z, ((0, 0), (0, PAD - 1), (0, W - 64)))
        acc = jnp.concatenate([acc[:half].reshape(NZ, half // NZ, W), norm_z], axis=1)
        acc = acc.astype(BF)
        acc, stats = lax.optimization_barrier((acc, stats))
        stats = lax.all_gather(stats, "z", axis=0)
        acc = exchange(acc, "z")
        acc = jnp.sum(acc.astype(F32), axis=0)
        grad_rows = acc[: half // NZ].astype(BF)
        norm_total = jnp.where(ci == 0, acc[half // NZ, :32], acc[half // NZ, 32:64])

    new_nm = 0.9 * norm_m + 0.1 * norm_total
    new_nv = 0.95 * norm_v + 0.05 * norm_total * norm_total
    norm_step = new_nm / FIX_ONE / (jnp.sqrt(new_nv / FIX_TWO) + 1e-08)

    with jax.named_scope("grad_all"):
        norm_row = jnp.pad(norm_step.astype(BF)[None], ((0, PAD - 1), (0, W - 32)))
        grad_z = everyone(jnp.concatenate([grad_rows, norm_row], axis=0), "z", NZ)
        norm_zs = grad_z[:, half // NZ, None, :32]
        norm_zs = jnp.where(jnp.arange(NC)[None, :, None] == ci, norm_zs, 0).reshape(2, W)
        grad_half = grad_z[:, : half // NZ].reshape(half, W)
        grad_own = all_turns(grad_half, turn)
        pack, norm_zs = lax.optimization_barrier((pack, norm_zs))
        pack_other = swap_cores(pack)
        left, right = call(
            prep_kernel,
            "prep",
            [((full, full), BF)] * 2,
            [],
            where,
            pack,
            pack_other,
            cost=COST,
        )
        grad_own[2], left, right = lax.optimization_barrier((grad_own[2], left, right))
        grad_other = [swap_cores(piece) for piece in grad_own]

    with jax.named_scope("rotate"):
        grad, work, direction, rot_home = call(
            rotate_kernel,
            "rotate",
            [
                ((full, full), BF),
                ((full, full), BF),
                ((half, W), BF),
                ((NX, B, W), BF),
            ],
            [((full, W), F32)],
            where,
            *grad_own,
            *grad_other,
            left,
            right,
            pack,
        )
        stats, rot_home = lax.optimization_barrier((stats, rot_home))
        direction = all_turns(direction, turn)
    with jax.named_scope("power"):
        (power_old,) = call(
            old_power_kernel,
            "old_power",
            [((full, full), F32)],
            [((10, W, W), BF)],
            where,
            stats,
            left,
            right,
            cost=COST,
        )
        outer, basis = call(
            power_kernel,
            "power",
            [((NX, NC * B, W), BF)] * 2,
            [((full, full), F32), ((full, full), BF)],
            where,
            grad,
            work,
            power_old,
            cost=COST,
        )
        norm_pad = jnp.pad(norm_zs, ((0, PAD - 2), (0, 0)))
        rest = pl.pallas_call(
            rest_kernel,
            out_shape=jax.ShapeDtypeStruct((NX, 5 * B + PAD, W), BF),
            in_specs=[VMEM] * 4,
            out_specs=VMEM,
            name="rest",
        )(rot_home, outer, basis, norm_pad)
        tile = lambda s: lax.dynamic_index_in_dim(rest, lax.rem(xi + s, NX), 0, keepdims=False)
        direction[2], rest = lax.optimization_barrier((direction[2], rest))
        rest = [tile(0)] + [turn_x(tile(s), s) for s in (1, 2, 3)]
    with jax.named_scope("update"):
        (back,) = call(back_kernel, "back", [((half, W), BF)], [], where, *direction, right)
        back_other = swap_cores(back)
        (update,) = call(
            update_kernel,
            "update",
            [((half, W), BF)],
            [((full, W), BF)],
            where,
            back,
            back_other,
            left,
        )

    with jax.named_scope("home"):
        update, *rest = lax.optimization_barrier((update, *rest))
        update = all_turns(update, turn_x)
        nb = NX * B
        own_slot, sent = call(
            relay_kernel,
            "relay",
            [((half, W), BF), ((half + 2 * nb + NX * PAD, W), BF)],
            [],
            where,
            *update,
            *rest,
        )
        recv = swap_cores(sent)
        state = ((NX, B, W), F32)
        outs = call(
            final_kernel,
            "final",
            [state] * 6 + [((1, full, W), BF), ((NX, 2, W), F32)],
            [],
            where,
            *rest,
            own_slot,
            recv,
            moment1,
            moment2,
            left_stats,
            right_stats,
        )
    *outs, norm_slot = outs
    return (*outs, new_nm, new_nv, norm_slot.reshape(1, -1))


def solution(mesh):
    mesh = Mesh(mesh.devices.reshape(NX, NZ, NC, NM), ("x", "z", "c", "mp"))
    dp = ("x", "z", "c")
    state = P(None, dp, "mp")
    in_specs = (
        P(dp, None),
        P(dp, None, "mp"),
        P(dp, None),
        P(),
        state,
        state,
        state,
        state,
        state,
        state,
        P(dp),
        P(dp),
    )
    out_specs = (
        state,
        state,
        state,
        state,
        state,
        state,
        P(dp, None, "mp"),
        P(dp),
        P(dp),
        P(dp, None),
    )
    return jax.shard_map(shards, mesh=mesh, in_specs=in_specs, out_specs=out_specs, check_vma=False)
```

```python
import jax
import jax.numpy as jnp
from jax import lax
from jax.experimental import pallas as pl
from jax.experimental.pallas import tpu as pltpu
from jax.sharding import Mesh, PartitionSpec as P

FIX_ONE = 1.0 - 0.9**10
FIX_TWO = 1.0 - 0.95**10
F32 = jnp.float32
BF = jnp.bfloat16
NX, NZ, NC, NM = 4, 8, 2, 4
B = 16
W = 256
PAD = 16


def contract(left, right, left_dim, right_dim):
    return lax.dot_general(
        left, right, (((left_dim,), (right_dim,)), ((), ())), preferred_element_type=F32
    )


def swap_cores(value):
    return lax.ppermute(value, "c", [(0, 1), (1, 0)])


def exchange(value, axis):
    return lax.all_to_all(value, axis, 0, 0, tiled=True)


def turn(value, s):
    return lax.ppermute(value, "mp", [(i, (i + s) % NM) for i in range(NM)])


def turn_x(value, s):
    return lax.ppermute(value, "x", [(i, (i + s) % NX) for i in range(NX)])


def all_turns(value, turn_by):
    far = turn_by(value, 2)
    return [value, turn_by(value, 1), far, turn_by(value, 3)]


def everyone(value, axis, count):
    return exchange(jnp.broadcast_to(value[None], (count, *value.shape)), axis)


def ordered(core, mine, other):
    return jnp.where(core == 0, jnp.stack([mine, other]), jnp.stack([other, mine]))


VMEM = pl.BlockSpec(memory_space=pltpu.VMEM)
SMEM = pl.BlockSpec(memory_space=pltpu.SMEM)


COST = pl.CostEstimate(flops=6 * 10**9, bytes_accessed=24 * 10**6, transcendentals=0)


def dot_nn(a, b):
    return contract(a, b, 1, 0)


def dot_nt(a, b):
    return contract(a, b, 1, 1)


def dot_tn(a, b):
    return contract(a, b, 0, 0)


def call(kernel, name, outs, scratch, *args, cost=None):
    n_scalar = 1
    return pl.pallas_call(
        kernel,
        out_shape=[jax.ShapeDtypeStruct(s, d) for s, d in outs],
        in_specs=[SMEM] * n_scalar + [VMEM] * (len(args) - n_scalar),
        out_specs=[VMEM] * len(outs),
        scratch_shapes=[pltpu.VMEM(s, d) for s, d in scratch],
        compiler_params=pltpu.CompilerParams(vmem_limit_bytes=16 * 1024 * 1024),
        cost_estimate=cost,
        name=name,
    )(*args)


def pack_kernel(*refs):
    states, outs, (held, sems) = refs[:6], refs[6:10], refs[10:]
    x, c = lax.axis_index("x"), lax.axis_index("c")
    copies = [pltpu.make_async_copy(ref, held.at[k], sems.at[k]) for k, ref in enumerate(states)]
    for copy in copies:
        copy.start()
    for copy in copies:
        copy.wait()
    for shift, out in enumerate(outs):
        tile = lax.rem(x + shift, NX)
        for k in range(4):
            out[k] = held[k, tile].astype(BF)
        lefts, rights = held[4, tile], held[5, tile]
        out[4] = jnp.where(c == 0, lefts, rights).astype(BF)
        out[5] = jnp.where(c == 0, rights, lefts).astype(BF)


def join_kernel(*refs):
    *parts, out = refs
    start = 0
    for part in parts:
        out[start : start + part.shape[0]] = part[...]
        start += part.shape[0]


def join(*parts):
    shape = (sum(p.shape[0] for p in parts), *parts[0].shape[1:])
    return pl.pallas_call(
        join_kernel,
        out_shape=jax.ShapeDtypeStruct(shape, parts[0].dtype),
        in_specs=[VMEM] * len(parts),
        out_specs=VMEM,
        name="join",
    )(*parts)


def sum_kernel(a0, a1, a2, a3, out):
    size = out.shape[1] - PAD
    half = size * NZ

    def added(rows):
        total = a0[rows].astype(F32)
        for ref in (a1, a2, a3):
            total += ref[rows].astype(F32)
        return total.astype(BF)

    norm = added(slice(half, half + PAD))
    for z in range(NZ):
        out[z, :size] = added(slice(z * size, (z + 1) * size))
        out[z, size:] = norm


def spread_kernel(r0, r1, r2, r3, trigger, bases, moments, keep, send):
    for s, ref in enumerate((r0, r1, r2, r3)):
        for k in range(2):
            bases[NX * k + s] = ref[k]
            moments[NX * k + s] = ref[2 + k]
        keep[s] = ref[4]
        send[s] = ref[5]


def choose_kernel(keep, other, trigger, stats, near, far):
    x, m = lax.axis_index("x"), lax.axis_index("mp")
    stats[:NX] = keep[...]
    stats[NX:] = other[...]
    for out, steps in ((near, (0, 1)), (far, (0, 2))):
        for j, step in enumerate(steps):
            shift = lax.rem(x - lax.rem(m + step, NM) + NX, NX)
            out[j] = keep[shift]
            out[2 + j] = other[shift]


def small(kernel, name, counts, *args):
    return pl.pallas_call(
        kernel,
        out_shape=[jax.ShapeDtypeStruct((n, B, W), BF) for n in counts],
        in_specs=[VMEM] * (len(args) - 1) + [pl.BlockSpec(memory_space=pl.ANY)],
        out_specs=[VMEM] * len(counts),
        name=name,
    )(*args)


def block_start(index, size):
    return pl.multiple_of(index * size, size)


def shift_of(where, xp):
    return lax.rem(where[0] - xp + NX, NX)


def prep_kernel(where, own, oth, left, right):
    c, m = where[2], where[3]
    for shift in range(NX):
        start = shift_of(where, shift) * (NZ * NC * B)
        for t in range(NM):
            col = block_start(lax.rem(m - t + NM, NM), W)
            for z in range(NZ):
                for ref, core in ((own, c), (oth, 1 - c)):
                    row = pl.multiple_of(start + z * (NC * B) + core * B, B)
                    left[pl.ds(row, B), pl.ds(col, W)] = ref[z, 2 * NX * t + shift]
                    right[pl.ds(row, B), pl.ds(col, W)] = ref[z, 2 * NX * t + NX + shift]


def old_power_kernel(where, pack, left, right, out, block):
    c, m = where[2], where[3]

    def fill(n, piece):
        for z in range(NZ):
            for k, core in ((0, c), (1, 1 - c)):
                row = pl.multiple_of(z * (NC * B) + core * B, B)
                block[n, pl.ds(row, B), :] = piece(z, k)

    for u in range(NM):
        shift = shift_of(where, lax.rem(m + u, NM))
        fill(u, lambda z, k: pack[z, NX * k + shift])
    for n in range(3):
        for j in range(2):
            fill(4 + 2 * n + j, lambda z, k: pack[z, 8 + 4 * n + 2 * k + j])
    table = (
        ((0, 0), (1, 1), (2, 1), (3, 1)),
        ((1, 0), (6, 0), (7, 1), (5, 0)),
        ((2, 0), (7, 0), (8, 0), (9, 1)),
        ((3, 0), (5, 1), (9, 0), (4, 0)),
    )

    def product(basis):
        for u in range(NM):
            total = None
            for v in range(NM):
                rows = basis[pl.ds(block_start(lax.rem(m + v, NM), W), W), :]
                place, turned = table[u][v]
                part = (dot_tn if turned else dot_nn)(block[place], rows)
                total = part if total is None else total + part
            out[pl.ds(block_start(lax.rem(m + u, NM), W), W), :] = total

    @pl.when(c == 0)
    def _():
        product(left)

    @pl.when(c == 1)
    def _():
        product(right)


def rotate_kernel(where, *refs):
    own, oth = refs[:NM], refs[NM : 2 * NM]
    left, right, pack, grad, work, direct, rot_home, rot = refs[2 * NM :]
    z, c, m = where[1], where[2], where[3]
    half = own[0].shape[0]
    for pieces, core in ((own, c), (oth, 1 - c)):
        r = pl.ds(block_start(core, half), half)
        for s in range(NM):
            grad[r, pl.ds(block_start(lax.rem(m - s + NM, NM), W), W)] = pieces[s][...]
    col = pl.ds(block_start(m, W), W)

    @pl.when(c == 0)
    def _():
        work[...] = dot_tn(left[...], grad[...]).astype(BF)
        rot[...] = dot_nn(work[...], right[:, col])

    @pl.when(c == 1)
    def _():
        work[...] = dot_nn(grad[...], right[...]).astype(BF)
        rot[...] = dot_tn(left[...], work[:, col])

    for xp in range(NX):
        shift = shift_of(where, xp)
        for zp in range(NZ):
            k = xp * NZ + zp
            value = rot[pl.ds(pl.multiple_of(k * (NC * B) + c * B, B), B), :]
            one = 0.9 * pack[zp, 8 * NX + shift].astype(F32) + 0.1 * value
            two = 0.95 * pack[zp, 9 * NX + shift].astype(F32) + 0.05 * value * value
            value = (one / FIX_ONE / (jnp.sqrt(two / FIX_TWO) + 1e-08)).astype(BF)
            direct[k * B : (k + 1) * B, :] = value
    for xp in range(NX):
        row = pl.multiple_of(xp * (NZ * NC * B) + z * (NC * B) + c * B, B)
        rot_home[xp] = rot[pl.ds(row, B), :].astype(BF)


def power_kernel(where, grad, work, old, outer, basis, power, iterate):
    z, c, m = where[1], where[2], where[3]
    col = pl.ds(block_start(m, W), W)
    total = NM * W

    def z_rows(xp):
        return pl.ds(pl.multiple_of(xp * (NZ * NC * B) + z * (NC * B), NC * B), NC * B)

    @pl.when(c == 0)
    def _():
        def rows(i, sums):
            r = pl.ds(block_start(i, W), W)
            value = 0.95 * old[r, :] + 0.05 * dot_nt(grad[r, :], work[...])
            power[r, :] = value
            return sums + jnp.sum(value * value, axis=0, keepdims=True)

        sums = lax.fori_loop(0, NM, rows, jnp.zeros((1, total), F32))
        scale = lax.rsqrt(sums + 1e-06)
        for i in range(NM):
            r = slice(i * W, (i + 1) * W)
            iterate[r, :] = (power[r, :] * scale).astype(BF)
        for xp in range(NX):
            outer[xp] = dot_nt(grad[z_rows(xp), :], grad[col, :]).astype(BF)

    @pl.when(c == 1)
    def _():
        def rows(i, sums):
            r = pl.ds(block_start(i, W), W)
            value = 0.95 * old[r, :] + 0.05 * dot_tn(grad[:, r], work[...])
            power[r, :] = value
            return sums + jnp.sum(value * value, axis=0, keepdims=True)

        sums = lax.fori_loop(0, NM, rows, jnp.zeros((1, total), F32))
        scale = lax.rsqrt(sums + 1e-06)
        for i in range(NM):
            r = slice(i * W, (i + 1) * W)
            iterate[r, :] = (power[r, :] * scale).astype(BF)

        def gram_rows(i, carry):
            r = pl.ds(block_start(i, W), W)
            power[r, 0:W] = dot_tn(grad[:, r], grad[:, col])
            return carry

        lax.fori_loop(0, NM, gram_rows, 0)
        for xp in range(NX):
            outer[xp] = power[z_rows(xp), 0:W].astype(BF)

    gram = dot_tn(iterate[:, col], iterate[...]).astype(BF)
    for xp in range(NX):
        here = iterate[z_rows(xp), :]
        value = 1.5 * iterate[z_rows(xp), col].astype(F32) - 0.5 * dot_nt(here, gram)
        basis[xp] = value.astype(BF)


def back_kernel(where, d0, d1, d2, d3, right, back):
    m = where[3]
    rows = pl.ds(block_start(m, W), W)
    total = None
    for k, ref in enumerate((d0, d1, d2, d3)):
        col = pl.ds(block_start(lax.rem(m - k + NM, NM), W), W)
        part = dot_nt(ref[...], right[rows, col])
        total = part if total is None else total + part
    back[...] = total.astype(BF)


def update_kernel(where, own, oth, left, sent, back):
    c = where[2]
    half = own.shape[0]

    def step(k, carry):
        src = pl.ds(block_start(k, B), B)
        for ref, core in ((own, c), (oth, 1 - c)):
            back[pl.ds(pl.multiple_of(k * (NC * B) + core * B, B), B), :] = ref[src, :]
        return carry

    lax.fori_loop(0, NX * NZ, step, 0)
    value = dot_nn(left[pl.ds(block_start(c, half), half), :], back[...]).astype(BF)
    sent[...] = value


def rest_kernel(rot_home, outer, basis, norm, out):
    for xp in range(NX):
        out[xp, :B] = rot_home[xp]
        out[xp, B : 3 * B] = outer[xp]
        out[xp, 3 * B : 5 * B] = basis[xp]
        out[xp, 5 * B :] = norm[...]


def relay_kernel(where, u0, u1, u2, u3, h0, h1, h2, h3, own_slot, sent):
    c = where[2]
    half = own_slot.shape[0]
    nb = NX * B
    for out, hit, tile in ((own_slot, where[4], where[5]), (sent, where[6], where[7])):
        place = shift_of(where, tile)

        @pl.when(hit == 0)
        def _():
            out[:half] = jnp.zeros((half, W), BF)

        for s, ref in enumerate((u0, u1, u2, u3)):

            @pl.when((hit > 0) & (place == s))
            def _():
                out[:half] = ref[...]

    row = pl.multiple_of((1 - c) * B, B)
    for s, ref in enumerate((h0, h1, h2, h3)):
        sent[half + s * B : half + (s + 1) * B] = ref[pl.ds(B + row, B)]
        sent[half + nb + s * B : half + nb + (s + 1) * B] = ref[pl.ds(3 * B + row, B)]
        sent[half + 2 * nb + s * PAD : half + 2 * nb + (s + 1) * PAD] = ref[5 * B :]


def final_kernel(
    where,
    h0,
    h1,
    h2,
    h3,
    own_slot,
    recv,
    m1,
    m2,
    sl,
    sr,
    o1,
    o2,
    osl,
    osr,
    obl,
    obr,
    slot,
    norm,
):
    c = where[2]
    half = own_slot.shape[0]
    nb = NX * B
    slot[0, pl.ds(block_start(c, half), half)] = own_slot[...]
    slot[0, pl.ds(block_start(1 - c, half), half)] = recv[:half]
    row = pl.multiple_of(c * B, B)
    for s, ref in enumerate((h0, h1, h2, h3)):
        t = shift_of(where, s)
        other = recv[half + 2 * nb + s * PAD : half + 2 * nb + (s + 1) * PAD].astype(F32)
        value = (ref[5 * B :].astype(F32) + other)[0:2]
        norm[t] = jnp.where(where[8] > 0, value, 0.0)
        rot = ref[:B].astype(F32)
        o1[t] = 0.9 * m1[t] + 0.1 * rot
        o2[t] = 0.95 * m2[t] + 0.05 * rot * rot
        outer_own = ref[pl.ds(B + row, B)].astype(F32)
        outer_oth = recv[half + s * B : half + (s + 1) * B].astype(F32)
        basis_own = ref[pl.ds(3 * B + row, B)].astype(F32)
        basis_oth = recv[half + nb + s * B : half + nb + (s + 1) * B].astype(F32)
        osl[t] = 0.95 * sl[t] + 0.05 * jnp.where(c == 0, outer_own, outer_oth)
        osr[t] = 0.95 * sr[t] + 0.05 * jnp.where(c == 0, outer_oth, outer_own)
        obl[t] = jnp.where(c == 0, basis_own, basis_oth)
        obr[t] = jnp.where(c == 0, basis_oth, basis_own)


def shards(
    features,
    out_grads,
    norm_grads,
    owners,
    moment1,
    moment2,
    left_stats,
    right_stats,
    left_basis,
    right_basis,
    norm_m,
    norm_v,
):
    xi = lax.axis_index("x")
    zi = lax.axis_index("z")
    ci = lax.axis_index("c")
    mi = lax.axis_index("mp")
    mine_dp = (xi * NZ + zi) * NC + ci
    other_dp = (xi * NZ + zi) * NC + (1 - ci)
    left_core = ci == 0
    half = features.shape[1] // 2
    full = 2 * half
    tile_owner = owners[:NX]

    def owned(index):
        hit = tile_owner == index
        which = jnp.sum(jnp.where(hit, jnp.arange(NX, dtype=jnp.int32), 0))
        return [jnp.any(hit).astype(jnp.int32), which]

    where = jnp.stack([xi, zi, ci, mi, *owned(mine_dp), *owned(other_dp), mine_dp == owners[NX]])
    where = where.astype(jnp.int32)

    with jax.named_scope("state_rows"):
        home = pl.pallas_call(
            pack_kernel,
            out_shape=[jax.ShapeDtypeStruct((6, B, W), BF)] * NX,
            in_specs=[pl.BlockSpec(memory_space=pl.ANY)] * 6,
            out_specs=[VMEM] * NX,
            scratch_shapes=[pltpu.VMEM((6, NX, B, W), F32), pltpu.SemaphoreType.DMA((6,))],
            name="pack",
        )(left_basis, right_basis, moment1, moment2, left_stats, right_stats)
        rows = [home[0]] + [
            lax.ppermute(home[s], "x", [(i, (i + s) % NX) for i in range(NX)]) for s in (1, 2, 3)
        ]
    with jax.named_scope("grad_sum"):
        feat_other = lax.dynamic_slice_in_dim(features, (1 - ci) * half, half, 1)
        feat_mine = lax.dynamic_slice_in_dim(features, ci * half, half, 1)
        norm = jnp.pad(norm_grads.reshape(NX, 2, W), ((0, 0), (0, PAD - 2), (0, 0)))

        def partial(feat):
            return jnp.einsum("ti,tnc->nic", feat, out_grads, preferred_element_type=F32)

        sent = jnp.concatenate([partial(feat_other).astype(BF), norm.astype(BF)], axis=1)
        *rows, sent = lax.optimization_barrier((*rows, sent))
        got = swap_cores(sent)
        acc = jnp.concatenate([partial(feat_mine), norm], axis=1) + got.astype(F32)
        acc = acc.astype(BF)
        bases, moments, keep, send = small(spread_kernel, "spread", (8, 8, 4, 4), *rows, acc)
        turned = [turn(bases, s) for s in (1, 2, 3)]
        pack = join(bases, *turned, moments)
        pack = lax.all_gather(pack, "z", axis=0)
        tile = lambda s: lax.dynamic_index_in_dim(acc, lax.rem(xi + s, NX), 0, keepdims=False)
        acc = [tile(0)] + [
            lax.ppermute(tile(s), "x", [(i, (i + s) % NX) for i in range(NX)]) for s in (2, 1, 3)
        ]

    with jax.named_scope("grad_sum"):
        acc = pl.pallas_call(
            sum_kernel,
            out_shape=jax.ShapeDtypeStruct((NZ, half // NZ + PAD, W), BF),
            in_specs=[VMEM] * NX,
            out_specs=VMEM,
            cost_estimate=pl.CostEstimate(
                flops=10**6, bytes_accessed=300000000, transcendentals=0
            ),
            name="sum_x",
        )(*acc)
        stats, near, far = small(choose_kernel, "choose", (8, 4, 4), keep, swap_cores(send), acc)
        stats = join(stats, turn(far, 1), turn(near, 3), turn(near, 2))
        acc = exchange(acc, "z")
        acc, stats = lax.optimization_barrier((acc, stats))
        stats = lax.all_gather(stats, "z", axis=0)
        acc = jnp.sum(acc.astype(F32), axis=0)
        grad_rows = acc[: half // NZ].astype(BF)
        norm_total = lax.dynamic_slice(
            acc[half // NZ : half // NZ + 2].reshape(-1), ((zi * NC + ci) * 32,), (32,)
        )

    new_nm = 0.9 * norm_m + 0.1 * norm_total
    new_nv = 0.95 * norm_v + 0.05 * norm_total * norm_total
    norm_step = new_nm / FIX_ONE / (jnp.sqrt(new_nv / FIX_TWO) + 1e-08)

    with jax.named_scope("grad_all"):
        norm_row = jnp.pad(norm_step.astype(BF)[None], ((0, PAD - 1), (0, W - 32)))
        grad_z = everyone(jnp.concatenate([grad_rows, norm_row], axis=0), "z", NZ)
        norm_zs = grad_z[:, half // NZ, None, :32]
        norm_zs = jnp.where(jnp.arange(NC)[None, :, None] == ci, norm_zs, 0).reshape(2, W)
        grad_half = grad_z[:, : half // NZ].reshape(half, W)
        grad_own = all_turns(grad_half, turn)
        pack, norm_zs = lax.optimization_barrier((pack, norm_zs))
        pack_other = swap_cores(pack)
        left, right = call(
            prep_kernel,
            "prep",
            [((full, full), BF)] * 2,
            [],
            where,
            pack,
            pack_other,
        )
        grad_own[2], left, right = lax.optimization_barrier((grad_own[2], left, right))
        grad_other = [swap_cores(piece) for piece in grad_own]

    with jax.named_scope("rotate"):
        grad, work, direction, rot_home = call(
            rotate_kernel,
            "rotate",
            [
                ((full, full), BF),
                ((full, full), BF),
                ((half, W), BF),
                ((NX, B, W), BF),
            ],
            [((full, W), F32)],
            where,
            *grad_own,
            *grad_other,
            left,
            right,
            pack,
        )
        stats, rot_home = lax.optimization_barrier((stats, rot_home))
        direction = all_turns(direction, turn)
    with jax.named_scope("power"):
        (power_old,) = call(
            old_power_kernel,
            "old_power",
            [((full, full), F32)],
            [((10, W, W), BF)],
            where,
            stats,
            left,
            right,
            cost=COST,
        )
        outer, basis = call(
            power_kernel,
            "power",
            [((NX, NC * B, W), BF)] * 2,
            [((full, full), F32), ((full, full), BF)],
            where,
            grad,
            work,
            power_old,
            cost=COST,
        )
        norm_pad = jnp.pad(norm_zs, ((0, PAD - 2), (0, 0)))
        rest = pl.pallas_call(
            rest_kernel,
            out_shape=jax.ShapeDtypeStruct((NX, 5 * B + PAD, W), BF),
            in_specs=[VMEM] * 4,
            out_specs=VMEM,
            name="rest",
        )(rot_home, outer, basis, norm_pad)
        tile = lambda s: lax.dynamic_index_in_dim(rest, lax.rem(xi + s, NX), 0, keepdims=False)
        direction[2], rest = lax.optimization_barrier((direction[2], rest))
        rest = [tile(0)] + [turn_x(tile(s), s) for s in (1, 2, 3)]
    with jax.named_scope("update"):
        (back,) = call(back_kernel, "back", [((half, W), BF)], [], where, *direction, right)
        back_other = swap_cores(back)
        (update,) = call(
            update_kernel,
            "update",
            [((half, W), BF)],
            [((full, W), BF)],
            where,
            back,
            back_other,
            left,
        )

    with jax.named_scope("home"):
        update, *rest = lax.optimization_barrier((update, *rest))
        update = all_turns(update, turn_x)
        nb = NX * B
        own_slot, sent = call(
            relay_kernel,
            "relay",
            [((half, W), BF), ((half + 2 * nb + NX * PAD, W), BF)],
            [],
            where,
            *update,
            *rest,
        )
        recv = swap_cores(sent)
        state = ((NX, B, W), F32)
        outs = call(
            final_kernel,
            "final",
            [state] * 6 + [((1, full, W), BF), ((NX, 2, W), F32)],
            [],
            where,
            *rest,
            own_slot,
            recv,
            moment1,
            moment2,
            left_stats,
            right_stats,
        )
    *outs, norm_slot = outs
    return (*outs, new_nm, new_nv, norm_slot.reshape(1, -1))


def solution(mesh):
    mesh = Mesh(mesh.devices.reshape(NX, NZ, NC, NM), ("x", "z", "c", "mp"))
    dp = ("x", "z", "c")
    state = P(None, dp, "mp")
    in_specs = (
        P(dp, None),
        P(dp, None, "mp"),
        P(dp, None),
        P(),
        state,
        state,
        state,
        state,
        state,
        state,
        P(dp),
        P(dp),
    )
    out_specs = (
        state,
        state,
        state,
        state,
        state,
        state,
        P(dp, None, "mp"),
        P(dp),
        P(dp),
        P(dp, None),
    )
    return jax.shard_map(shards, mesh=mesh, in_specs=in_specs, out_specs=out_specs, check_vma=False)
```

```python
import jax
import jax.numpy as jnp
from jax import lax
from jax.experimental import pallas as pl
from jax.experimental.pallas import tpu as pltpu
from jax.sharding import Mesh, PartitionSpec as P

FIX_ONE = 1.0 - 0.9**10
FIX_TWO = 1.0 - 0.95**10
F32 = jnp.float32
BF = jnp.bfloat16
NX, NZ, NC, NM = 4, 8, 2, 4
B = 16
W = 256
PAD = 16


def contract(left, right, left_dim, right_dim):
    return lax.dot_general(
        left, right, (((left_dim,), (right_dim,)), ((), ())), preferred_element_type=F32
    )


def swap_cores(value):
    return lax.ppermute(value, "c", [(0, 1), (1, 0)])


def exchange(value, axis):
    return lax.all_to_all(value, axis, 0, 0, tiled=True)


def turn(value, s):
    return lax.ppermute(value, "mp", [(i, (i + s) % NM) for i in range(NM)])


def turn_x(value, s):
    return lax.ppermute(value, "x", [(i, (i + s) % NX) for i in range(NX)])


def all_turns(value, turn_by):
    far = turn_by(value, 2)
    return [value, turn_by(value, 1), far, turn_by(value, 3)]


def everyone(value, axis, count):
    return exchange(jnp.broadcast_to(value[None], (count, *value.shape)), axis)


def ordered(core, mine, other):
    return jnp.where(core == 0, jnp.stack([mine, other]), jnp.stack([other, mine]))


VMEM = pl.BlockSpec(memory_space=pltpu.VMEM)
SMEM = pl.BlockSpec(memory_space=pltpu.SMEM)


COST = pl.CostEstimate(flops=6 * 10**9, bytes_accessed=24 * 10**6, transcendentals=0)


def dot_nn(a, b):
    return contract(a, b, 1, 0)


def dot_nt(a, b):
    return contract(a, b, 1, 1)


def dot_tn(a, b):
    return contract(a, b, 0, 0)


def call(kernel, name, outs, scratch, *args, cost=None):
    n_scalar = 1
    return pl.pallas_call(
        kernel,
        out_shape=[jax.ShapeDtypeStruct(s, d) for s, d in outs],
        in_specs=[SMEM] * n_scalar + [VMEM] * (len(args) - n_scalar),
        out_specs=[VMEM] * len(outs),
        scratch_shapes=[pltpu.VMEM(s, d) for s, d in scratch],
        compiler_params=pltpu.CompilerParams(vmem_limit_bytes=16 * 1024 * 1024),
        cost_estimate=cost,
        name=name,
    )(*args)


def pack_kernel(*refs):
    states, outs, (held, sems) = refs[:6], refs[6:10], refs[10:]
    x, c = lax.axis_index("x"), lax.axis_index("c")
    copies = [pltpu.make_async_copy(ref, held.at[k], sems.at[k]) for k, ref in enumerate(states)]
    for copy in copies:
        copy.start()
    for copy in copies:
        copy.wait()
    for shift, out in enumerate(outs):
        tile = lax.rem(x + shift, NX)
        for k in range(4):
            out[k] = held[k, tile].astype(BF)
        lefts, rights = held[4, tile], held[5, tile]
        out[4] = jnp.where(c == 0, lefts, rights).astype(BF)
        out[5] = jnp.where(c == 0, rights, lefts).astype(BF)


def join_kernel(*refs):
    *parts, out = refs
    start = 0
    for part in parts:
        out[start : start + part.shape[0]] = part[...]
        start += part.shape[0]


def join(*parts):
    shape = (sum(p.shape[0] for p in parts), *parts[0].shape[1:])
    return pl.pallas_call(
        join_kernel,
        out_shape=jax.ShapeDtypeStruct(shape, parts[0].dtype),
        in_specs=[VMEM] * len(parts),
        out_specs=VMEM,
        name="join",
    )(*parts)


def sum_kernel(a0, a1, a2, a3, out):
    size = out.shape[1] - PAD
    half = size * NZ

    def added(rows):
        total = a0[rows].astype(F32)
        for ref in (a1, a2, a3):
            total += ref[rows].astype(F32)
        return total.astype(BF)

    norm = added(slice(half, half + PAD))
    for z in range(NZ):
        out[z, :size] = added(slice(z * size, (z + 1) * size))
        out[z, size:] = norm


def spread_kernel(r0, r1, r2, r3, trigger, bases, moments, keep, send):
    for s, ref in enumerate((r0, r1, r2, r3)):
        for k in range(2):
            bases[NX * k + s] = ref[k]
            moments[NX * k + s] = ref[2 + k]
        keep[s] = ref[4]
        send[s] = ref[5]


def choose_kernel(keep, other, trigger, stats, near, far):
    x, m = lax.axis_index("x"), lax.axis_index("mp")
    stats[:NX] = keep[...]
    stats[NX:] = other[...]
    for out, steps in ((near, (0, 1)), (far, (0, 2))):
        for j, step in enumerate(steps):
            shift = lax.rem(x - lax.rem(m + step, NM) + NX, NX)
            out[j] = keep[shift]
            out[2 + j] = other[shift]


def small(kernel, name, counts, *args):
    return pl.pallas_call(
        kernel,
        out_shape=[jax.ShapeDtypeStruct((n, B, W), BF) for n in counts],
        in_specs=[VMEM] * (len(args) - 1) + [pl.BlockSpec(memory_space=pl.ANY)],
        out_specs=[VMEM] * len(counts),
        name=name,
    )(*args)


def block_start(index, size):
    return pl.multiple_of(index * size, size)


def shift_of(where, xp):
    return lax.rem(where[0] - xp + NX, NX)


def prep_kernel(where, own, oth, left, right):
    c, m = where[2], where[3]
    for shift in range(NX):
        start = shift_of(where, shift) * (NZ * NC * B)
        for t in range(NM):
            col = block_start(lax.rem(m - t + NM, NM), W)
            for z in range(NZ):
                for ref, core in ((own, c), (oth, 1 - c)):
                    row = pl.multiple_of(start + z * (NC * B) + core * B, B)
                    left[pl.ds(row, B), pl.ds(col, W)] = ref[z, 2 * NX * t + shift]
                    right[pl.ds(row, B), pl.ds(col, W)] = ref[z, 2 * NX * t + NX + shift]


def old_power_kernel(where, pack, left, right, out, block):
    c, m = where[2], where[3]

    def fill(n, piece):
        for z in range(NZ):
            for k, core in ((0, c), (1, 1 - c)):
                row = pl.multiple_of(z * (NC * B) + core * B, B)
                block[n, pl.ds(row, B), :] = piece(z, k)

    for u in range(NM):
        shift = shift_of(where, lax.rem(m + u, NM))
        fill(u, lambda z, k: pack[z, NX * k + shift])
    for n in range(3):
        for j in range(2):
            fill(4 + 2 * n + j, lambda z, k: pack[z, 8 + 4 * n + 2 * k + j])
    table = (
        ((0, 0), (1, 1), (2, 1), (3, 1)),
        ((1, 0), (6, 0), (7, 1), (5, 0)),
        ((2, 0), (7, 0), (8, 0), (9, 1)),
        ((3, 0), (5, 1), (9, 0), (4, 0)),
    )

    def product(basis):
        for u in range(NM):
            total = None
            for v in range(NM):
                rows = basis[pl.ds(block_start(lax.rem(m + v, NM), W), W), :]
                place, turned = table[u][v]
                part = (dot_tn if turned else dot_nn)(block[place], rows)
                total = part if total is None else total + part
            out[pl.ds(block_start(lax.rem(m + u, NM), W), W), :] = total

    @pl.when(c == 0)
    def _():
        product(left)

    @pl.when(c == 1)
    def _():
        product(right)


def rotate_kernel(where, *refs):
    own, oth = refs[:NM], refs[NM : 2 * NM]
    left, right, pack, grad, work, direct, rot_home, rot = refs[2 * NM :]
    z, c, m = where[1], where[2], where[3]
    half = own[0].shape[0]
    for pieces, core in ((own, c), (oth, 1 - c)):
        r = pl.ds(block_start(core, half), half)
        for s in range(NM):
            grad[r, pl.ds(block_start(lax.rem(m - s + NM, NM), W), W)] = pieces[s][...]
    col = pl.ds(block_start(m, W), W)

    @pl.when(c == 0)
    def _():
        work[...] = dot_tn(left[...], grad[...]).astype(BF)
        rot[...] = dot_nn(work[...], right[:, col])

    @pl.when(c == 1)
    def _():
        work[...] = dot_nn(grad[...], right[...]).astype(BF)
        rot[...] = dot_tn(left[...], work[:, col])

    for xp in range(NX):
        shift = shift_of(where, xp)
        for zp in range(NZ):
            k = xp * NZ + zp
            value = rot[pl.ds(pl.multiple_of(k * (NC * B) + c * B, B), B), :]
            one = 0.9 * pack[zp, 8 * NX + shift].astype(F32) + 0.1 * value
            two = 0.95 * pack[zp, 9 * NX + shift].astype(F32) + 0.05 * value * value
            value = (one / FIX_ONE / (jnp.sqrt(two / FIX_TWO) + 1e-08)).astype(BF)
            for copy in range(NM):
                direct[copy, k * B : (k + 1) * B, :] = value
    for xp in range(NX):
        row = pl.multiple_of(xp * (NZ * NC * B) + z * (NC * B) + c * B, B)
        rot_home[xp] = rot[pl.ds(row, B), :].astype(BF)


def power_kernel(where, grad, work, old, outer, basis, power, iterate):
    z, c, m = where[1], where[2], where[3]
    col = pl.ds(block_start(m, W), W)
    total = NM * W

    def z_rows(xp):
        return pl.ds(pl.multiple_of(xp * (NZ * NC * B) + z * (NC * B), NC * B), NC * B)

    @pl.when(c == 0)
    def _():
        def rows(i, sums):
            r = pl.ds(block_start(i, W), W)
            value = 0.95 * old[r, :] + 0.05 * dot_nt(grad[r, :], work[...])
            power[r, :] = value
            return sums + jnp.sum(value * value, axis=0, keepdims=True)

        sums = lax.fori_loop(0, NM, rows, jnp.zeros((1, total), F32))
        scale = lax.rsqrt(sums + 1e-06)
        for i in range(NM):
            r = slice(i * W, (i + 1) * W)
            iterate[r, :] = (power[r, :] * scale).astype(BF)
        for xp in range(NX):
            outer[xp] = dot_nt(grad[z_rows(xp), :], grad[col, :]).astype(BF)

    @pl.when(c == 1)
    def _():
        def rows(i, sums):
            r = pl.ds(block_start(i, W), W)
            value = 0.95 * old[r, :] + 0.05 * dot_tn(grad[:, r], work[...])
            power[r, :] = value
            return sums + jnp.sum(value * value, axis=0, keepdims=True)

        sums = lax.fori_loop(0, NM, rows, jnp.zeros((1, total), F32))
        scale = lax.rsqrt(sums + 1e-06)
        for i in range(NM):
            r = slice(i * W, (i + 1) * W)
            iterate[r, :] = (power[r, :] * scale).astype(BF)

        def gram_rows(i, carry):
            r = pl.ds(block_start(i, W), W)
            power[r, 0:W] = dot_tn(grad[:, r], grad[:, col])
            return carry

        lax.fori_loop(0, NM, gram_rows, 0)
        for xp in range(NX):
            outer[xp] = power[z_rows(xp), 0:W].astype(BF)

    gram = dot_tn(iterate[:, col], iterate[...]).astype(BF)
    for xp in range(NX):
        here = iterate[z_rows(xp), :]
        value = 1.5 * iterate[z_rows(xp), col].astype(F32) - 0.5 * dot_nt(here, gram)
        basis[xp] = value.astype(BF)


def back_kernel(where, direct, right, back):
    m = where[3]
    rows = pl.ds(block_start(m, W), W)
    total = dot_nt(direct[0], right[rows, 0:W])
    for k in range(1, NM):
        total += dot_nt(direct[k], right[rows, k * W : (k + 1) * W])
    back[...] = total.astype(BF)


def update_kernel(
    where, own, oth, left, rot_home, outer, basis, norm, s0, s1, s2, s3, back
):
    c = where[2]
    half = own.shape[0]

    def step(k, carry):
        src = pl.ds(block_start(k, B), B)
        for ref, core in ((own, c), (oth, 1 - c)):
            back[pl.ds(pl.multiple_of(k * (NC * B) + core * B, B), B), :] = ref[src, :]
        return carry

    lax.fori_loop(0, NX * NZ, step, 0)
    value = dot_nn(left[pl.ds(block_start(c, half), half), :], back[...]).astype(BF)
    for s, out in enumerate((s0, s1, s2, s3)):
        xp = lax.rem(where[0] + s, NX)
        out[:half] = value
        out[half : half + B] = rot_home[xp]
        out[half + B : half + 3 * B] = outer[xp]
        out[half + 3 * B : half + 5 * B] = basis[xp]
        out[half + 5 * B :] = norm[...]


def relay_kernel(where, g0, g1, g2, g3, own_slot, sent):
    c = where[2]
    half = own_slot.shape[0]
    nb = NX * B
    for out, hit, tile in ((own_slot, where[4], where[5]), (sent, where[6], where[7])):
        place = shift_of(where, tile)

        @pl.when(hit == 0)
        def _():
            out[:half] = jnp.zeros((half, W), BF)

        for s, ref in enumerate((g0, g1, g2, g3)):

            @pl.when((hit > 0) & (place == s))
            def _():
                out[:half] = ref[:half]

    row = pl.multiple_of((1 - c) * B, B)
    for s, ref in enumerate((g0, g1, g2, g3)):
        outer = ref[pl.ds(half + B + row, B)]
        basis = ref[pl.ds(half + 3 * B + row, B)]
        sent[half + s * B : half + (s + 1) * B] = outer
        sent[half + nb + s * B : half + nb + (s + 1) * B] = basis
        sent[half + 2 * nb + s * PAD : half + 2 * nb + (s + 1) * PAD] = ref[half + 5 * B :]


def final_kernel(
    where,
    g0,
    g1,
    g2,
    g3,
    own_slot,
    recv,
    m1,
    m2,
    sl,
    sr,
    o1,
    o2,
    osl,
    osr,
    obl,
    obr,
    slot,
    norm,
):
    c = where[2]
    half = own_slot.shape[0]
    nb = NX * B
    slot[0, pl.ds(block_start(c, half), half)] = own_slot[...]
    slot[0, pl.ds(block_start(1 - c, half), half)] = recv[:half]
    row = pl.multiple_of(c * B, B)
    for s, ref in enumerate((g0, g1, g2, g3)):
        t = shift_of(where, s)
        other = recv[half + 2 * nb + s * PAD : half + 2 * nb + (s + 1) * PAD].astype(F32)
        value = (ref[half + 5 * B :].astype(F32) + other)[0:2]
        norm[t] = jnp.where(where[8] > 0, value, 0.0)
        rot = ref[half : half + B].astype(F32)
        o1[t] = 0.9 * m1[t] + 0.1 * rot
        o2[t] = 0.95 * m2[t] + 0.05 * rot * rot
        outer_own = ref[pl.ds(half + B + row, B)].astype(F32)
        outer_oth = recv[half + s * B : half + (s + 1) * B].astype(F32)
        basis_own = ref[pl.ds(half + 3 * B + row, B)].astype(F32)
        basis_oth = recv[half + nb + s * B : half + nb + (s + 1) * B].astype(F32)
        osl[t] = 0.95 * sl[t] + 0.05 * jnp.where(c == 0, outer_own, outer_oth)
        osr[t] = 0.95 * sr[t] + 0.05 * jnp.where(c == 0, outer_oth, outer_own)
        obl[t] = jnp.where(c == 0, basis_own, basis_oth)
        obr[t] = jnp.where(c == 0, basis_oth, basis_own)


def shards(
    features,
    out_grads,
    norm_grads,
    owners,
    moment1,
    moment2,
    left_stats,
    right_stats,
    left_basis,
    right_basis,
    norm_m,
    norm_v,
):
    xi = lax.axis_index("x")
    zi = lax.axis_index("z")
    ci = lax.axis_index("c")
    mi = lax.axis_index("mp")
    mine_dp = (xi * NZ + zi) * NC + ci
    other_dp = (xi * NZ + zi) * NC + (1 - ci)
    left_core = ci == 0
    half = features.shape[1] // 2
    full = 2 * half
    tile_owner = owners[:NX]

    def owned(index):
        hit = tile_owner == index
        which = jnp.sum(jnp.where(hit, jnp.arange(NX, dtype=jnp.int32), 0))
        return [jnp.any(hit).astype(jnp.int32), which]

    where = jnp.stack([xi, zi, ci, mi, *owned(mine_dp), *owned(other_dp), mine_dp == owners[NX]])
    where = where.astype(jnp.int32)

    with jax.named_scope("state_rows"):
        home = pl.pallas_call(
            pack_kernel,
            out_shape=[jax.ShapeDtypeStruct((6, B, W), BF)] * NX,
            in_specs=[pl.BlockSpec(memory_space=pl.ANY)] * 6,
            out_specs=[VMEM] * NX,
            scratch_shapes=[pltpu.VMEM((6, NX, B, W), F32), pltpu.SemaphoreType.DMA((6,))],
            name="pack",
        )(left_basis, right_basis, moment1, moment2, left_stats, right_stats)
        rows = [home[0]] + [
            lax.ppermute(home[s], "x", [(i, (i + s) % NX) for i in range(NX)]) for s in (1, 2, 3)
        ]
    with jax.named_scope("grad_sum"):
        feat_other = lax.dynamic_slice_in_dim(features, (1 - ci) * half, half, 1)
        feat_mine = lax.dynamic_slice_in_dim(features, ci * half, half, 1)
        norm = jnp.pad(norm_grads.reshape(NX, 2, W), ((0, 0), (0, PAD - 2), (0, 0)))

        def partial(feat):
            return jnp.einsum("ti,tnc->nic", feat, out_grads, preferred_element_type=F32)

        sent = jnp.concatenate([partial(feat_other).astype(BF), norm.astype(BF)], axis=1)
        *rows, sent = lax.optimization_barrier((*rows, sent))
        got = swap_cores(sent)
        acc = jnp.concatenate([partial(feat_mine), norm], axis=1) + got.astype(F32)
        acc = acc.astype(BF)
        bases, moments, keep, send = small(spread_kernel, "spread", (8, 8, 4, 4), *rows, acc)
        turned = [turn(bases, s) for s in (1, 2, 3)]
        pack = join(bases, *turned, moments)
        pack = lax.all_gather(pack, "z", axis=0)
        tile = lambda s: lax.dynamic_index_in_dim(acc, lax.rem(xi + s, NX), 0, keepdims=False)
        acc = [tile(0)] + [
            lax.ppermute(tile(s), "x", [(i, (i + s) % NX) for i in range(NX)]) for s in (2, 1, 3)
        ]

    with jax.named_scope("grad_sum"):
        acc = pl.pallas_call(
            sum_kernel,
            out_shape=jax.ShapeDtypeStruct((NZ, half // NZ + PAD, W), BF),
            in_specs=[VMEM] * NX,
            out_specs=VMEM,
            cost_estimate=pl.CostEstimate(
                flops=10**6, bytes_accessed=300000000, transcendentals=0
            ),
            name="sum_x",
        )(*acc)
        stats, near, far = small(choose_kernel, "choose", (8, 4, 4), keep, swap_cores(send), acc)
        stats = join(stats, turn(far, 1), turn(near, 3), turn(near, 2))
        acc = exchange(acc, "z")
        acc, stats = lax.optimization_barrier((acc, stats))
        stats = lax.all_gather(stats, "z", axis=0)
        acc = jnp.sum(acc.astype(F32), axis=0)
        grad_rows = acc[: half // NZ].astype(BF)
        norm_total = lax.dynamic_slice(
            acc[half // NZ : half // NZ + 2].reshape(-1), ((zi * NC + ci) * 32,), (32,)
        )

    new_nm = 0.9 * norm_m + 0.1 * norm_total
    new_nv = 0.95 * norm_v + 0.05 * norm_total * norm_total
    norm_step = new_nm / FIX_ONE / (jnp.sqrt(new_nv / FIX_TWO) + 1e-08)

    with jax.named_scope("grad_all"):
        norm_row = jnp.pad(norm_step.astype(BF)[None], ((0, PAD - 1), (0, W - 32)))
        grad_z = everyone(jnp.concatenate([grad_rows, norm_row], axis=0), "z", NZ)
        norm_zs = grad_z[:, half // NZ, None, :32]
        norm_zs = jnp.where(jnp.arange(NC)[None, :, None] == ci, norm_zs, 0).reshape(2, W)
        grad_half = grad_z[:, : half // NZ].reshape(half, W)
        grad_own = all_turns(grad_half, turn)
        pack, norm_zs = lax.optimization_barrier((pack, norm_zs))
        pack_other = swap_cores(pack)
        left, right = call(
            prep_kernel,
            "prep",
            [((full, full), BF)] * 2,
            [],
            where,
            pack,
            pack_other,
        )
        grad_own[2], left, right = lax.optimization_barrier((grad_own[2], left, right))
        grad_other = [swap_cores(piece) for piece in grad_own]

    with jax.named_scope("rotate"):
        grad, work, direction, rot_home = call(
            rotate_kernel,
            "rotate",
            [
                ((full, full), BF),
                ((full, full), BF),
                ((NM, half, W), BF),
                ((NX, B, W), BF),
            ],
            [((full, W), F32)],
            where,
            *grad_own,
            *grad_other,
            left,
            right,
            pack,
        )
        stats, rot_home = lax.optimization_barrier((stats, rot_home))
        direction = exchange(direction, "mp")
    with jax.named_scope("power"):
        (power_old,) = call(
            old_power_kernel,
            "old_power",
            [((full, full), F32)],
            [((10, W, W), BF)],
            where,
            stats,
            left,
            right,
            cost=COST,
        )
        outer, basis = call(
            power_kernel,
            "power",
            [((NX, NC * B, W), BF)] * 2,
            [((full, full), F32), ((full, full), BF)],
            where,
            grad,
            work,
            power_old,
            cost=COST,
        )
        norm_pad = jnp.pad(norm_zs, ((0, PAD - 2), (0, 0)))
        direction, outer, basis = lax.optimization_barrier((direction, outer, basis))
    with jax.named_scope("update"):
        (back,) = call(back_kernel, "back", [((half, W), BF)], [], where, direction, right)
        back_other = swap_cores(back)
        update = call(
            update_kernel,
            "update",
            [((half + 5 * B + PAD, W), BF)] * NX,
            [((full, W), BF)],
            where,
            back,
            back_other,
            left,
            rot_home,
            outer,
            basis,
            norm_pad,
        )

    with jax.named_scope("home"):
        update = [update[0]] + [turn_x(update[s], s) for s in (1, 2, 3)]
        nb = NX * B
        own_slot, sent = call(
            relay_kernel,
            "relay",
            [((half, W), BF), ((half + 2 * nb + NX * PAD, W), BF)],
            [],
            where,
            *update,
        )
        recv = swap_cores(sent)
        state = ((NX, B, W), F32)
        outs = call(
            final_kernel,
            "final",
            [state] * 6 + [((1, full, W), BF), ((NX, 2, W), F32)],
            [],
            where,
            *update,
            own_slot,
            recv,
            moment1,
            moment2,
            left_stats,
            right_stats,
        )
    *outs, norm_slot = outs
    return (*outs, new_nm, new_nv, norm_slot.reshape(1, -1))


def solution(mesh):
    mesh = Mesh(mesh.devices.reshape(NX, NZ, NC, NM), ("x", "z", "c", "mp"))
    dp = ("x", "z", "c")
    state = P(None, dp, "mp")
    in_specs = (
        P(dp, None),
        P(dp, None, "mp"),
        P(dp, None),
        P(),
        state,
        state,
        state,
        state,
        state,
        state,
        P(dp),
        P(dp),
    )
    out_specs = (
        state,
        state,
        state,
        state,
        state,
        state,
        P(dp, None, "mp"),
        P(dp),
        P(dp),
        P(dp, None),
    )
    return jax.shard_map(shards, mesh=mesh, in_specs=in_specs, out_specs=out_specs, check_vma=False)
```

```python
import jax
import jax.numpy as jnp
from jax import lax
from jax.experimental import pallas as pl
from jax.experimental.pallas import tpu as pltpu
from jax.sharding import Mesh, PartitionSpec as P

FIX_ONE = 1.0 - 0.9**10
FIX_TWO = 1.0 - 0.95**10
F32 = jnp.float32
BF = jnp.bfloat16
NX, NZ, NC, NM = 4, 8, 2, 4
B = 16
W = 256
PAD = 16


def contract(left, right, left_dim, right_dim):
    return lax.dot_general(
        left, right, (((left_dim,), (right_dim,)), ((), ())), preferred_element_type=F32
    )


def swap_cores(value):
    return lax.ppermute(value, "c", [(0, 1), (1, 0)])


def exchange(value, axis):
    return lax.all_to_all(value, axis, 0, 0, tiled=True)


def turn(value, s):
    return lax.ppermute(value, "mp", [(i, (i + s) % NM) for i in range(NM)])


def turn_x(value, s):
    return lax.ppermute(value, "x", [(i, (i + s) % NX) for i in range(NX)])


def all_turns(value, turn_by):
    far = turn_by(value, 2)
    return [value, turn_by(value, 1), far, turn_by(value, 3)]


def everyone(value, axis, count):
    return exchange(jnp.broadcast_to(value[None], (count, *value.shape)), axis)


def ordered(core, mine, other):
    return jnp.where(core == 0, jnp.stack([mine, other]), jnp.stack([other, mine]))


VMEM = pl.BlockSpec(memory_space=pltpu.VMEM)
SMEM = pl.BlockSpec(memory_space=pltpu.SMEM)


COST = pl.CostEstimate(flops=6 * 10**9, bytes_accessed=24 * 10**6, transcendentals=0)


def dot_nn(a, b):
    return contract(a, b, 1, 0)


def dot_nt(a, b):
    return contract(a, b, 1, 1)


def dot_tn(a, b):
    return contract(a, b, 0, 0)


def call(kernel, name, outs, scratch, *args, cost=None):
    n_scalar = 1
    return pl.pallas_call(
        kernel,
        out_shape=[jax.ShapeDtypeStruct(s, d) for s, d in outs],
        in_specs=[SMEM] * n_scalar + [VMEM] * (len(args) - n_scalar),
        out_specs=[VMEM] * len(outs),
        scratch_shapes=[pltpu.VMEM(s, d) for s, d in scratch],
        compiler_params=pltpu.CompilerParams(vmem_limit_bytes=16 * 1024 * 1024),
        cost_estimate=cost,
        name=name,
    )(*args)


def pack_kernel(*refs):
    states, outs, (held, sems) = refs[:6], refs[6:10], refs[10:]
    x, c = lax.axis_index("x"), lax.axis_index("c")
    copies = [pltpu.make_async_copy(ref, held.at[k], sems.at[k]) for k, ref in enumerate(states)]
    for copy in copies:
        copy.start()
    for copy in copies:
        copy.wait()
    for shift, out in enumerate(outs):
        tile = lax.rem(x + shift, NX)
        for k in range(4):
            out[k] = held[k, tile].astype(BF)
        lefts, rights = held[4, tile], held[5, tile]
        out[4] = jnp.where(c == 0, lefts, rights).astype(BF)
        out[5] = jnp.where(c == 0, rights, lefts).astype(BF)


def join_kernel(*refs):
    *parts, out = refs
    start = 0
    for part in parts:
        out[start : start + part.shape[0]] = part[...]
        start += part.shape[0]


def join(*parts):
    shape = (sum(p.shape[0] for p in parts), *parts[0].shape[1:])
    return pl.pallas_call(
        join_kernel,
        out_shape=jax.ShapeDtypeStruct(shape, parts[0].dtype),
        in_specs=[VMEM] * len(parts),
        out_specs=VMEM,
        name="join",
    )(*parts)


def norm_kernel(row, out):
    out[...] = jnp.zeros(out.shape, F32)
    for k in range(2 * NX):
        out[k // 2, k % 2 : k % 2 + 1] = row[:, k * W : (k + 1) * W]


def sum_kernel(a0, a1, a2, a3, out):
    size = out.shape[1] - PAD
    half = size * NZ

    def added(rows):
        total = a0[rows].astype(F32)
        for ref in (a1, a2, a3):
            total += ref[rows].astype(F32)
        return total.astype(BF)

    norm = added(slice(half, half + PAD))
    for z in range(NZ):
        out[z, :size] = added(slice(z * size, (z + 1) * size))
        out[z, size:] = norm


def spread_kernel(r0, r1, r2, r3, trigger, bases, moments, keep, send):
    for s, ref in enumerate((r0, r1, r2, r3)):
        for k in range(2):
            bases[NX * k + s] = ref[k]
            moments[NX * k + s] = ref[2 + k]
        keep[s] = ref[4]
        send[s] = ref[5]


def choose_kernel(keep, other, trigger, stats, near, far):
    x, m = lax.axis_index("x"), lax.axis_index("mp")
    stats[:NX] = keep[...]
    stats[NX:] = other[...]
    for out, steps in ((near, (0, 1)), (far, (0, 2))):
        for j, step in enumerate(steps):
            shift = lax.rem(x - lax.rem(m + step, NM) + NX, NX)
            out[j] = keep[shift]
            out[2 + j] = other[shift]


def small(kernel, name, counts, *args):
    return pl.pallas_call(
        kernel,
        out_shape=[jax.ShapeDtypeStruct((n, B, W), BF) for n in counts],
        in_specs=[VMEM] * (len(args) - 1) + [pl.BlockSpec(memory_space=pl.ANY)],
        out_specs=[VMEM] * len(counts),
        name=name,
    )(*args)


def block_start(index, size):
    return pl.multiple_of(index * size, size)


def shift_of(where, xp):
    return lax.rem(where[0] - xp + NX, NX)


def prep_kernel(where, own, oth, left, right):
    c, m = where[2], where[3]
    for shift in range(NX):
        start = shift_of(where, shift) * (NZ * NC * B)
        for t in range(NM):
            col = block_start(lax.rem(m - t + NM, NM), W)
            for z in range(NZ):
                for ref, core in ((own, c), (oth, 1 - c)):
                    row = pl.multiple_of(start + z * (NC * B) + core * B, B)
                    left[pl.ds(row, B), pl.ds(col, W)] = ref[z, 2 * NX * t + shift]
                    right[pl.ds(row, B), pl.ds(col, W)] = ref[z, 2 * NX * t + NX + shift]


def old_power_kernel(where, pack, left, right, out, block):
    c, m = where[2], where[3]

    def fill(n, piece):
        for z in range(NZ):
            for k, core in ((0, c), (1, 1 - c)):
                row = pl.multiple_of(z * (NC * B) + core * B, B)
                block[n, pl.ds(row, B), :] = piece(z, k)

    for u in range(NM):
        shift = shift_of(where, lax.rem(m + u, NM))
        fill(u, lambda z, k: pack[z, NX * k + shift])
    for n in range(3):
        for j in range(2):
            fill(4 + 2 * n + j, lambda z, k: pack[z, 8 + 4 * n + 2 * k + j])
    table = (
        ((0, 0), (1, 1), (2, 1), (3, 1)),
        ((1, 0), (6, 0), (7, 1), (5, 0)),
        ((2, 0), (7, 0), (8, 0), (9, 1)),
        ((3, 0), (5, 1), (9, 0), (4, 0)),
    )

    def product(basis):
        for u in range(NM):
            total = None
            for v in range(NM):
                rows = basis[pl.ds(block_start(lax.rem(m + v, NM), W), W), :]
                place, turned = table[u][v]
                part = (dot_tn if turned else dot_nn)(block[place], rows)
                total = part if total is None else total + part
            out[pl.ds(block_start(lax.rem(m + u, NM), W), W), :] = total

    @pl.when(c == 0)
    def _():
        product(left)

    @pl.when(c == 1)
    def _():
        product(right)


def rotate_kernel(where, *refs):
    own, oth = refs[:NM], refs[NM : 2 * NM]
    left, right, pack, grad, work, direct, rot_home, rot = refs[2 * NM :]
    z, c, m = where[1], where[2], where[3]
    half = own[0].shape[0]
    for pieces, core in ((own, c), (oth, 1 - c)):
        r = pl.ds(block_start(core, half), half)
        for s in range(NM):
            grad[r, pl.ds(block_start(lax.rem(m - s + NM, NM), W), W)] = pieces[s][...]
    col = pl.ds(block_start(m, W), W)

    @pl.when(c == 0)
    def _():
        work[...] = dot_tn(left[...], grad[...]).astype(BF)
        rot[...] = dot_nn(work[...], right[:, col])

    @pl.when(c == 1)
    def _():
        work[...] = dot_nn(grad[...], right[...]).astype(BF)
        rot[...] = dot_tn(left[...], work[:, col])

    for xp in range(NX):
        shift = shift_of(where, xp)
        for zp in range(NZ):
            k = xp * NZ + zp
            value = rot[pl.ds(pl.multiple_of(k * (NC * B) + c * B, B), B), :]
            one = 0.9 * pack[zp, 8 * NX + shift].astype(F32) + 0.1 * value
            two = 0.95 * pack[zp, 9 * NX + shift].astype(F32) + 0.05 * value * value
            value = (one / FIX_ONE / (jnp.sqrt(two / FIX_TWO) + 1e-08)).astype(BF)
            for copy in range(NM):
                direct[copy, k * B : (k + 1) * B, :] = value
    for xp in range(NX):
        row = pl.multiple_of(xp * (NZ * NC * B) + z * (NC * B) + c * B, B)
        rot_home[xp] = rot[pl.ds(row, B), :].astype(BF)


def power_kernel(where, grad, work, old, outer, basis, power, iterate):
    z, c, m = where[1], where[2], where[3]
    col = pl.ds(block_start(m, W), W)
    total = NM * W

    def z_rows(xp):
        return pl.ds(pl.multiple_of(xp * (NZ * NC * B) + z * (NC * B), NC * B), NC * B)

    @pl.when(c == 0)
    def _():
        def rows(i, sums):
            r = pl.ds(block_start(i, W), W)
            value = 0.95 * old[r, :] + 0.05 * dot_nt(grad[r, :], work[...])
            power[r, :] = value
            return sums + jnp.sum(value * value, axis=0, keepdims=True)

        sums = lax.fori_loop(0, NM, rows, jnp.zeros((1, total), F32))
        scale = lax.rsqrt(sums + 1e-06)
        for i in range(NM):
            r = slice(i * W, (i + 1) * W)
            iterate[r, :] = (power[r, :] * scale).astype(BF)
        for xp in range(NX):
            outer[xp] = dot_nt(grad[z_rows(xp), :], grad[col, :]).astype(BF)

    @pl.when(c == 1)
    def _():
        def rows(i, sums):
            r = pl.ds(block_start(i, W), W)
            value = 0.95 * old[r, :] + 0.05 * dot_tn(grad[:, r], work[...])
            power[r, :] = value
            return sums + jnp.sum(value * value, axis=0, keepdims=True)

        sums = lax.fori_loop(0, NM, rows, jnp.zeros((1, total), F32))
        scale = lax.rsqrt(sums + 1e-06)
        for i in range(NM):
            r = slice(i * W, (i + 1) * W)
            iterate[r, :] = (power[r, :] * scale).astype(BF)

        def gram_rows(i, carry):
            r = pl.ds(block_start(i, W), W)
            power[r, 0:W] = dot_tn(grad[:, r], grad[:, col])
            return carry

        lax.fori_loop(0, NM, gram_rows, 0)
        for xp in range(NX):
            outer[xp] = power[z_rows(xp), 0:W].astype(BF)

    gram = dot_tn(iterate[:, col], iterate[...]).astype(BF)
    for xp in range(NX):
        here = iterate[z_rows(xp), :]
        value = 1.5 * iterate[z_rows(xp), col].astype(F32) - 0.5 * dot_nt(here, gram)
        basis[xp] = value.astype(BF)


def back_kernel(where, direct, right, back):
    m = where[3]
    rows = pl.ds(block_start(m, W), W)
    total = dot_nt(direct[0], right[rows, 0:W])
    for k in range(1, NM):
        total += dot_nt(direct[k], right[rows, k * W : (k + 1) * W])
    back[...] = total.astype(BF)


def update_kernel(
    where, own, oth, left, rot_home, outer, basis, norm, s0, s1, s2, s3, back
):
    c = where[2]
    half = own.shape[0]

    def step(k, carry):
        src = pl.ds(block_start(k, B), B)
        for ref, core in ((own, c), (oth, 1 - c)):
            back[pl.ds(pl.multiple_of(k * (NC * B) + core * B, B), B), :] = ref[src, :]
        return carry

    lax.fori_loop(0, NX * NZ, step, 0)
    value = dot_nn(left[pl.ds(block_start(c, half), half), :], back[...]).astype(BF)
    for s, out in enumerate((s0, s1, s2, s3)):
        xp = lax.rem(where[0] + s, NX)
        out[:half] = value
        out[half : half + B] = rot_home[xp]
        out[half + B : half + 3 * B] = outer[xp]
        out[half + 3 * B : half + 5 * B] = basis[xp]
        out[half + 5 * B :] = norm[...]


def relay_kernel(where, g0, g1, g2, g3, own_slot, sent):
    c = where[2]
    half = own_slot.shape[0]
    nb = NX * B
    for out, hit, tile in ((own_slot, where[4], where[5]), (sent, where[6], where[7])):
        place = shift_of(where, tile)

        @pl.when(hit == 0)
        def _():
            out[:half] = jnp.zeros((half, W), BF)

        for s, ref in enumerate((g0, g1, g2, g3)):

            @pl.when((hit > 0) & (place == s))
            def _():
                out[:half] = ref[:half]

    row = pl.multiple_of((1 - c) * B, B)
    for s, ref in enumerate((g0, g1, g2, g3)):
        outer = ref[pl.ds(half + B + row, B)]
        basis = ref[pl.ds(half + 3 * B + row, B)]
        sent[half + s * B : half + (s + 1) * B] = outer
        sent[half + nb + s * B : half + nb + (s + 1) * B] = basis
        sent[half + 2 * nb + s * PAD : half + 2 * nb + (s + 1) * PAD] = ref[half + 5 * B :]


def final_kernel(
    where,
    g0,
    g1,
    g2,
    g3,
    own_slot,
    recv,
    m1,
    m2,
    sl,
    sr,
    o1,
    o2,
    osl,
    osr,
    obl,
    obr,
    slot,
    norm,
):
    c = where[2]
    half = own_slot.shape[0]
    nb = NX * B
    slot[0, pl.ds(block_start(c, half), half)] = own_slot[...]
    slot[0, pl.ds(block_start(1 - c, half), half)] = recv[:half]
    row = pl.multiple_of(c * B, B)
    for s, ref in enumerate((g0, g1, g2, g3)):
        t = shift_of(where, s)
        other = recv[half + 2 * nb + s * PAD : half + 2 * nb + (s + 1) * PAD].astype(F32)
        value = (ref[half + 5 * B :].astype(F32) + other)[0:2]
        norm[t] = jnp.where(where[8] > 0, value, 0.0)
        rot = ref[half : half + B].astype(F32)
        o1[t] = 0.9 * m1[t] + 0.1 * rot
        o2[t] = 0.95 * m2[t] + 0.05 * rot * rot
        outer_own = ref[pl.ds(half + B + row, B)].astype(F32)
        outer_oth = recv[half + s * B : half + (s + 1) * B].astype(F32)
        basis_own = ref[pl.ds(half + 3 * B + row, B)].astype(F32)
        basis_oth = recv[half + nb + s * B : half + nb + (s + 1) * B].astype(F32)
        osl[t] = 0.95 * sl[t] + 0.05 * jnp.where(c == 0, outer_own, outer_oth)
        osr[t] = 0.95 * sr[t] + 0.05 * jnp.where(c == 0, outer_oth, outer_own)
        obl[t] = jnp.where(c == 0, basis_own, basis_oth)
        obr[t] = jnp.where(c == 0, basis_oth, basis_own)


def shards(
    features,
    out_grads,
    norm_grads,
    owners,
    moment1,
    moment2,
    left_stats,
    right_stats,
    left_basis,
    right_basis,
    norm_m,
    norm_v,
):
    xi = lax.axis_index("x")
    zi = lax.axis_index("z")
    ci = lax.axis_index("c")
    mi = lax.axis_index("mp")
    mine_dp = (xi * NZ + zi) * NC + ci
    other_dp = (xi * NZ + zi) * NC + (1 - ci)
    left_core = ci == 0
    half = features.shape[1] // 2
    full = 2 * half
    tile_owner = owners[:NX]

    def owned(index):
        hit = tile_owner == index
        which = jnp.sum(jnp.where(hit, jnp.arange(NX, dtype=jnp.int32), 0))
        return [jnp.any(hit).astype(jnp.int32), which]

    where = jnp.stack([xi, zi, ci, mi, *owned(mine_dp), *owned(other_dp), mine_dp == owners[NX]])
    where = where.astype(jnp.int32)

    with jax.named_scope("state_rows"):
        home = pl.pallas_call(
            pack_kernel,
            out_shape=[jax.ShapeDtypeStruct((6, B, W), BF)] * NX,
            in_specs=[pl.BlockSpec(memory_space=pl.ANY)] * 6,
            out_specs=[VMEM] * NX,
            scratch_shapes=[pltpu.VMEM((6, NX, B, W), F32), pltpu.SemaphoreType.DMA((6,))],
            name="pack",
        )(left_basis, right_basis, moment1, moment2, left_stats, right_stats)
        rows = [home[0]] + [
            lax.ppermute(home[s], "x", [(i, (i + s) % NX) for i in range(NX)]) for s in (1, 2, 3)
        ]
    with jax.named_scope("grad_sum"):
        feat_other = lax.dynamic_slice_in_dim(features, (1 - ci) * half, half, 1)
        feat_mine = lax.dynamic_slice_in_dim(features, ci * half, half, 1)
        norm = pl.pallas_call(
            norm_kernel,
            out_shape=jax.ShapeDtypeStruct((NX, PAD, W), F32),
            in_specs=[VMEM],
            out_specs=VMEM,
            name="norm_rows",
        )(norm_grads)

        def partial(feat):
            return jnp.einsum("ti,tnc->nic", feat, out_grads, preferred_element_type=F32)

        sent = jnp.concatenate([partial(feat_other).astype(BF), norm.astype(BF)], axis=1)
        *rows, sent = lax.optimization_barrier((*rows, sent))
        got = swap_cores(sent)
        acc = jnp.concatenate([partial(feat_mine), norm], axis=1) + got.astype(F32)
        acc = acc.astype(BF)
        bases, moments, keep, send = small(spread_kernel, "spread", (8, 8, 4, 4), *rows, acc)
        turned = [turn(bases, s) for s in (1, 2, 3)]
        pack = join(bases, *turned, moments)
        pack = lax.all_gather(pack, "z", axis=0)
        tile = lambda s: lax.dynamic_index_in_dim(acc, lax.rem(xi + s, NX), 0, keepdims=False)
        acc = [tile(0)] + [
            lax.ppermute(tile(s), "x", [(i, (i + s) % NX) for i in range(NX)]) for s in (2, 1, 3)
        ]

    with jax.named_scope("grad_sum"):
        acc = pl.pallas_call(
            sum_kernel,
            out_shape=jax.ShapeDtypeStruct((NZ, half // NZ + PAD, W), BF),
            in_specs=[VMEM] * NX,
            out_specs=VMEM,
            cost_estimate=pl.CostEstimate(
                flops=10**6, bytes_accessed=300000000, transcendentals=0
            ),
            name="sum_x",
        )(*acc)
        stats, near, far = small(choose_kernel, "choose", (8, 4, 4), keep, swap_cores(send), acc)
        acc, where = lax.optimization_barrier((acc, where))
        stats = join(stats, turn(far, 1), turn(near, 3), turn(near, 2))
        acc = exchange(acc, "z")
        acc, stats = lax.optimization_barrier((acc, stats))
        stats = lax.all_gather(stats, "z", axis=0)
        acc = jnp.sum(acc.astype(F32), axis=0)
        grad_rows = acc[: half // NZ].astype(BF)
        norm_total = lax.dynamic_slice(
            acc[half // NZ : half // NZ + 2].reshape(-1), ((zi * NC + ci) * 32,), (32,)
        )

    new_nm = 0.9 * norm_m + 0.1 * norm_total
    new_nv = 0.95 * norm_v + 0.05 * norm_total * norm_total
    norm_step = new_nm / FIX_ONE / (jnp.sqrt(new_nv / FIX_TWO) + 1e-08)

    with jax.named_scope("grad_all"):
        norm_row = jnp.pad(norm_step.astype(BF)[None], ((0, PAD - 1), (0, W - 32)))
        grad_z = everyone(jnp.concatenate([grad_rows, norm_row], axis=0), "z", NZ)
        norm_zs = grad_z[:, half // NZ, None, :32]
        norm_zs = jnp.where(jnp.arange(NC)[None, :, None] == ci, norm_zs, 0).reshape(2, W)
        grad_half = grad_z[:, : half // NZ].reshape(half, W)
        grad_own = all_turns(grad_half, turn)
        pack, norm_zs = lax.optimization_barrier((pack, norm_zs))
        pack_other = swap_cores(pack)
        left, right = call(
            prep_kernel,
            "prep",
            [((full, full), BF)] * 2,
            [],
            where,
            pack,
            pack_other,
        )
        grad_own[2], left, right = lax.optimization_barrier((grad_own[2], left, right))
        grad_other = [swap_cores(piece) for piece in grad_own]

    with jax.named_scope("rotate"):
        grad, work, direction, rot_home = call(
            rotate_kernel,
            "rotate",
            [
                ((full, full), BF),
                ((full, full), BF),
                ((NM, half, W), BF),
                ((NX, B, W), BF),
            ],
            [((full, W), F32)],
            where,
            *grad_own,
            *grad_other,
            left,
            right,
            pack,
        )
        stats, rot_home = lax.optimization_barrier((stats, rot_home))
        direction = exchange(direction, "mp")
    with jax.named_scope("power"):
        (power_old,) = call(
            old_power_kernel,
            "old_power",
            [((full, full), F32)],
            [((10, W, W), BF)],
            where,
            stats,
            left,
            right,
            cost=COST,
        )
        outer, basis = call(
            power_kernel,
            "power",
            [((NX, NC * B, W), BF)] * 2,
            [((full, full), F32), ((full, full), BF)],
            where,
            grad,
            work,
            power_old,
            cost=COST,
        )
        norm_pad = jnp.pad(norm_zs, ((0, PAD - 2), (0, 0)))
        direction, outer, basis = lax.optimization_barrier((direction, outer, basis))
    with jax.named_scope("update"):
        (back,) = call(back_kernel, "back", [((half, W), BF)], [], where, direction, right)
        back_other = swap_cores(back)
        update = call(
            update_kernel,
            "update",
            [((half + 5 * B + PAD, W), BF)] * NX,
            [((full, W), BF)],
            where,
            back,
            back_other,
            left,
            rot_home,
            outer,
            basis,
            norm_pad,
        )

    with jax.named_scope("home"):
        update = [update[0]] + [turn_x(update[s], s) for s in (1, 2, 3)]
        nb = NX * B
        own_slot, sent = call(
            relay_kernel,
            "relay",
            [((half, W), BF), ((half + 2 * nb + NX * PAD, W), BF)],
            [],
            where,
            *update,
        )
        recv = swap_cores(sent)
        state = ((NX, B, W), F32)
        outs = call(
            final_kernel,
            "final",
            [state] * 6 + [((1, full, W), BF), ((NX, 2, W), F32)],
            [],
            where,
            *update,
            own_slot,
            recv,
            moment1,
            moment2,
            left_stats,
            right_stats,
        )
    *outs, norm_slot = outs
    return (*outs, new_nm, new_nv, norm_slot.reshape(1, -1))


def solution(mesh):
    mesh = Mesh(mesh.devices.reshape(NX, NZ, NC, NM), ("x", "z", "c", "mp"))
    dp = ("x", "z", "c")
    state = P(None, dp, "mp")
    in_specs = (
        P(dp, None),
        P(dp, None, "mp"),
        P(dp, None),
        P(),
        state,
        state,
        state,
        state,
        state,
        state,
        P(dp),
        P(dp),
    )
    out_specs = (
        state,
        state,
        state,
        state,
        state,
        state,
        P(dp, None, "mp"),
        P(dp),
        P(dp),
        P(dp, None),
    )
    return jax.shard_map(shards, mesh=mesh, in_specs=in_specs, out_specs=out_specs, check_vma=False)
```

```python
import jax
import jax.numpy as jnp
from jax import lax
from jax.experimental import pallas as pl
from jax.experimental.pallas import tpu as pltpu
from jax.sharding import Mesh, PartitionSpec as P

FIX_ONE = 1.0 - 0.9**10
FIX_TWO = 1.0 - 0.95**10
F32 = jnp.float32
BF = jnp.bfloat16
NX, NZ, NC, NM = 4, 8, 2, 4
B = 16
W = 256
PAD = 16


def contract(left, right, left_dim, right_dim):
    return lax.dot_general(
        left, right, (((left_dim,), (right_dim,)), ((), ())), preferred_element_type=F32
    )


def swap_cores(value):
    return lax.ppermute(value, "c", [(0, 1), (1, 0)])


def exchange(value, axis):
    return lax.all_to_all(value, axis, 0, 0, tiled=True)


def turn(value, s):
    return lax.ppermute(value, "mp", [(i, (i + s) % NM) for i in range(NM)])


def turn_x(value, s):
    return lax.ppermute(value, "x", [(i, (i + s) % NX) for i in range(NX)])


def all_turns(value, turn_by):
    far = turn_by(value, 2)
    return [value, turn_by(value, 1), far, turn_by(value, 3)]


def everyone(value, axis, count):
    return exchange(jnp.broadcast_to(value[None], (count, *value.shape)), axis)


def ordered(core, mine, other):
    return jnp.where(core == 0, jnp.stack([mine, other]), jnp.stack([other, mine]))


VMEM = pl.BlockSpec(memory_space=pltpu.VMEM)
SMEM = pl.BlockSpec(memory_space=pltpu.SMEM)


COST = pl.CostEstimate(flops=6 * 10**9, bytes_accessed=24 * 10**6, transcendentals=0)


def dot_nn(a, b):
    return contract(a, b, 1, 0)


def dot_nt(a, b):
    return contract(a, b, 1, 1)


def dot_tn(a, b):
    return contract(a, b, 0, 0)


def call(kernel, name, outs, scratch, *args, cost=None):
    n_scalar = 1
    return pl.pallas_call(
        kernel,
        out_shape=[jax.ShapeDtypeStruct(s, d) for s, d in outs],
        in_specs=[SMEM] * n_scalar + [VMEM] * (len(args) - n_scalar),
        out_specs=[VMEM] * len(outs),
        scratch_shapes=[pltpu.VMEM(s, d) for s, d in scratch],
        compiler_params=pltpu.CompilerParams(vmem_limit_bytes=16 * 1024 * 1024),
        cost_estimate=cost,
        name=name,
    )(*args)


def pack_kernel(*refs):
    states, outs, (held, sems) = refs[:6], refs[6:10], refs[10:]
    x, c = lax.axis_index("x"), lax.axis_index("c")
    copies = [pltpu.make_async_copy(ref, held.at[k], sems.at[k]) for k, ref in enumerate(states)]
    for copy in copies:
        copy.start()
    for copy in copies:
        copy.wait()
    for shift, out in enumerate(outs):
        tile = lax.rem(x + shift, NX)
        for k in range(4):
            out[k] = held[k, tile].astype(BF)
        lefts, rights = held[4, tile], held[5, tile]
        out[4] = jnp.where(c == 0, lefts, rights).astype(BF)
        out[5] = jnp.where(c == 0, rights, lefts).astype(BF)


def join_kernel(*refs):
    *parts, out = refs
    start = 0
    for part in parts:
        out[start : start + part.shape[0]] = part[...]
        start += part.shape[0]


def join(*parts):
    shape = (sum(p.shape[0] for p in parts), *parts[0].shape[1:])
    return pl.pallas_call(
        join_kernel,
        out_shape=jax.ShapeDtypeStruct(shape, parts[0].dtype),
        in_specs=[VMEM] * len(parts),
        out_specs=VMEM,
        name="join",
    )(*parts)


def sum_kernel(a0, a1, a2, a3, out):
    size = out.shape[1] - PAD
    half = size * NZ

    def added(rows):
        total = a0[rows].astype(F32)
        for ref in (a1, a2, a3):
            total += ref[rows].astype(F32)
        return total.astype(BF)

    norm = added(slice(half, half + PAD))
    for z in range(NZ):
        out[z, :size] = added(slice(z * size, (z + 1) * size))
        out[z, size:] = norm


def spread_kernel(r0, r1, r2, r3, trigger, bases, moments, keep, send):
    for s, ref in enumerate((r0, r1, r2, r3)):
        for k in range(2):
            bases[NX * k + s] = ref[k]
            moments[NX * k + s] = ref[2 + k]
        keep[s] = ref[4]
        send[s] = ref[5]


def choose_kernel(keep, other, trigger, stats, near, far):
    x, m = lax.axis_index("x"), lax.axis_index("mp")
    stats[:NX] = keep[...]
    stats[NX:] = other[...]
    for out, steps in ((near, (0, 1)), (far, (0, 2))):
        for j, step in enumerate(steps):
            shift = lax.rem(x - lax.rem(m + step, NM) + NX, NX)
            out[j] = keep[shift]
            out[2 + j] = other[shift]


def small(kernel, name, counts, *args):
    return pl.pallas_call(
        kernel,
        out_shape=[jax.ShapeDtypeStruct((n, B, W), BF) for n in counts],
        in_specs=[VMEM] * (len(args) - 1) + [pl.BlockSpec(memory_space=pl.ANY)],
        out_specs=[VMEM] * len(counts),
        name=name,
    )(*args)


def block_start(index, size):
    return pl.multiple_of(index * size, size)


def shift_of(where, xp):
    return lax.rem(where[0] - xp + NX, NX)


def prep_kernel(where, own, oth, left, right):
    c, m = where[2], where[3]
    for shift in range(NX):
        start = shift_of(where, shift) * (NZ * NC * B)
        for t in range(NM):
            col = block_start(lax.rem(m - t + NM, NM), W)
            for z in range(NZ):
                for ref, core in ((own, c), (oth, 1 - c)):
                    row = pl.multiple_of(start + z * (NC * B) + core * B, B)
                    left[pl.ds(row, B), pl.ds(col, W)] = ref[z, 2 * NX * t + shift]
                    right[pl.ds(row, B), pl.ds(col, W)] = ref[z, 2 * NX * t + NX + shift]


def old_power_kernel(where, pack, left, right, out, block):
    c, m = where[2], where[3]

    def fill(n, piece):
        for z in range(NZ):
            for k, core in ((0, c), (1, 1 - c)):
                row = pl.multiple_of(z * (NC * B) + core * B, B)
                block[n, pl.ds(row, B), :] = piece(z, k)

    for u in range(NM):
        shift = shift_of(where, lax.rem(m + u, NM))
        fill(u, lambda z, k: pack[z, NX * k + shift])
    for n in range(3):
        for j in range(2):
            fill(4 + 2 * n + j, lambda z, k: pack[z, 8 + 4 * n + 2 * k + j])
    table = (
        ((0, 0), (1, 1), (2, 1), (3, 1)),
        ((1, 0), (6, 0), (7, 1), (5, 0)),
        ((2, 0), (7, 0), (8, 0), (9, 1)),
        ((3, 0), (5, 1), (9, 0), (4, 0)),
    )

    def product(basis):
        for u in range(NM):
            total = None
            for v in range(NM):
                rows = basis[pl.ds(block_start(lax.rem(m + v, NM), W), W), :]
                place, turned = table[u][v]
                part = (dot_tn if turned else dot_nn)(block[place], rows)
                total = part if total is None else total + part
            out[pl.ds(block_start(lax.rem(m + u, NM), W), W), :] = total

    @pl.when(c == 0)
    def _():
        product(left)

    @pl.when(c == 1)
    def _():
        product(right)


def rotate_kernel(where, *refs):
    own, oth = refs[:NM], refs[NM : 2 * NM]
    left, right, pack, grad_out, work_out, direct, rot_home, rot, grad, work, sems = refs[2 * NM :]
    z, c, m = where[1], where[2], where[3]
    half = own[0].shape[0]
    for pieces, core in ((own, c), (oth, 1 - c)):
        r = pl.ds(block_start(core, half), half)
        for s in range(NM):
            grad[r, pl.ds(block_start(lax.rem(m - s + NM, NM), W), W)] = pieces[s][...]
    col = pl.ds(block_start(m, W), W)
    grad_copy = pltpu.make_async_copy(grad, grad_out, sems.at[0])
    work_copy = pltpu.make_async_copy(work, work_out, sems.at[1])
    grad_copy.start()

    @pl.when(c == 0)
    def _():
        work[...] = dot_tn(left[...], grad[...]).astype(BF)
        rot[...] = dot_nn(work[...], right[:, col])

    @pl.when(c == 1)
    def _():
        work[...] = dot_nn(grad[...], right[...]).astype(BF)
        rot[...] = dot_tn(left[...], work[:, col])

    work_copy.start()
    for xp in range(NX):
        shift = shift_of(where, xp)
        for zp in range(NZ):
            k = xp * NZ + zp
            value = rot[pl.ds(pl.multiple_of(k * (NC * B) + c * B, B), B), :]
            one = 0.9 * pack[zp, 8 * NX + shift].astype(F32) + 0.1 * value
            two = 0.95 * pack[zp, 9 * NX + shift].astype(F32) + 0.05 * value * value
            value = (one / FIX_ONE / (jnp.sqrt(two / FIX_TWO) + 1e-08)).astype(BF)
            for copy in range(NM):
                direct[copy, k * B : (k + 1) * B, :] = value
    for xp in range(NX):
        row = pl.multiple_of(xp * (NZ * NC * B) + z * (NC * B) + c * B, B)
        rot_home[xp] = rot[pl.ds(row, B), :].astype(BF)
    grad_copy.wait()
    work_copy.wait()


def power_kernel(where, grad, work, old, outer, basis, power, iterate):
    z, c, m = where[1], where[2], where[3]
    col = pl.ds(block_start(m, W), W)
    total = NM * W

    def z_rows(xp):
        return pl.ds(pl.multiple_of(xp * (NZ * NC * B) + z * (NC * B), NC * B), NC * B)

    @pl.when(c == 0)
    def _():
        def rows(i, sums):
            r = pl.ds(block_start(i, W), W)
            value = 0.95 * old[r, :] + 0.05 * dot_nt(grad[r, :], work[...])
            power[r, :] = value
            return sums + jnp.sum(value * value, axis=0, keepdims=True)

        sums = lax.fori_loop(0, NM, rows, jnp.zeros((1, total), F32))
        scale = lax.rsqrt(sums + 1e-06)
        for i in range(NM):
            r = slice(i * W, (i + 1) * W)
            iterate[r, :] = (power[r, :] * scale).astype(BF)
        for xp in range(NX):
            outer[xp] = dot_nt(grad[z_rows(xp), :], grad[col, :]).astype(BF)

    @pl.when(c == 1)
    def _():
        def rows(i, sums):
            r = pl.ds(block_start(i, W), W)
            value = 0.95 * old[r, :] + 0.05 * dot_tn(grad[:, r], work[...])
            power[r, :] = value
            return sums + jnp.sum(value * value, axis=0, keepdims=True)

        sums = lax.fori_loop(0, NM, rows, jnp.zeros((1, total), F32))
        scale = lax.rsqrt(sums + 1e-06)
        for i in range(NM):
            r = slice(i * W, (i + 1) * W)
            iterate[r, :] = (power[r, :] * scale).astype(BF)

        def gram_rows(i, carry):
            r = pl.ds(block_start(i, W), W)
            power[r, 0:W] = dot_tn(grad[:, r], grad[:, col])
            return carry

        lax.fori_loop(0, NM, gram_rows, 0)
        for xp in range(NX):
            outer[xp] = power[z_rows(xp), 0:W].astype(BF)

    gram = dot_tn(iterate[:, col], iterate[...]).astype(BF)
    for xp in range(NX):
        here = iterate[z_rows(xp), :]
        value = 1.5 * iterate[z_rows(xp), col].astype(F32) - 0.5 * dot_nt(here, gram)
        basis[xp] = value.astype(BF)


def back_kernel(where, direct, right, back):
    m = where[3]
    rows = pl.ds(block_start(m, W), W)
    total = dot_nt(direct[0], right[rows, 0:W])
    for k in range(1, NM):
        total += dot_nt(direct[k], right[rows, k * W : (k + 1) * W])
    back[...] = total.astype(BF)


def update_kernel(
    where, own, oth, left, rot_home, outer, basis, norm, s0, s1, s2, s3, back
):
    c = where[2]
    half = own.shape[0]

    def step(k, carry):
        src = pl.ds(block_start(k, B), B)
        for ref, core in ((own, c), (oth, 1 - c)):
            back[pl.ds(pl.multiple_of(k * (NC * B) + core * B, B), B), :] = ref[src, :]
        return carry

    lax.fori_loop(0, NX * NZ, step, 0)
    value = dot_nn(left[pl.ds(block_start(c, half), half), :], back[...]).astype(BF)
    for s, out in enumerate((s0, s1, s2, s3)):
        xp = lax.rem(where[0] + s, NX)
        out[:half] = value
        out[half : half + B] = rot_home[xp]
        out[half + B : half + 3 * B] = outer[xp]
        out[half + 3 * B : half + 5 * B] = basis[xp]
        out[half + 5 * B :] = norm[...]


def relay_kernel(where, g0, g1, g2, g3, own_slot, sent):
    c = where[2]
    half = own_slot.shape[0]
    nb = NX * B
    for out, hit, tile in ((own_slot, where[4], where[5]), (sent, where[6], where[7])):
        place = shift_of(where, tile)

        @pl.when(hit == 0)
        def _():
            out[:half] = jnp.zeros((half, W), BF)

        for s, ref in enumerate((g0, g1, g2, g3)):

            @pl.when((hit > 0) & (place == s))
            def _():
                out[:half] = ref[:half]

    row = pl.multiple_of((1 - c) * B, B)
    for s, ref in enumerate((g0, g1, g2, g3)):
        outer = ref[pl.ds(half + B + row, B)]
        basis = ref[pl.ds(half + 3 * B + row, B)]
        sent[half + s * B : half + (s + 1) * B] = outer
        sent[half + nb + s * B : half + nb + (s + 1) * B] = basis
        sent[half + 2 * nb + s * PAD : half + 2 * nb + (s + 1) * PAD] = ref[half + 5 * B :]


def final_kernel(
    where,
    g0,
    g1,
    g2,
    g3,
    own_slot,
    recv,
    m1,
    m2,
    sl,
    sr,
    o1,
    o2,
    osl,
    osr,
    obl,
    obr,
    slot,
    norm,
):
    c = where[2]
    half = own_slot.shape[0]
    nb = NX * B
    slot[0, pl.ds(block_start(c, half), half)] = own_slot[...]
    slot[0, pl.ds(block_start(1 - c, half), half)] = recv[:half]
    row = pl.multiple_of(c * B, B)
    for s, ref in enumerate((g0, g1, g2, g3)):
        t = shift_of(where, s)
        other = recv[half + 2 * nb + s * PAD : half + 2 * nb + (s + 1) * PAD].astype(F32)
        value = (ref[half + 5 * B :].astype(F32) + other)[0:2]
        norm[t] = jnp.where(where[8] > 0, value, 0.0)
        rot = ref[half : half + B].astype(F32)
        o1[t] = 0.9 * m1[t] + 0.1 * rot
        o2[t] = 0.95 * m2[t] + 0.05 * rot * rot
        outer_own = ref[pl.ds(half + B + row, B)].astype(F32)
        outer_oth = recv[half + s * B : half + (s + 1) * B].astype(F32)
        basis_own = ref[pl.ds(half + 3 * B + row, B)].astype(F32)
        basis_oth = recv[half + nb + s * B : half + nb + (s + 1) * B].astype(F32)
        osl[t] = 0.95 * sl[t] + 0.05 * jnp.where(c == 0, outer_own, outer_oth)
        osr[t] = 0.95 * sr[t] + 0.05 * jnp.where(c == 0, outer_oth, outer_own)
        obl[t] = jnp.where(c == 0, basis_own, basis_oth)
        obr[t] = jnp.where(c == 0, basis_oth, basis_own)


def shards(
    features,
    out_grads,
    norm_grads,
    owners,
    moment1,
    moment2,
    left_stats,
    right_stats,
    left_basis,
    right_basis,
    norm_m,
    norm_v,
):
    xi = lax.axis_index("x")
    zi = lax.axis_index("z")
    ci = lax.axis_index("c")
    mi = lax.axis_index("mp")
    mine_dp = (xi * NZ + zi) * NC + ci
    other_dp = (xi * NZ + zi) * NC + (1 - ci)
    left_core = ci == 0
    half = features.shape[1] // 2
    full = 2 * half
    tile_owner = owners[:NX]

    def owned(index):
        hit = tile_owner == index
        which = jnp.sum(jnp.where(hit, jnp.arange(NX, dtype=jnp.int32), 0))
        return [jnp.any(hit).astype(jnp.int32), which]

    where = jnp.stack([xi, zi, ci, mi, *owned(mine_dp), *owned(other_dp), mine_dp == owners[NX]])
    where = where.astype(jnp.int32)

    with jax.named_scope("state_rows"):
        home = pl.pallas_call(
            pack_kernel,
            out_shape=[jax.ShapeDtypeStruct((6, B, W), BF)] * NX,
            in_specs=[pl.BlockSpec(memory_space=pl.ANY)] * 6,
            out_specs=[VMEM] * NX,
            scratch_shapes=[pltpu.VMEM((6, NX, B, W), F32), pltpu.SemaphoreType.DMA((6,))],
            name="pack",
        )(left_basis, right_basis, moment1, moment2, left_stats, right_stats)
        rows = [home[0]] + [
            lax.ppermute(home[s], "x", [(i, (i + s) % NX) for i in range(NX)]) for s in (1, 2, 3)
        ]
    with jax.named_scope("grad_sum"):
        feat_other = lax.dynamic_slice_in_dim(features, (1 - ci) * half, half, 1)
        feat_mine = lax.dynamic_slice_in_dim(features, ci * half, half, 1)
        norm = jnp.pad(norm_grads.reshape(NX, 2, W), ((0, 0), (0, PAD - 2), (0, 0)))

        def partial(feat):
            return jnp.einsum("ti,tnc->nic", feat, out_grads, preferred_element_type=F32)

        sent = jnp.concatenate([partial(feat_other).astype(BF), norm.astype(BF)], axis=1)
        *rows, sent = lax.optimization_barrier((*rows, sent))
        got = swap_cores(sent)
        acc = jnp.concatenate([partial(feat_mine), norm], axis=1) + got.astype(F32)
        acc = acc.astype(BF)
        bases, moments, keep, send = small(spread_kernel, "spread", (8, 8, 4, 4), *rows, acc)
        turned = [turn(bases, s) for s in (1, 2, 3)]
        pack = join(bases, *turned, moments)
        pack = lax.all_gather(pack, "z", axis=0)
        tile = lambda s: lax.dynamic_index_in_dim(acc, lax.rem(xi + s, NX), 0, keepdims=False)
        acc = [tile(0)] + [
            lax.ppermute(tile(s), "x", [(i, (i + s) % NX) for i in range(NX)]) for s in (2, 1, 3)
        ]

    with jax.named_scope("grad_sum"):
        acc = pl.pallas_call(
            sum_kernel,
            out_shape=jax.ShapeDtypeStruct((NZ, half // NZ + PAD, W), BF),
            in_specs=[VMEM] * NX,
            out_specs=VMEM,
            cost_estimate=pl.CostEstimate(
                flops=10**6, bytes_accessed=300000000, transcendentals=0
            ),
            name="sum_x",
        )(*acc)
        stats, near, far = small(choose_kernel, "choose", (8, 4, 4), keep, swap_cores(send), acc)
        stats = join(stats, turn(far, 1), turn(near, 3), turn(near, 2))
        acc = exchange(acc, "z")
        acc, stats = lax.optimization_barrier((acc, stats))
        stats = lax.all_gather(stats, "z", axis=0)
        acc = jnp.sum(acc.astype(F32), axis=0)
        grad_rows = acc[: half // NZ].astype(BF)
        norm_total = lax.dynamic_slice(
            acc[half // NZ : half // NZ + 2].reshape(-1), ((zi * NC + ci) * 32,), (32,)
        )

    new_nm = 0.9 * norm_m + 0.1 * norm_total
    new_nv = 0.95 * norm_v + 0.05 * norm_total * norm_total
    norm_step = new_nm / FIX_ONE / (jnp.sqrt(new_nv / FIX_TWO) + 1e-08)

    with jax.named_scope("grad_all"):
        norm_row = jnp.pad(norm_step.astype(BF)[None], ((0, PAD - 1), (0, W - 32)))
        grad_z = everyone(jnp.concatenate([grad_rows, norm_row], axis=0), "z", NZ)
        norm_zs = grad_z[:, half // NZ, None, :32]
        norm_zs = jnp.where(jnp.arange(NC)[None, :, None] == ci, norm_zs, 0).reshape(2, W)
        grad_half = grad_z[:, : half // NZ].reshape(half, W)
        grad_own = all_turns(grad_half, turn)
        pack, norm_zs = lax.optimization_barrier((pack, norm_zs))
        pack_other = swap_cores(pack)
        left, right = call(
            prep_kernel,
            "prep",
            [((full, full), BF)] * 2,
            [],
            where,
            pack,
            pack_other,
        )
        grad_own[2], left, right = lax.optimization_barrier((grad_own[2], left, right))
        grad_other = [swap_cores(piece) for piece in grad_own]

    with jax.named_scope("rotate"):
        any_space = pl.BlockSpec(memory_space=pl.ANY)
        grad, work, direction, rot_home = pl.pallas_call(
            rotate_kernel,
            out_shape=[
                jax.ShapeDtypeStruct((full, full), BF),
                jax.ShapeDtypeStruct((full, full), BF),
                jax.ShapeDtypeStruct((NM, half, W), BF),
                jax.ShapeDtypeStruct((NX, B, W), BF),
            ],
            in_specs=[SMEM] + [VMEM] * (2 * NM + 3),
            out_specs=[any_space, any_space, VMEM, VMEM],
            scratch_shapes=[
                pltpu.VMEM((full, W), F32),
                pltpu.VMEM((full, full), BF),
                pltpu.VMEM((full, full), BF),
                pltpu.SemaphoreType.DMA((2,)),
            ],
            compiler_params=pltpu.CompilerParams(vmem_limit_bytes=24 * 1024 * 1024),
            name="rotate",
        )(where, *grad_own, *grad_other, left, right, pack)
        stats, rot_home = lax.optimization_barrier((stats, rot_home))
        direction = exchange(direction, "mp")
    with jax.named_scope("power"):
        (power_old,) = call(
            old_power_kernel,
            "old_power",
            [((full, full), F32)],
            [((10, W, W), BF)],
            where,
            stats,
            left,
            right,
            cost=COST,
        )
        outer, basis = call(
            power_kernel,
            "power",
            [((NX, NC * B, W), BF)] * 2,
            [((full, full), F32), ((full, full), BF)],
            where,
            grad,
            work,
            power_old,
            cost=COST,
        )
        norm_pad = jnp.pad(norm_zs, ((0, PAD - 2), (0, 0)))
        direction, outer, basis = lax.optimization_barrier((direction, outer, basis))
    with jax.named_scope("update"):
        (back,) = call(back_kernel, "back", [((half, W), BF)], [], where, direction, right)
        back_other = swap_cores(back)
        update = call(
            update_kernel,
            "update",
            [((half + 5 * B + PAD, W), BF)] * NX,
            [((full, W), BF)],
            where,
            back,
            back_other,
            left,
            rot_home,
            outer,
            basis,
            norm_pad,
        )

    with jax.named_scope("home"):
        update = [update[0]] + [turn_x(update[s], s) for s in (1, 2, 3)]
        nb = NX * B
        own_slot, sent = call(
            relay_kernel,
            "relay",
            [((half, W), BF), ((half + 2 * nb + NX * PAD, W), BF)],
            [],
            where,
            *update,
        )
        recv = swap_cores(sent)
        state = ((NX, B, W), F32)
        outs = call(
            final_kernel,
            "final",
            [state] * 6 + [((1, full, W), BF), ((NX, 2, W), F32)],
            [],
            where,
            *update,
            own_slot,
            recv,
            moment1,
            moment2,
            left_stats,
            right_stats,
        )
    *outs, norm_slot = outs
    return (*outs, new_nm, new_nv, norm_slot.reshape(1, -1))


def solution(mesh):
    mesh = Mesh(mesh.devices.reshape(NX, NZ, NC, NM), ("x", "z", "c", "mp"))
    dp = ("x", "z", "c")
    state = P(None, dp, "mp")
    in_specs = (
        P(dp, None),
        P(dp, None, "mp"),
        P(dp, None),
        P(),
        state,
        state,
        state,
        state,
        state,
        state,
        P(dp),
        P(dp),
    )
    out_specs = (
        state,
        state,
        state,
        state,
        state,
        state,
        P(dp, None, "mp"),
        P(dp),
        P(dp),
        P(dp, None),
    )
    return jax.shard_map(shards, mesh=mesh, in_specs=in_specs, out_specs=out_specs, check_vma=False)
```
